32 devices in a mesh: dp: 2 (over x), seq: 4 (over z), expert: 4 (over y, core).
Axes of the slice: x: 2, y: 2, z: 4, core: 2. Of those that a mesh axis runs over, the one named last changes fastest.
Arguments:
- tokens: bfloat16 [32, 1024, 1152], P(('dp', 'expert'), 'seq'), may hold values from -6 to 6
- segment_ids: int32 [32, 1024], P(('dp', 'expert'), 'seq'), may hold values from 0 to 7, never falling along the last dimension, each value on 1 to 512 neighbouring positions
- routes: int32 [32, 1024, 1], P(('dp', 'expert'), 'seq'), may hold values from 0 to 7; in each aligned block of 256 rows (0 to 255, 256 to 511, ..., all dimensions but the last counted through in order) at most 48 rows name the same one
- keep_mask: int32 [32, 1024], P(('dp', 'expert'), 'seq'), may hold values 0 or 1
- out_grad: bfloat16 [32, 1024, 1152], P(('dp', 'expert'), 'seq'), may hold values from -6 to 6
- norm_one: bfloat16 [1152], replicated, may hold values from 0.5 to 1.5
- in_proj: bfloat16 [1152, 4608], P(None, ('dp', 'seq', 'expert')), may hold values from -0.1875 to 0.1875
- conv_weight: bfloat16 [4, 2304], P(None, ('dp', 'seq', 'expert')), may hold values from -3 to 3
- conv_bias: bfloat16 [2304], P(('dp', 'seq', 'expert')), may hold values from -3 to 3
- x_proj: bfloat16 [2304, 104], P(('dp', 'seq', 'expert')), may hold values from -0.125 to 0.125
- dt_proj: bfloat16 [72, 2304], P(None, ('dp', 'seq', 'expert')), may hold values from -0.75 to 0.75
- dt_bias: bfloat16 [2304], P(('dp', 'seq', 'expert')), may hold values from -7 to -2
- a_log: bfloat16 [16, 2304], P(None, ('dp', 'seq', 'expert')), may hold values from -4 to 2
- d_skip: bfloat16 [2304], P(('dp', 'seq', 'expert')), may hold values from 0.5 to 1.5
- out_proj: bfloat16 [2304, 1152], P(('dp', 'seq', 'expert')), may hold values from -0.5 to 0.5
- norm_two: bfloat16 [1152], replicated, may hold values from 0.5 to 1.5
- router: bfloat16 [1152, 8], replicated, may hold values from -0.125 to 0.125
- expert_up: bfloat16 [8, 1152, 3072], P('expert', None, ('dp', 'seq')), may hold values from -0.1875 to 0.1875
- expert_down: bfloat16 [8, 3072, 1152], P('expert', ('dp', 'seq')), may hold values from -0.4375 to 0.4375
Outputs:
- out_tokens: bfloat16 [32, 1024, 1152], P(('dp', 'expert'), 'seq')
- grad_tokens: float32 [32, 1024, 1152], P(('dp', 'expert'), 'seq')
- grad_norm_one: float32 [1152], replicated
- grad_in_proj: float32 [1152, 4608], P(None, ('dp', 'seq', 'expert'))
- grad_conv_weight: float32 [4, 2304], P(None, ('dp', 'seq', 'expert'))
- grad_conv_bias: float32 [2304], P(('dp', 'seq', 'expert'))
- grad_x_proj: float32 [2304, 104], P(('dp', 'seq', 'expert'))
- grad_dt_proj: float32 [72, 2304], P(None, ('dp', 'seq', 'expert'))
- grad_dt_bias: float32 [2304], P(('dp', 'seq', 'expert'))
- grad_a_log: float32 [16, 2304], P(None, ('dp', 'seq', 'expert'))
- grad_d_skip: float32 [2304], P(('dp', 'seq', 'expert'))
- grad_out_proj: float32 [2304, 1152], P(('dp', 'seq', 'expert'))
- grad_norm_two: float32 [1152], replicated
- grad_router: float32 [1152, 8], replicated
- grad_expert_up: float32 [8, 1152, 3072], P('expert', None, ('dp', 'seq'))
- grad_expert_down: float32 [8, 3072, 1152], P('expert', ('dp', 'seq'))
The draws below stay inside these ranges and needn't reach their ends.
Inputs may be any that keep to these rules, and one draw needn't show every extreme that they name: `segment_ids`: along each sequence the ids never fall. `routes`: in each aligned block of 256 positions of a sequence no expert is named more than 48 times.
All inputs are finite; a program needn't handle non-finite values. No bound on the sum of `keep_mask` on one device may be relied on, other than what follows from the above.
Results may differ from the reference program's by a relative error of at most 0.011.
Values may be sent and summed in bfloat16 or wider, within the bound.
A program may use at most 384 MiB of HBM per device.

```python
import math
import jax
import jax.numpy as jnp
import numpy as np
from jax import lax

D = 1152
DI = 2304
NSTATE = 16
DTR = 72
CONVK = 4
EXPERTS = 8
FFE = 3072
XW = 104
SPAN = 256
LENGTH = 1024
SEQ_GROUP = 4
SEQS = 32
SEGS = 8
CAP_CH = 48
N_SEQ = 4


def plant(values, key, smallest, largest):
    longest = values.shape.index(max(values.shape))
    spots = []
    for shift in (0, 1):
        where = [jax.random.randint(jax.random.fold_in(key, axis), (), 0, length) for axis, length in enumerate(values.shape)]
        where[longest] = (where[longest] + shift) % values.shape[longest]
        spots.append(tuple(where))
    return values.at[spots[0]].set(smallest).at[spots[1]].set(largest)


def level_of(rng, shape, cuts, least, top_value):
    loudness, own = 1.0, jax.random.fold_in(rng, 6)
    for position, blocks in cuts:
        steps = jnp.exp(jax.random.uniform(jax.random.fold_in(own, position), (blocks,), jnp.float32, least / len(cuts), top_value / len(cuts)))
        loudness = loudness * jnp.repeat(steps, shape[position] // blocks).reshape([-1 if axis == position else 1 for axis in range(len(shape))])
    return loudness


def split_up(amount, total, most, lean):
    weights = [(1 << 20) // math.isqrt(rank ** lean) + 1 for rank in range(2, amount + 1)]
    rest, counts = total - most - (amount - 1), [1] * (amount - 1)
    while rest > 0:
        free = [i for i in range(amount - 1) if counts[i] < most]
        mass, budget = sum([weights[i] for i in free]), rest
        for i in free:
            more = min(most - counts[i], max(1, budget * weights[i] // mass), rest)
            counts[i] = counts[i] + more
            rest = rest - more
    return np.array([most] + counts)


def ragged(stream_key, number_of, total, limit, skew):
    if number_of == 2:
        one = jax.random.randint(stream_key, (), max(1, total - limit), min(limit, total - 1) + 1)
        return jnp.stack([one, total - one])
    tallies = jnp.asarray(split_up(number_of, total, limit, skew), jnp.int32)
    twos = (number_of - 1) // 2
    giver, sink = tallies[1:1 + 2 * twos:2], tallies[2:2 + 2 * twos:2]
    room = jnp.minimum(giver - 1, limit - sink)
    shifted = jax.random.randint(jax.random.fold_in(stream_key, 1), (twos,), 0, 1 << 20) % (room + 1)
    tallies = tallies.at[1:1 + 2 * twos:2].set(giver - shifted).at[2:2 + 2 * twos:2].set(sink + shifted)
    return tallies[jax.random.permutation(jax.random.fold_in(stream_key, 2), number_of)]


def assign_block(rng, own, number, rows, count, top, limit, slope):
    ranking = jax.random.permutation(rng, count)
    heavy_load, usual = shares(count, rows * top, limit, slope, True), shares(count, rows * top, limit, slope, False)
    places = jnp.arange(count)

    def named(sizes, offset_by):
        used = int((sizes > 0).sum())
        fixed = max(1, used // 4)
        passed = fixed + (places - fixed + offset_by * (used - fixed)) % max(1, count - fixed)
        return jnp.zeros((count,), jnp.int32).at[ranking[jnp.where(places < fixed, places, passed)]].set(jnp.asarray(sizes, jnp.int32))

    sizes = jnp.where(number % 4 == 0, named(heavy_load, number // 4), named(usual, number - number // 4 - 1))
    mixed = jax.random.permutation(jax.random.fold_in(own, 3), count)
    giver, taker = mixed[0:count // 2 * 2:2], mixed[1:count // 2 * 2:2]
    margin = jnp.minimum(sizes[giver] - 1, limit - sizes[taker]) // 2
    margin = jnp.where((giver == ranking[0]) | (taker == ranking[0]) | (sizes[taker] == 0), 0, jnp.maximum(margin, 0))
    passed = jax.random.randint(jax.random.fold_in(own, 4), (count // 2,), 0, 1 << 20) % (margin + 1)
    sizes = sizes.at[giver].add(-passed).at[taker].add(passed)
    items = jnp.searchsorted(jnp.cumsum(sizes), jnp.arange(rows * top), side="right").astype(jnp.int32)
    grid = items.reshape(top, rows).T
    grid = grid[jax.random.permutation(jax.random.fold_in(own, 1), rows)]
    offset_by = jax.random.randint(jax.random.fold_in(own, 2), (rows, 1), 0, top)
    return jnp.take_along_axis(grid, (jnp.arange(top)[None, :] + offset_by) % top, axis=1)


def shares(amount, total, limit, lean, full):
    weights = [(1 << 20) // math.isqrt(standing ** lean) + 1 for standing in range(1, amount + 1)]
    largest = limit if full else min(limit, max(-(-total // amount), total * weights[0] // sum(weights)))
    least = 1 if total - largest >= amount - 1 else 0
    holding, spare = [largest] + [least] * (amount - 1), total - largest - least * (amount - 1)
    while spare > 0:
        free = [i for i in range(1, amount) if holding[i] < largest] or [i for i in range(1, amount) if holding[i] < limit]
        whole, left = sum([weights[i] for i in free]), spare
        for i in free:
            more = min(limit - holding[i], max(1, left * weights[i] // whole), spare)
            holding[i] = holding[i] + more
            spare = spare - more
    return np.array(holding)


def scatter_about(key, extent, deviation, reach, cuts=(), held_as=jnp.bfloat16):
    drawn = deviation * jax.random.normal(key, extent, jnp.float32)
    if cuts:
        drawn = drawn * level_of(key, extent, cuts, -0.22, 0.18)
    return jnp.clip(drawn, -reach, reach).astype(held_as)


def setup_inputs(seed: int = 0) -> dict:
    keys = jax.random.split(jax.random.key(seed), 20)
    tokens = scatter_about(keys[0], (SEQS, LENGTH, D), 1.0, 6.0, ((0, 8), (1, 4)))
    segment_ids = jax.vmap(lambda own: jnp.searchsorted(jnp.cumsum(ragged(own, SEGS, LENGTH, LENGTH // 2, 2)), jnp.arange(LENGTH), side="right"))(jax.random.split(keys[1], SEQS)).reshape((SEQS, LENGTH)).astype(jnp.int32)
    routes_keys = jax.random.split(jax.random.fold_in(keys[2], 1), SEQS * LENGTH // SPAN)
    routes_turns = jax.random.permutation(jax.random.fold_in(keys[2], 3), SEQS * LENGTH // SPAN)
    routes = jax.vmap(lambda own, number: assign_block(jax.random.fold_in(keys[2], 2), own, number, SPAN, EXPERTS, 1, CAP_CH, 1))(routes_keys, routes_turns).reshape((SEQS, LENGTH, 1))
    keep_mask = plant((jax.random.randint(keys[3], (SEQS, LENGTH), 0, 8) < 7).astype(jnp.int32), jax.random.fold_in(keys[3], 1), 0, 1)
    out_grad = scatter_about(keys[4], (SEQS, LENGTH, D), 1.0, 6.0, ((0, 8), (1, 4)))
    norm_one = jnp.clip(1.0 + 0.1 * jax.random.normal(keys[5], (D,), jnp.float32), 0.5, 1.5).astype(jnp.bfloat16)
    in_proj = scatter_about(keys[6], (D, 2 * DI), D ** -0.5, 0.1875, ((1, 32),))
    conv_weight = scatter_about(keys[7], (CONVK, DI), CONVK ** -0.5, 3.0, ((1, 32),))
    conv_bias = scatter_about(keys[8], (DI,), 0.5, 3.0, ((0, 32),))
    x_proj = scatter_about(keys[9], (DI, XW), DI ** -0.5, 0.125, ((0, 32),))
    dt_proj = scatter_about(keys[10], (DTR, DI), DTR ** -0.5, 0.75, ((1, 32),))
    dt_bias = jnp.clip(-7.0 + 5.0 * jax.random.uniform(keys[11], (DI,), jnp.float32) ** level_of(keys[11], (DI,), ((0, 32),), -0.2, 0.2), -7.0, -2.0).astype(jnp.bfloat16)
    a_log = jnp.clip(-4.0 + 6.0 * jax.random.uniform(keys[12], (NSTATE, DI), jnp.float32) ** level_of(keys[12], (NSTATE, DI), ((1, 32),), -0.2, 0.2), -4.0, 2.0).astype(jnp.bfloat16)
    d_skip = jnp.clip(0.5 + 1.0 * jax.random.uniform(keys[13], (DI,), jnp.float32) ** level_of(keys[13], (DI,), ((0, 32),), -0.2, 0.2), 0.5, 1.5).astype(jnp.bfloat16)
    out_proj = scatter_about(keys[14], (DI, D), (DI // 16) ** -0.5, 0.5, ((0, 32),))
    norm_two = jnp.clip(1.0 + 0.1 * jax.random.normal(keys[15], (D,), jnp.float32), 0.5, 1.5).astype(jnp.bfloat16)
    router = scatter_about(keys[16], (D, EXPERTS), (2 * D) ** -0.5, 0.125)
    expert_up = scatter_about(keys[17], (EXPERTS, D, FFE), D ** -0.5, 0.1875, ((0, 4), (2, 8)))
    expert_down = scatter_about(keys[18], (EXPERTS, FFE, D), (FFE // 16) ** -0.5, 0.4375, ((0, 4), (1, 8)))
    return dict(tokens=tokens, segment_ids=segment_ids, routes=routes, keep_mask=keep_mask, out_grad=out_grad, norm_one=norm_one, in_proj=in_proj, conv_weight=conv_weight, conv_bias=conv_bias, x_proj=x_proj, dt_proj=dt_proj, dt_bias=dt_bias, a_log=a_log, d_skip=d_skip, out_proj=out_proj, norm_two=norm_two, router=router, expert_up=expert_up, expert_down=expert_down)


norm_eps = 1e-05
ref_block = 64

@jax.custom_vjp
def low(v):
    return lax.optimization_barrier(v.astype(jnp.bfloat16)).astype(jnp.float32)

@jax.custom_vjp
def low_back(v):
    return v

def low_keep(v):
    return (low(v), None)

def low_pass(kept, grad):
    return (grad,)

def back_keep(v):
    return (v, None)

def back_low(kept, grad):
    return (low(grad),)
low.defvjp(low_keep, low_pass)
low_back.defvjp(back_keep, back_low)

def rms_norm(values, gain_vec):
    inv_rms = lax.rsqrt(lax.optimization_barrier(jnp.mean(values * values, axis=-1, keepdims=True)) + norm_eps)
    return values * inv_rms * gain_vec

def mat_mul(formula, left_op, right_op):
    return jnp.einsum(formula, left_op, right_op, precision=lax.Precision.HIGHEST, preferred_element_type=jnp.float32)

def ssm_scan(xs_vals, delta_val, b_mat, c_mat, keep_flag, a_mat):
    groups, length = (xs_vals.shape[0], xs_vals.shape[1])

    def token_step(state_now, token_in):
        xs_t, delta_t, b_t, c_t, keep_t = token_in
        decay_now = jnp.exp(delta_t[:, :, None] * a_mat[None]) * keep_t[:, None, None]
        state_now = decay_now * state_now + (delta_t * xs_t)[:, :, None] * b_t[:, None, :]
        return (state_now, lax.optimization_barrier(jnp.sum(state_now * c_t[:, None, :], axis=-1)))

    def block_step(state_now, block_in):
        return lax.scan(token_step, state_now, block_in)

    def arrange(values):
        moved_axis = jnp.moveaxis(values, 1, 0)
        return moved_axis.reshape((length // ref_block, ref_block) + moved_axis.shape[1:])
    start_state = jnp.zeros((groups, DI, NSTATE), jnp.float32)
    _, outputs = lax.scan(jax.checkpoint(block_step), start_state, (arrange(xs_vals), arrange(delta_val), arrange(b_mat), arrange(c_mat), arrange(keep_flag)))
    return jnp.moveaxis(outputs.reshape(length, groups, DI), 0, 1)

def group_forward(weights, pieces):
    norm_one, in_proj, conv_weight, conv_bias, x_proj, dt_proj, dt_bias, a_log, d_skip, out_proj, norm_two, router, expert_up, expert_down = weights
    inputs, segments, route_vals, drop_vals = pieces
    groups, length = segments.shape
    normed_one = low(rms_norm(inputs, norm_one))
    mixed_all = low_back(mat_mul('gld,de->gle', normed_one, in_proj))
    conv_in = mixed_all[..., :DI]
    gate_z = mixed_all[..., DI:]
    padded = jnp.pad(conv_in, ((0, 0), (CONVK - 1, 0), (0, 0)))
    seg_pad = jnp.pad(segments, ((0, 0), (CONVK - 1, 0)), constant_values=-1)
    conv_out = jnp.zeros_like(conv_in) + conv_bias
    for offset in range(CONVK):
        same_seg = (seg_pad[:, offset:offset + length] == segments).astype(jnp.float32)
        conv_out = conv_out + conv_weight[offset] * padded[:, offset:offset + length] * same_seg[..., None]
    xs_vals = low(jax.nn.silu(conv_out))
    proj_out = low_back(mat_mul('gle,ef->glf', xs_vals, x_proj))
    delta_in = low(proj_out[..., :DTR])
    b_mat = proj_out[..., DTR:DTR + NSTATE]
    c_mat = proj_out[..., DTR + NSTATE:]
    delta_val = jax.nn.softplus(low_back(mat_mul('glr,re->gle', delta_in, dt_proj)) + dt_bias)
    keep_flag = jnp.concatenate([jnp.ones((groups, 1), jnp.float32), (segments[:, 1:] == segments[:, :-1]).astype(jnp.float32)], axis=1)
    a_mat = -jnp.exp(a_log).T
    ssm_out = ssm_scan(xs_vals, delta_val, b_mat, c_mat, keep_flag, a_mat) + d_skip * xs_vals
    branch = low(ssm_out * jax.nn.silu(gate_z))
    first_sum = inputs + low_back(mat_mul('gle,ed->gld', branch, out_proj))
    normed_two = low(rms_norm(first_sum, norm_two))
    probs_all = jax.nn.softmax(mat_mul('gld,de->gle', normed_two, router), axis=-1)
    onehot = (route_vals[..., None] == jnp.arange(EXPERTS, dtype=jnp.int32)).astype(jnp.float32)
    gate_val = lax.optimization_barrier(jnp.sum(probs_all * onehot, axis=-1)) * drop_vals
    blocks = groups * N_SEQ
    hot_blocks = onehot.reshape(blocks, SPAN, EXPERTS)
    rank_vals = lax.optimization_barrier(jnp.sum((jnp.cumsum(hot_blocks, axis=1) - hot_blocks) * hot_blocks, axis=-1)).astype(jnp.int32)
    block_ids = jnp.arange(blocks, dtype=jnp.int32)[:, None]
    slot_ids = ((route_vals.reshape(blocks, SPAN) * blocks + block_ids) * CAP_CH + rank_vals).reshape(-1)
    per_expert = blocks * CAP_CH
    buffer = jnp.zeros((EXPERTS * per_expert, D), jnp.float32).at[slot_ids].set(normed_two.reshape(-1, D))

    def expert_map(operands):
        rows_in, up_w, down_w = operands
        hidden = low(jax.nn.gelu(low_back(mat_mul('kd,df->kf', rows_in, up_w)), approximate=True))
        return low_back(low(mat_mul('kf,fd->kd', hidden, down_w)))
    produced = lax.map(jax.checkpoint(expert_map), (buffer.reshape(EXPERTS, per_expert, D), expert_up, expert_down))
    expert_rows = produced.reshape(-1, D)[slot_ids].reshape(groups, length, D)
    return first_sum + gate_val[..., None] * expert_rows

def reference(tokens, segment_ids, routes, keep_mask, out_grad, norm_one, in_proj, conv_weight, conv_bias, x_proj, dt_proj, dt_bias, a_log, d_skip, out_proj, norm_two, router, expert_up, expert_down):
    weights = tuple((weight.astype(jnp.float32) for weight in (norm_one, in_proj, conv_weight, conv_bias, x_proj, dt_proj, dt_bias, a_log, d_skip, out_proj, norm_two, router, expert_up, expert_down)))
    seq_count = tokens.shape[0]
    group_size = SEQ_GROUP
    stacked_ints = (segment_ids.reshape(seq_count // group_size, group_size, LENGTH), routes[..., 0].reshape(seq_count // group_size, group_size, LENGTH), keep_mask.astype(jnp.float32).reshape(seq_count // group_size, group_size, LENGTH))

    def forward(inputs, weight_set):

        def one_group(carry_in, pieces):
            return (carry_in, group_forward(weight_set, pieces))
        stacked = (inputs.reshape(seq_count // group_size, group_size, LENGTH, D),) + stacked_ints
        _, outputs = lax.scan(jax.checkpoint(one_group), jnp.zeros((), jnp.float32), stacked)
        return outputs.reshape(seq_count, LENGTH, D)
    outputs, pullback = jax.vjp(forward, tokens.astype(jnp.float32), weights)
    grad_tokens, grad_weights = pullback(out_grad.astype(jnp.float32))
    return (outputs.astype(jnp.bfloat16), grad_tokens, grad_weights[0], grad_weights[1], grad_weights[2], grad_weights[3], grad_weights[4], grad_weights[5], grad_weights[6], grad_weights[7], grad_weights[8], grad_weights[9], grad_weights[10], grad_weights[11], grad_weights[12], grad_weights[13])
```

```python
import functools

import jax
import jax.numpy as jnp
from jax import lax
from jax.experimental import pallas as pl
from jax.experimental.pallas import tpu as pltpu
from jax.sharding import PartitionSpec as P

D = 1152
DI = 2304
NSTATE = 16
DTR = 72
CONVK = 4
EXPERTS = 8
XW = DTR + 2 * NSTATE
HALVES = 2
LANES = 128
LN2 = 0.6931471805599453
SPLITS = 3
SUB = 8
PACK = 256
CHUNK = 16
BIG = 1e30
VMEM = 60 * 1024 * 1024

norm_eps = 1e-05
ALL = ("dp", "seq", "expert")


def shifted(value, axis, steps):
    count = lax.axis_size(axis)
    first, last = (max(0, -steps), min(count, count - steps))
    return lax.ppermute(value, axis, [(source, source + steps) for source in range(first, last)])


def dot(left, right, dims, out=jnp.float32):
    return lax.dot_general(left, right, (dims, ((), ())), preferred_element_type=out)


NN = ((1,), (0,))
NT = ((1,), (1,))
TN = ((0,), (0,))


def to_rows(value):
    seqs, length = value.shape[:2]
    rest = value.shape[2:]
    split = value.reshape((seqs, HALVES, length // HALVES) + rest)
    return jnp.moveaxis(split, 2, 0).reshape((seqs * length,) + rest)


def from_rows(value, seqs):
    rest = value.shape[1:]
    length = value.shape[0] // seqs
    split = value.reshape((length // HALVES, seqs, HALVES) + rest)
    return jnp.moveaxis(split, 0, 2).reshape((seqs, length) + rest)


def to_ext_rows(value, halo):
    seqs, length = value.shape[:2]
    rest = value.shape[2:]
    part = length // HALVES
    ext = jnp.concatenate([halo, value], axis=1)
    split = jnp.stack([ext[:, h * part : h * part + part + CONVK - 1] for h in range(HALVES)], axis=1)
    return jnp.moveaxis(split, 2, 0).reshape(((part + CONVK - 1) * seqs * HALVES,) + rest)


def decay_rates(alog_ref, a_s):
    rates = -(1.0 / LN2) * jnp.exp(alog_ref[...].astype(jnp.float32))
    for n in range(NSTATE):
        a_s[n] = jnp.broadcast_to(rates[n : n + 1, :], (SUB, LANES))


def spread(src_ref, dst, first):
    src = src_ref[...]
    high = src.astype(jnp.bfloat16)
    both = jnp.concatenate([high, (src - high.astype(jnp.float32)).astype(jnp.bfloat16)], axis=1)
    line = lax.broadcasted_iota(jnp.int32, (4 * NSTATE, LANES), 0)

    def body(n, carry):
        pick = (line == first + n) | (line == 2 * NSTATE + first + n)
        dst[n] = dot(both, jnp.where(pick, 1.0, 0.0).astype(jnp.bfloat16), NN)
        return carry

    lax.fori_loop(0, NSTATE, body, 0)


def tree_sum(parts):
    while len(parts) > 1:
        parts = [parts[i] + parts[i + 1] if i + 1 < len(parts) else parts[i] for i in range(0, len(parts), 2)]
    return parts[0]


UNROLL = 8


def unrolled(first, count, body, carry):
    def group(i, inner):
        for u in range(UNROLL):
            inner = body(first + i * UNROLL + u, inner)
        return inner

    return lax.fori_loop(0, count // UNROLL, group, carry)


def row_at(t):
    return pl.ds(pl.multiple_of(t * SUB, SUB), SUB)


def end_kernel(xs_ref, din_ref, dtw_ref, dtb_ref, alog_ref, bc_ref, cut_ref, delta_ref, end_ref, sum_ref, b_s, a_s, dx_s):
    steps = delta_ref.shape[0] // SUB

    @pl.when(pl.program_id(0) == 0)
    def _():
        spread(bc_ref, b_s, 0)

    decay_rates(alog_ref, a_s)
    pre = dot(din_ref[...], dtw_ref[...], NT) + dtb_ref[...].astype(jnp.float32)
    low = jnp.exp(-jnp.abs(pre))
    delta = jnp.maximum(pre, 0.0) + jnp.where(low < 0.01, low * (1.0 - low * (0.5 - low * (1.0 / 3.0))), jnp.log(1.0 + low))
    delta_ref[...] = delta
    dx_s[...] = delta * xs_ref[...].astype(jnp.float32)
    rates = [a_s[n] for n in range(NSTATE)]

    def body(t, carry):
        total, state = carry
        at = row_at(t)
        step = jnp.maximum(delta_ref[at, :], cut_ref[at, :])
        dx = dx_s[at, :]
        state = [jnp.exp2(step * rates[n]) * state[n] + dx * b_s[n, at, :] for n in range(NSTATE)]
        return (total + step, state)

    zero = jnp.zeros((SUB, LANES), jnp.float32)
    total, state = unrolled(0, steps, body, (zero, [zero] * NSTATE))
    sum_ref[...] = total
    for n in range(NSTATE):
        end_ref[n] = state[n]


def out_kernel(xs_ref, delta_ref, alog_ref, bc_ref, cut_ref, start_ref, z_ref, skip_ref, branch_ref, ssm_ref, held_ref, b_s, c_s, a_s, dx_s, y_s):
    steps = delta_ref.shape[0] // SUB

    @pl.when(pl.program_id(0) == 0)
    def _():
        spread(bc_ref, b_s, 0)
        spread(bc_ref, c_s, NSTATE)

    decay_rates(alog_ref, a_s)
    xs = xs_ref[...].astype(jnp.float32)
    dx_s[...] = delta_ref[...] * xs
    rates = [a_s[n] for n in range(NSTATE)]

    def body(t, state):
        at = row_at(t)
        step = jnp.maximum(delta_ref[at, :], cut_ref[at, :])
        dx = dx_s[at, :]
        state = [jnp.exp2(step * rates[n]) * state[n] + dx * b_s[n, at, :] for n in range(NSTATE)]
        y_s[at, :] = tree_sum([state[n] * c_s[n, at, :] for n in range(NSTATE)])
        return state

    def chunk(i, state):
        for n in range(NSTATE):
            held_ref[i, n] = state[n]
        return unrolled(i * CHUNK, CHUNK, body, state)

    lax.fori_loop(0, steps // CHUNK, chunk, [start_ref[n] for n in range(NSTATE)])
    ssm = y_s[...] + skip_ref[...].astype(jnp.float32) * xs
    z = z_ref[...]
    ssm_ref[...] = ssm.astype(jnp.bfloat16)
    branch_ref[...] = (ssm * (z / (1.0 + jnp.exp(-z)))).astype(jnp.bfloat16)


def first_kernel(delta_ref, alog_ref, bc_ref, cut_ref, gb_ref, z_ref, ssm_ref, lead_ref, gz_ref, g_s, c_s, a_s):
    steps = delta_ref.shape[0] // SUB

    @pl.when(pl.program_id(0) == 0)
    def _():
        spread(bc_ref, c_s, NSTATE)

    decay_rates(alog_ref, a_s)
    z = z_ref[...]
    grad = gb_ref[...]
    sig = 1.0 / (1.0 + jnp.exp(-z))
    g_s[...] = grad * (z * sig)
    gz_ref[...] = (grad * ssm_ref[...].astype(jnp.float32) * (sig * (1.0 + z * (1.0 - sig)))).astype(jnp.bfloat16)
    rates = [a_s[n] for n in range(NSTATE)]

    def body(k, lead):
        at = row_at(steps - 1 - k)
        step = jnp.maximum(delta_ref[at, :], cut_ref[at, :])
        g = g_s[at, :]
        return [jnp.exp2(step * rates[n]) * (lead[n] + g * c_s[n, at, :]) for n in range(NSTATE)]

    zero = jnp.zeros((SUB, LANES), jnp.float32)
    lead = unrolled(0, steps, body, [zero] * NSTATE)
    for n in range(NSTATE):
        lead_ref[n] = lead[n]


def back_kernel(
    xs_ref, delta_ref, alog_ref, bc_ref, cut_ref, g_ref, skip_ref, held_ref, last_ref,
    gxs_ref, gpre_ref, galog_ref, gvec_ref, gbc_ref,
    b_s, c_s, gb_s, gc_s, a_s, dx_s, x_s, gx_s, gd_s, hd_s, dec_s,
):
    steps = delta_ref.shape[0] // SUB

    @pl.when(pl.program_id(0) == 0)
    def _():
        spread(bc_ref, b_s, 0)
        spread(bc_ref, c_s, NSTATE)
        gb_s[...] = jnp.zeros_like(gb_s)
        gc_s[...] = jnp.zeros_like(gc_s)

    decay_rates(alog_ref, a_s)
    xs = xs_ref[...].astype(jnp.float32)
    x_s[...] = xs
    dx_s[...] = delta_ref[...] * xs

    def ahead(j, state, base):
        at = row_at(base + j)
        step = jnp.maximum(delta_ref[at, :], cut_ref[at, :])
        dx = dx_s[at, :]
        g = g_ref[at, :]
        new = []
        for n in range(NSTATE):
            dec = jnp.exp2(step * a_s[n])
            hd = dec * state[n]
            dec_s[j, n] = dec
            hd_s[j, n] = hd
            h = hd + dx * b_s[n, at, :]
            gc_s[n, at, :] = gc_s[n, at, :] + g * h
            new.append(h)
        return new

    def behind(k, carry, base):
        coming, rate_grad = carry
        j = CHUNK - 1 - k
        at = row_at(base + j)
        delta = delta_ref[at, :]
        dx = dx_s[at, :]
        g = g_ref[at, :]
        next_coming, next_rate, with_b, with_a = [], [], [], []
        for n in range(NSTATE):
            lam = coming[n] + g * c_s[n, at, :]
            with_b.append(lam * b_s[n, at, :])
            gb_s[n, at, :] = gb_s[n, at, :] + lam * dx
            q = lam * hd_s[j, n]
            with_a.append(q * a_s[n])
            next_rate.append(rate_grad[n] + delta * q)
            next_coming.append(lam * dec_s[j, n])
        by_b = tree_sum(with_b)
        gx_s[at, :] = by_b * delta
        gd_s[at, :] = by_b * x_s[at, :] + LN2 * tree_sum(with_a)
        return (next_coming, next_rate)

    chunks = steps // CHUNK

    def chunk(i, carry):
        c = chunks - 1 - i
        base = c * CHUNK
        unrolled(0, CHUNK, functools.partial(ahead, base=base), [held_ref[c, n] for n in range(NSTATE)])
        return unrolled(0, CHUNK, functools.partial(behind, base=base), carry)

    zero = jnp.zeros((SUB, LANES), jnp.float32)
    _, rate_grad = lax.fori_loop(0, chunks, chunk, ([last_ref[n] for n in range(NSTATE)], [zero] * NSTATE))
    for n in range(NSTATE):
        galog_ref[n : n + 1, :] = LN2 * jnp.sum(rate_grad[n] * a_s[n], axis=0, keepdims=True)
    skip = skip_ref[...].astype(jnp.float32)
    grad_ssm = g_ref[...]
    gxs_ref[...] = gx_s[...] + grad_ssm * skip
    delta = delta_ref[...]
    slope = jnp.where(delta < 0.01, delta * (1.0 - 0.5 * delta * (1.0 - delta * (1.0 / 3.0))), 1.0 - jnp.exp(-delta))
    gpre = gd_s[...] * slope
    gpre_ref[...] = gpre.astype(jnp.bfloat16)
    gvec_ref[0:1, :] = jnp.sum(gpre, axis=0, keepdims=True)
    gvec_ref[1:2, :] = jnp.sum(grad_ssm * xs, axis=0, keepdims=True)
    gvec_ref[2:SUB, :] = jnp.zeros((SUB - 2, LANES), jnp.float32)

    @pl.when(pl.program_id(0) == pl.num_programs(0) - 1)
    def _():
        lane = lax.broadcasted_iota(jnp.int32, (LANES, LANES), 1)
        gbc_ref[...] = jnp.zeros_like(gbc_ref)

        def gather(n, carry):
            for part, first in ((gb_s, 0), (gc_s, NSTATE)):
                pick = jnp.where(lane == first + n, 1.0, 0.0).astype(jnp.bfloat16)
                gbc_ref[...] += dot(part[n].astype(jnp.bfloat16), pick, NN)
            return carry

        lax.fori_loop(0, NSTATE, gather, 0)


def col_spec(rows):
    return pl.BlockSpec((rows, LANES), lambda c: (0, c))


def full_spec(shape):
    return pl.BlockSpec(shape, lambda c: (0,) * len(shape))


def state_spec():
    return pl.BlockSpec((NSTATE, SUB, LANES), lambda c: (0, 0, c))


def params():
    return pltpu.CompilerParams(vmem_limit_bytes=VMEM)


def f32s(*shape):
    return jax.ShapeDtypeStruct(shape, jnp.float32)


def b16s(*shape):
    return jax.ShapeDtypeStruct(shape, jnp.bfloat16)


def vm(*shape):
    return pltpu.VMEM(shape, jnp.float32)


def cost(rows, width, per_value):
    work = rows * width * NSTATE
    return pl.CostEstimate(flops=work * 8, bytes_accessed=work * per_value, transcendentals=work)


def run_end(xs, din, dtw, dtb, alog, bc, cut):
    rows = xs.shape[0]
    return pl.pallas_call(
        end_kernel,
        grid=(DI // LANES,),
        in_specs=[
            col_spec(rows), full_spec(din.shape), pl.BlockSpec((LANES, DTR), lambda c: (c, 0)),
            col_spec(1), col_spec(NSTATE), full_spec(bc.shape), full_spec(cut.shape),
        ],
        out_specs=[col_spec(rows), state_spec(), col_spec(SUB)],
        out_shape=[f32s(rows, DI), f32s(NSTATE, SUB, DI), f32s(SUB, DI)],
        scratch_shapes=[vm(NSTATE, rows, LANES), vm(NSTATE, SUB, LANES), vm(rows, LANES)],
        compiler_params=params(),
        cost_estimate=cost(rows, DI, 4),
        name="end",
    )(xs, din, dtw, dtb, alog, bc, cut)


def run_out(xs, delta, alog, bc, cut, start, z, skip):
    rows = xs.shape[0]
    chunks = rows // SUB // CHUNK
    return pl.pallas_call(
        out_kernel,
        grid=(DI // LANES,),
        in_specs=[
            col_spec(rows), col_spec(rows), col_spec(NSTATE), full_spec(bc.shape), full_spec(cut.shape),
            state_spec(), col_spec(rows), col_spec(1),
        ],
        out_specs=[
            col_spec(rows), col_spec(rows),
            pl.BlockSpec((chunks, NSTATE, SUB, LANES), lambda c: (0, 0, 0, c)),
        ],
        out_shape=[b16s(rows, DI), b16s(rows, DI), f32s(chunks, NSTATE, SUB, DI)],
        scratch_shapes=[
            vm(NSTATE, rows, LANES), vm(NSTATE, rows, LANES), vm(NSTATE, SUB, LANES), vm(rows, LANES), vm(rows, LANES),
        ],
        compiler_params=params(),
        cost_estimate=cost(rows, DI, 5),
        name="out",
    )(xs, delta, alog, bc, cut, start, z, skip)


def run_first(delta, alog, bc, cut, gbranch, z, ssm):
    rows = delta.shape[0]
    return pl.pallas_call(
        first_kernel,
        grid=(DI // LANES,),
        in_specs=[
            col_spec(rows), col_spec(NSTATE), full_spec(bc.shape), full_spec(cut.shape), col_spec(rows), col_spec(rows),
            col_spec(rows),
        ],
        out_specs=[state_spec(), col_spec(rows), col_spec(rows)],
        out_shape=[f32s(NSTATE, SUB, DI), b16s(rows, DI), f32s(rows, DI)],
        scratch_shapes=[vm(NSTATE, rows, LANES), vm(NSTATE, SUB, LANES)],
        compiler_params=params(),
        cost_estimate=cost(rows, DI, 4),
        name="first",
    )(delta, alog, bc, cut, gbranch, z, ssm)


def run_back(xs, delta, alog, bc, cut, grad_ssm, skip, held, last, part):
    rows = xs.shape[0]
    chunks = rows // SUB // CHUNK
    big = (NSTATE, rows, LANES)
    row = (rows, LANES)
    width = DI // SPLITS
    first = part * (width // LANES)

    def col(count):
        return pl.BlockSpec((count, LANES), lambda c: (0, c + first))

    return pl.pallas_call(
        back_kernel,
        grid=(width // LANES,),
        in_specs=[
            col(rows), col(rows), col(NSTATE), full_spec(bc.shape), full_spec(cut.shape), col(rows), col(1),
            pl.BlockSpec((chunks, NSTATE, SUB, LANES), lambda c: (0, 0, 0, c + first)),
            pl.BlockSpec((NSTATE, SUB, LANES), lambda c: (0, 0, c + first)),
        ],
        out_specs=[col_spec(rows), col_spec(rows), col_spec(NSTATE), col_spec(SUB), full_spec(row)],
        out_shape=[f32s(rows, width), b16s(rows, width), f32s(NSTATE, width), f32s(SUB, width), f32s(*row)],
        scratch_shapes=[
            vm(*big), vm(*big), vm(*big), vm(*big), vm(NSTATE, SUB, LANES),
            vm(*row), vm(*row), vm(*row), vm(*row),
            vm(CHUNK, NSTATE, SUB, LANES), vm(CHUNK, NSTATE, SUB, LANES),
        ],
        compiler_params=params(),
        cost_estimate=cost(rows, width, 17),
        name="back",
    )(xs, delta, alog, bc, cut, grad_ssm, skip, held, last)


def conv_kernel(gxs_ref, gproj_ref, xproj_ref, ext_ref, taps_ref, bias_ref, same_ref, gext_ref, gvec_ref, acc_s):
    rows = gxs_ref.shape[0]
    halo = CONVK - 1
    taps = taps_ref[...]
    bias = bias_ref[...]
    pieces = []
    conv = bias
    for k in range(CONVK):
        piece = ext_ref[k * SUB : k * SUB + rows, :]
        if k < halo:
            piece = piece * same_ref[k]
        pieces.append(piece)
        conv = conv + taps[k : k + 1, :] * piece
    sig = 1.0 / (1.0 + jnp.exp(-conv))
    grad = gxs_ref[...] + dot(gproj_ref[...], xproj_ref[...], NT)
    grad = grad * (sig * (1.0 + conv * (1.0 - sig)))
    acc_s[...] = jnp.zeros_like(acc_s)
    for k in range(CONVK):
        gvec_ref[k : k + 1, :] = jnp.sum(grad * pieces[k], axis=0, keepdims=True)
        part = taps[k : k + 1, :] * grad
        if k < halo:
            part = part * same_ref[k]
        acc_s[k * SUB : k * SUB + rows, :] += part
    gvec_ref[CONVK : CONVK + 1, :] = jnp.sum(grad, axis=0, keepdims=True)
    gvec_ref[CONVK + 1 : SUB, :] = jnp.zeros((SUB - CONVK - 1, LANES), jnp.float32)
    gext_ref[...] = acc_s[...].astype(jnp.bfloat16)


def run_conv(gxs, gproj, xproj, ext, taps, bias, same, part):
    rows, width = gxs.shape
    long = ext.shape[0]
    first = part * (width // LANES)

    def col(count):
        return pl.BlockSpec((count, LANES), lambda c: (0, c + first))

    return pl.pallas_call(
        conv_kernel,
        grid=(width // LANES,),
        in_specs=[
            col_spec(rows), full_spec(gproj.shape), pl.BlockSpec((LANES, XW), lambda c: (c + first, 0)), col(long),
            col(CONVK), col(1), full_spec(same.shape),
        ],
        out_specs=[col_spec(long), col_spec(SUB)],
        out_shape=[b16s(long, width), f32s(SUB, width)],
        scratch_shapes=[vm(long, LANES)],
        compiler_params=params(),
        cost_estimate=pl.CostEstimate(flops=rows * width * 260, bytes_accessed=rows * width * 10, transcendentals=rows * width),
        name="conv",
    )(gxs, gproj, xproj, ext, taps, bias, same)


def halves_of(value, seqs):
    split = value.reshape(value.shape[:-2] + (seqs, HALVES, value.shape[-1]))
    return split[..., 0, :], split[..., 1, :]


def join_halves(first, second):
    both = jnp.stack([first, second], axis=-2)
    return both.reshape(both.shape[:-3] + (both.shape[-3] * HALVES, both.shape[-1]))


def chained(own, decay, steps):
    start = jnp.zeros_like(own)
    carry = own
    for k in range(lax.axis_size("seq") - 1):
        start = shifted(carry.astype(jnp.bfloat16), "seq", steps).astype(jnp.float32)
        carry = own + decay * start
    return start


def start_states(ends, sums, rates, seqs):
    end_0, end_1 = halves_of(ends, seqs)
    sum_0, sum_1 = halves_of(sums, seqs)
    decay_0 = jnp.exp(rates * sum_0)
    decay_1 = jnp.exp(rates * sum_1)
    start = chained(decay_1 * end_0 + end_1, decay_0 * decay_1, 1)
    return join_halves(start, decay_0 * start + end_0), (decay_0, decay_1)


def last_grads(leads, decays, seqs):
    decay_0, decay_1 = decays
    lead_0, lead_1 = halves_of(leads, seqs)
    last = chained(lead_0 + decay_0 * lead_1, decay_0 * decay_1, -1)
    return join_halves(lead_1 + decay_1 * last, last)


def ring(value, axis, step):
    count = lax.axis_size(axis)
    return lax.ppermute(value, axis, [(i, (i + step) % count) for i in range(count)])


def partner(value, axis, bits):
    count = lax.axis_size(axis)
    return lax.ppermute(value, axis, [(i, i ^ bits) for i in range(count)])


def held_for(first, *others):
    flat, tree = jax.tree.flatten((first,) + others)
    return jax.tree.unflatten(tree, lax.optimization_barrier(flat))


class Gather:
    def __init__(self, own):
        self.here, self.there = [own], []

    def step(self):
        self.there.append(ring(self.here[len(self.there)], "dp", 1))
        if len(self.here) < lax.axis_size("seq"):
            self.here.append(ring(self.here[-1], "seq", 1))

    def hold(self, value):
        value, here, there = held_for(value, self.here[1:], self.there)
        self.here[1:], self.there = here, there
        return value

    def done(self):
        return len(self.there) == lax.axis_size("seq")


class Reduce:
    def __init__(self, here, there, x_first):
        self.peers = lax.axis_size("seq")
        here = here.reshape(self.peers, -1, D)
        there = there.reshape(self.peers, -1, D)
        self.x_first, self.k, self.total = x_first, self.peers, None
        self.blocks = [(here[k], there[k]) for k in range(self.peers)]
        if x_first:
            self.moving = ring(there, "dp", 1)
        else:
            self.advance()

    def term(self, k):
        if self.x_first:
            return self.blocks[k][0].astype(jnp.float32) + self.other[k].astype(jnp.float32)
        return jnp.stack(self.blocks[k]).astype(jnp.float32)

    def advance(self):
        self.k -= 1
        self.total = self.term(self.k) if self.total is None else self.term(self.k) + self.moving.astype(jnp.float32)
        if self.k > 0:
            self.moving = ring(self.total.astype(jnp.bfloat16), "seq", -1)
        elif self.x_first:
            self.moving = None
        else:
            self.moving = ring(self.total[1].astype(jnp.bfloat16), "dp", 1)

    def step(self):
        if self.moving is None:
            return
        if self.x_first and self.total is None:
            self.other = self.moving
            self.advance()
        elif self.k > 0:
            self.advance()
        else:
            self.total = self.total[0] + self.moving.astype(jnp.float32)
            self.moving = None

    def finish(self):
        while self.moving is not None:
            self.step()
        return self.total


def hold_all(value, reduces):
    live = [r for r in reduces if r.moving is not None]
    value, moved = held_for(value, [r.moving for r in live])
    for r, m in zip(live, moved):
        r.moving = m
        r.step()
    return value


def sum_everywhere(value):
    for axis in ALL:
        bits = 1
        while bits < lax.axis_size(axis):
            value = value + partner(value, axis, bits)
            bits *= 2
    return value


def exchange(blocks):
    return [blocks[0]] + [partner(blocks[d], "expert", d) for d in range(1, len(blocks))]


def gelu_pair(v):
    inner = 0.7978845608 * (v + 0.044715 * v * v * v)
    t = jnp.tanh(inner)
    value = 0.5 * v * (1.0 + t)
    slope = 0.5 * (1.0 + t) + 0.5 * v * (1.0 - t * t) * (0.7978845608 * (1.0 + 3.0 * 0.044715 * v * v))
    return value, slope


def local(
    tokens, segment_ids, routes, keep_mask, out_grad, norm_one, in_proj, conv_weight, conv_bias, x_proj,
    dt_proj, dt_bias, a_log, d_skip, out_proj, norm_two, router, expert_up, expert_down,
):
    seqs, length = tokens.shape[:2]
    rows = seqs * length
    steps = length // HALVES
    halo = CONVK - 1
    capacity = seqs * max(2, length * 3 // 16)
    f32, b16 = jnp.float32, jnp.bfloat16
    own = in_proj.shape[1]

    small = jnp.concatenate(
        [x_proj, dt_proj.T, conv_weight.T, conv_bias[:, None], dt_bias[:, None], a_log.T, d_skip[:, None]], axis=1
    )
    used = small.shape[1]
    small = jnp.pad(small, ((0, 0), (0, PACK - used)))
    entry = lax.all_gather(jnp.concatenate([in_proj.T, small.reshape(-1, D)], axis=0), ALL, axis=0, tiled=False)
    in_full = entry[:, :own].reshape(2 * DI, D)
    small = entry[:, own:].reshape(DI, PACK)
    out_full = lax.all_gather(out_proj, ALL, axis=0, tiled=True)
    local_experts = expert_up.shape[0]
    shard = jnp.stack([m for e in range(local_experts) for m in (expert_up[e].T, expert_down[e])])
    shard, in_full = held_for(shard, in_full)
    gather = Gather(shard)
    gather.step()

    xproj_full = small[:, :XW]
    dtw = small[:, XW : XW + DTR]
    at = XW + DTR
    rest = small[:, at:used].T
    conv_w = rest[:CONVK].astype(f32)
    cbias = rest[CONVK : CONVK + 1].astype(f32)
    dtb = rest[CONVK + 1 : CONVK + 2]
    alog = rest[CONVK + 2 : CONVK + 2 + NSTATE]
    skip = rest[CONVK + 2 + NSTATE :]

    halo_tokens = shifted(tokens[:, length - halo :], "seq", 1)
    halo_segs = shifted(segment_ids[:, length - halo :].astype(f32), "seq", 1)
    inputs = to_ext_rows(tokens, halo_tokens).astype(f32)
    seg_ext = to_ext_rows(segment_ids.astype(f32), halo_segs)
    drop = to_rows(keep_mask).astype(f32)
    route = to_rows(routes[..., 0])
    grad_low = to_rows(out_grad)
    grad_final = grad_low.astype(f32)
    skip_rows = halo * SUB
    seg = seg_ext[skip_rows:]
    same = [(seg_ext[k * SUB : k * SUB + rows] == seg).astype(f32)[:, None] for k in range(halo)]
    same_wide = jnp.broadcast_to(jnp.stack(same), (halo, rows, LANES))
    cut = jnp.broadcast_to((1.0 - same[halo - 1]) * BIG, (rows, LANES))

    onehot = (route[:, None] == jnp.arange(EXPERTS, dtype=jnp.int32)).astype(f32)
    order = jnp.arange(rows)
    below = (order[None, :] < order[:, None]).astype(b16)
    rank = jnp.sum(dot(below, onehot.astype(b16), NN) * onehot, axis=-1).astype(jnp.int32)
    peers = lax.axis_size("expert")
    target = (route // local_experts) ^ lax.axis_index("expert")
    slot = (target * local_experts + route % local_experts) * capacity + rank
    placing = (jnp.arange(EXPERTS * capacity, dtype=jnp.int32)[:, None] == slot[None, :]).astype(b16)

    def dispatch(values):
        sent = dot(placing, values, NN, b16).reshape(peers, local_experts, capacity, values.shape[1])
        return exchange([sent[d] for d in range(peers)])

    gain_one = norm_one.astype(f32)
    inv_one = lax.rsqrt(jnp.mean(inputs * inputs, axis=-1, keepdims=True) + norm_eps)
    normed_one = (inputs * inv_one * gain_one).astype(b16)
    ext = dot(normed_one, in_full[:DI], NT)
    gate_z = dot(normed_one[skip_rows:], in_full[DI:], NT)
    conv_out = cbias + conv_w[halo] * ext[skip_rows:]
    for k in range(halo):
        conv_out = conv_out + conv_w[k] * (same[k] * ext[k * SUB : k * SUB + rows])
    xs = jax.nn.silu(conv_out).astype(b16)
    proj = dot(xs, xproj_full, NN)
    delta_in = proj[:, :DTR].astype(b16)
    bc = proj[:, DTR:]
    grad_arrived = dispatch(grad_low)
    delta, ends, sums = run_end(xs, delta_in, dtw, dtb, alog, bc, cut)
    ends, grad_arrived = held_for(ends, grad_arrived)
    rates = -jnp.exp(alog.astype(f32))[:, None, :]
    starts, decays = start_states(ends, sums, rates, seqs)
    starts = gather.hold(starts)
    gather.step()
    branch, ssm, held = run_out(xs, delta, alog, bc, cut, starts, gate_z, skip)
    tokens_rows = inputs[skip_rows:]
    first_sum = tokens_rows + dot(branch, out_full, NN)

    gain_two = norm_two.astype(f32)
    inv_two = lax.rsqrt(jnp.mean(first_sum * first_sum, axis=-1, keepdims=True) + norm_eps)
    normed_two = (first_sum * inv_two * gain_two).astype(b16)
    probs = jax.nn.softmax(dot(normed_two, router, NN), axis=-1)
    gate_raw = jnp.sum(probs * onehot, axis=-1)
    gate = gate_raw * drop
    gate_high = lax.reduce_precision(gate, 8, 7)
    gate_mid = lax.reduce_precision(gate - gate_high, 8, 7)
    gate_low = gate - gate_high - gate_mid
    gates = jnp.stack([gate_high, gate_mid, gate_low], axis=1).astype(b16)
    message = jnp.concatenate([normed_two, jnp.pad(gates, ((0, 0), (0, LANES - 3)))], axis=1)
    message = gather.hold(message)
    gather.step()
    arrived = dispatch(message)
    arrived = gather.hold(arrived)
    while not gather.done():
        gather.step()

    def matrices(blocks):
        return [jnp.concatenate([block[m] for block in blocks], axis=0) for m in range(2 * local_experts)]

    rows_of = []
    for e in range(local_experts):
        here = jnp.concatenate([part[e] for part in arrived], axis=0)
        gate_rows = jnp.sum(here[:, D : D + 3].astype(f32), axis=1, keepdims=True)
        g_rows = (gate_rows * jnp.concatenate([part[e] for part in grad_arrived], axis=0).astype(f32)).astype(b16)
        rows_of.append((here[:, :D], g_rows))
    sides, produced, grad_in = [], [0.0] * local_experts, [0.0] * local_experts
    for side in range(2):
        mats = matrices(gather.here if side == 0 else gather.there)
        kept = []
        for e in range(local_experts):
            x_rows, g_rows = rows_of[e]
            value, slope = gelu_pair(dot(x_rows, mats[2 * e], NT))
            hidden = value.astype(b16)
            produced[e] = produced[e] + dot(hidden, mats[2 * e + 1], NN)
            grad_pre = (slope * dot(g_rows, mats[2 * e + 1], NT)).astype(b16)
            grad_in[e] = grad_in[e] + dot(grad_pre, mats[2 * e], NN)
            kept.append((hidden, grad_pre))
        sides.append(kept)
        if side == 0:
            produced, grad_in = held_for(produced, grad_in)
            rows_of, produced, grad_in = gather.hold((rows_of, produced, grad_in))

    def send_back(parts):
        return [exchange([part.astype(b16).reshape(peers, capacity, D)[d] for d in range(peers)]) for part in parts]

    returned_y = send_back(produced)
    returned_g = send_back(grad_in)
    weight_grads = []
    for e in range(local_experts):
        x_rows, g_rows = rows_of[e]
        for m in range(2):
            left, right = (1, x_rows) if m == 0 else (0, g_rows)
            weight_grads.append([dot(sides[side][e][left], right, TN, b16) for side in range(2)])
    count = len(weight_grads)
    returned_y, returned_g, weight_grads = held_for(returned_y, returned_g, weight_grads)
    reduces = [Reduce(g[0], g[1], i < count - 1) for i, g in enumerate(weight_grads)]
    early = [reduces[0], reduces[-1]]

    def collect(parts):
        back_rows = jnp.stack([jnp.stack(part) for part in parts], axis=1).reshape(EXPERTS * capacity, D)
        return dot(placing, back_rows, TN)

    expert_rows = collect(returned_y)
    grad_back = collect(returned_g)
    output = (first_sum + gate[:, None] * expert_rows).astype(b16)

    grad_gate = jnp.sum(grad_final * expert_rows, axis=-1) * drop
    grad_logits = (grad_gate * gate_raw)[:, None] * (onehot - probs)
    logits_low = grad_logits.astype(b16)
    router_grad = dot(normed_two, logits_low, TN)
    grad_two = grad_back + dot(logits_low, router, NT)
    gain_two_grad = jnp.sum(grad_two * (first_sum * inv_two), axis=0)
    scaled = grad_two * gain_two
    grad_first = (
        grad_final + inv_two * scaled
        - first_sum * (inv_two * inv_two * inv_two * jnp.mean(scaled * first_sum, axis=-1, keepdims=True))
    )
    grad_first = hold_all(grad_first, reduces[-1:])
    first_low = grad_first.astype(b16)
    out_grad_part = dot(branch, first_low, TN, b16)
    grad_branch = dot(first_low, out_full, NT)
    grad_branch, out_grad_part = held_for(grad_branch, out_grad_part)
    out_sum = lax.psum_scatter(out_grad_part, ALL, scatter_dimension=0, tiled=True)
    grad_branch = hold_all(grad_branch, early)

    leads, grad_z, grad_ssm = run_first(delta, alog, bc, cut, grad_branch, gate_z, ssm)
    last = last_grads(leads, decays, seqs)
    gate_part = dot(grad_z, normed_one[skip_rows:], TN, b16)
    grad_normed_z = dot(grad_z, in_full[DI:], NN)
    grad_ssm, gate_part, grad_normed_z = held_for(grad_ssm, gate_part, grad_normed_z)
    gate_own = lax.psum_scatter(gate_part, ("seq", "expert"), scatter_dimension=0, tiled=True)
    grad_delta_in, gbc, parts = 0.0, 0.0, []
    width = DI // SPLITS
    for part in range(SPLITS):
        if part == 1:
            last, out_sum = held_for(last, out_sum)
        last = hold_all(last, reduces[: 2 + part] + reduces[-1:] if 2 + part < count else reduces)
        gxs, gpre, galog, gvec, gbc_part = run_back(xs, delta, alog, bc, cut, grad_ssm, skip, held, last, part)
        grad_delta_in = grad_delta_in + dot(gpre, dtw[part * width : (part + 1) * width], NN)
        gbc = gbc + gbc_part[:, : 2 * NSTATE]
        dtproj_part = dot(gpre, delta_in, TN)
        last, gxs, dtproj_part, grad_delta_in, gbc, galog, gvec = held_for(
            last, gxs, dtproj_part, grad_delta_in, gbc, galog, gvec
        )
        parts.append((gxs, dtproj_part, galog, gvec))
    grad_proj = jnp.concatenate([grad_delta_in, gbc], axis=1).astype(b16)
    grad_proj, gate_own = held_for(hold_all(grad_proj, reduces), gate_own)
    xproj_grad = dot(xs, grad_proj, TN)
    zeros = jnp.zeros((CONVK + 1, DI), f32)
    vecs = jnp.concatenate([p[3] for p in parts], axis=1)
    small_grad = jnp.concatenate(
        [
            xproj_grad,
            jnp.concatenate([p[1] for p in parts], axis=0),
            zeros.T,
            vecs[0][:, None],
            jnp.concatenate([p[2] for p in parts], axis=1).T,
            vecs[1][:, None],
        ],
        axis=1,
    ).astype(b16)
    small_grad = jnp.pad(small_grad, ((0, 0), (0, PACK - used)))
    small_grad, grad_proj = held_for(small_grad, grad_proj)
    small_sum = lax.psum_scatter(small_grad, ALL, scatter_dimension=0, tiled=True).astype(f32)
    grad_normed, conv_parts, conv_grads = 0.0, [], []
    for part in range(SPLITS):
        gext, gvec = run_conv(parts[part][0], grad_proj, xproj_full, ext, conv_w, cbias, same_wide, part)
        if part == SPLITS - 1:
            gext, small_sum = held_for(hold_all(gext, reduces), small_sum)
        conv_parts.append(dot(gext, normed_one, TN, b16))
        grad_normed = grad_normed + dot(gext, in_full[part * width : (part + 1) * width], NN)
        conv_grads.append(gvec)
    conv_all, grad_normed = held_for(jnp.concatenate(conv_parts, axis=0), grad_normed)
    conv_own = lax.psum_scatter(conv_all, ("seq", "expert"), scatter_dimension=0, tiled=True)
    is_gate = lax.axis_index("dp") == 1
    in_sum = jnp.where(is_gate, gate_own, conv_own).astype(f32)
    in_sum = in_sum + ring(jnp.where(is_gate, conv_own, gate_own), "dp", 1).astype(f32)

    over = grad_normed[:skip_rows].reshape(halo, seqs, HALVES, D)
    from_next = shifted(over[:, :, 0], "seq", -1)
    edge = jnp.stack([over[:, :, 1], from_next], axis=2).reshape(skip_rows, D)
    grad_normed = grad_normed[skip_rows:] + grad_normed_z
    grad_normed = grad_normed + jnp.pad(edge, ((rows - skip_rows, 0), (0, 0)))
    inv_rows = inv_one[skip_rows:]
    gain_one_grad = jnp.sum(grad_normed * (tokens_rows * inv_rows), axis=0)
    scaled_one = grad_normed * gain_one
    grad_tokens = (
        grad_first + inv_rows * scaled_one
        - tokens_rows * (inv_rows * inv_rows * inv_rows * jnp.mean(scaled_one * tokens_rows, axis=-1, keepdims=True))
    )
    conv_grad = jnp.concatenate(conv_grads, axis=1)[: CONVK + 1]
    flat = jnp.concatenate([gain_one_grad, gain_two_grad, router_grad.reshape(-1), conv_grad.reshape(-1)])
    flat = sum_everywhere(flat.reshape(-1, LANES)).reshape(-1)
    gain_one_sum, gain_two_sum = flat[:D], flat[D : 2 * D]
    router_sum = flat[2 * D : (2 + EXPERTS) * D].reshape(D, EXPERTS)
    conv_sum = flat[(2 + EXPERTS) * D :].reshape(CONVK + 1, DI)
    place = (lax.axis_index("dp") * lax.axis_size("seq") + lax.axis_index("seq")) * peers + lax.axis_index("expert")
    channels = own // 2
    conv_sum = lax.dynamic_slice_in_dim(conv_sum, place * channels, channels, axis=1)

    small_sum = small_sum.T
    return (
        from_rows(output, seqs),
        from_rows(grad_tokens, seqs),
        gain_one_sum,
        in_sum.T,
        conv_sum[:CONVK],
        conv_sum[CONVK],
        small_sum[:XW].T,
        small_sum[XW : XW + DTR],
        small_sum[at + CONVK + 1],
        small_sum[at + CONVK + 2 : at + CONVK + 2 + NSTATE],
        small_sum[used - 1],
        out_sum.astype(f32),
        gain_two_sum,
        router_sum,
        jnp.stack([r.finish().T for r in reduces[0::2]]),
        jnp.stack([r.finish() for r in reduces[1::2]]),
    )


def solution(mesh):
    batch = ("dp", "expert")
    split = ("dp", "seq")
    return jax.shard_map(
        local,
        mesh=mesh,
        in_specs=(
            P(batch, "seq", None),
            P(batch, "seq"),
            P(batch, "seq", None),
            P(batch, "seq"),
            P(batch, "seq", None),
            P(),
            P(None, ALL),
            P(None, ALL),
            P(ALL),
            P(ALL, None),
            P(None, ALL),
            P(ALL),
            P(None, ALL),
            P(ALL),
            P(ALL, None),
            P(),
            P(),
            P("expert", None, split),
            P("expert", split, None),
        ),
        out_specs=(
            P(batch, "seq", None),
            P(batch, "seq", None),
            P(),
            P(None, ALL),
            P(None, ALL),
            P(ALL),
            P(ALL, None),
            P(None, ALL),
            P(ALL),
            P(None, ALL),
            P(ALL),
            P(ALL, None),
            P(),
            P(),
            P("expert", None, split),
            P("expert", split, None),
        ),
        check_vma=False,
    )
```

```python
import functools

import jax
import jax.numpy as jnp
from jax import lax
from jax.experimental import pallas as pl
from jax.experimental.pallas import tpu as pltpu
from jax.sharding import PartitionSpec as P

D = 1152
DI = 2304
NSTATE = 16
DTR = 72
CONVK = 4
EXPERTS = 8
XW = DTR + 2 * NSTATE
HALVES = 2
LANES = 128
LN2 = 0.6931471805599453
SPLITS = 3
SUB = 8
PACK = 256
CHUNK = 16
BIG = 1e30
VMEM = 60 * 1024 * 1024

norm_eps = 1e-05
ALL = ("dp", "seq", "expert")


def shifted(value, axis, steps):
    count = lax.axis_size(axis)
    first, last = (max(0, -steps), min(count, count - steps))
    return lax.ppermute(value, axis, [(source, source + steps) for source in range(first, last)])


def dot(left, right, dims, out=jnp.float32):
    return lax.dot_general(left, right, (dims, ((), ())), preferred_element_type=out)


NN = ((1,), (0,))
NT = ((1,), (1,))
TN = ((0,), (0,))


def to_rows(value):
    seqs, length = value.shape[:2]
    rest = value.shape[2:]
    split = value.reshape((seqs, HALVES, length // HALVES) + rest)
    return jnp.moveaxis(split, 2, 0).reshape((seqs * length,) + rest)


def from_rows(value, seqs):
    rest = value.shape[1:]
    length = value.shape[0] // seqs
    split = value.reshape((length // HALVES, seqs, HALVES) + rest)
    return jnp.moveaxis(split, 0, 2).reshape((seqs, length) + rest)


def to_ext_rows(value, halo):
    seqs, length = value.shape[:2]
    rest = value.shape[2:]
    part = length // HALVES
    ext = jnp.concatenate([halo, value], axis=1)
    split = jnp.stack([ext[:, h * part : h * part + part + CONVK - 1] for h in range(HALVES)], axis=1)
    return jnp.moveaxis(split, 2, 0).reshape(((part + CONVK - 1) * seqs * HALVES,) + rest)


def decay_rates(alog_ref, a_s):
    rates = -(1.0 / LN2) * jnp.exp(alog_ref[...].astype(jnp.float32))
    for n in range(NSTATE):
        a_s[n] = jnp.broadcast_to(rates[n : n + 1, :], (SUB, LANES))


def spread(src_ref, dst, first):
    src = src_ref[...]
    high = src.astype(jnp.bfloat16)
    both = jnp.concatenate([high, (src - high.astype(jnp.float32)).astype(jnp.bfloat16)], axis=1)
    line = lax.broadcasted_iota(jnp.int32, (4 * NSTATE, LANES), 0)

    def body(n, carry):
        pick = (line == first + n) | (line == 2 * NSTATE + first + n)
        dst[n] = dot(both, jnp.where(pick, 1.0, 0.0).astype(jnp.bfloat16), NN)
        return carry

    lax.fori_loop(0, NSTATE, body, 0)


def tree_sum(parts):
    while len(parts) > 1:
        parts = [parts[i] + parts[i + 1] if i + 1 < len(parts) else parts[i] for i in range(0, len(parts), 2)]
    return parts[0]


UNROLL = 8


def unrolled(first, count, body, carry):
    def group(i, inner):
        for u in range(UNROLL):
            inner = body(first + i * UNROLL + u, inner)
        return inner

    return lax.fori_loop(0, count // UNROLL, group, carry)


def row_at(t):
    return pl.ds(pl.multiple_of(t * SUB, SUB), SUB)


def end_kernel(xs_ref, din_ref, dtw_ref, dtb_ref, alog_ref, bc_ref, cut_ref, delta_ref, end_ref, sum_ref, b_s, a_s, dx_s):
    steps = delta_ref.shape[0] // SUB

    @pl.when(pl.program_id(0) == 0)
    def _():
        spread(bc_ref, b_s, 0)

    decay_rates(alog_ref, a_s)
    pre = dot(din_ref[...], dtw_ref[...], NT) + dtb_ref[...].astype(jnp.float32)
    low = jnp.exp(-jnp.abs(pre))
    delta = jnp.maximum(pre, 0.0) + jnp.where(low < 0.01, low * (1.0 - low * (0.5 - low * (1.0 / 3.0))), jnp.log(1.0 + low))
    delta_ref[...] = delta
    dx_s[...] = delta * xs_ref[...].astype(jnp.float32)
    rates = [a_s[n] for n in range(NSTATE)]

    def body(t, carry):
        total, state = carry
        at = row_at(t)
        step = jnp.maximum(delta_ref[at, :], cut_ref[at, :])
        dx = dx_s[at, :]
        state = [jnp.exp2(step * rates[n]) * state[n] + dx * b_s[n, at, :] for n in range(NSTATE)]
        return (total + step, state)

    zero = jnp.zeros((SUB, LANES), jnp.float32)
    total, state = unrolled(0, steps, body, (zero, [zero] * NSTATE))
    sum_ref[...] = total
    for n in range(NSTATE):
        end_ref[n] = state[n]


def out_kernel(xs_ref, delta_ref, alog_ref, bc_ref, cut_ref, start_ref, z_ref, skip_ref, branch_ref, ssm_ref, held_ref, b_s, c_s, a_s, dx_s, y_s):
    steps = delta_ref.shape[0] // SUB

    @pl.when(pl.program_id(0) == 0)
    def _():
        spread(bc_ref, b_s, 0)
        spread(bc_ref, c_s, NSTATE)

    decay_rates(alog_ref, a_s)
    xs = xs_ref[...].astype(jnp.float32)
    dx_s[...] = delta_ref[...] * xs
    rates = [a_s[n] for n in range(NSTATE)]

    def body(t, state):
        at = row_at(t)
        step = jnp.maximum(delta_ref[at, :], cut_ref[at, :])
        dx = dx_s[at, :]
        state = [jnp.exp2(step * rates[n]) * state[n] + dx * b_s[n, at, :] for n in range(NSTATE)]
        y_s[at, :] = tree_sum([state[n] * c_s[n, at, :] for n in range(NSTATE)])
        return state

    def chunk(i, state):
        for n in range(NSTATE):
            held_ref[i, n] = state[n]
        return unrolled(i * CHUNK, CHUNK, body, state)

    lax.fori_loop(0, steps // CHUNK, chunk, [start_ref[n] for n in range(NSTATE)])
    ssm = y_s[...] + skip_ref[...].astype(jnp.float32) * xs
    z = z_ref[...]
    ssm_ref[...] = ssm.astype(jnp.bfloat16)
    branch_ref[...] = (ssm * (z / (1.0 + jnp.exp(-z)))).astype(jnp.bfloat16)


def first_kernel(delta_ref, alog_ref, bc_ref, cut_ref, gb_ref, z_ref, ssm_ref, lead_ref, gz_ref, g_s, c_s, a_s):
    steps = delta_ref.shape[0] // SUB

    @pl.when(pl.program_id(0) == 0)
    def _():
        spread(bc_ref, c_s, NSTATE)

    decay_rates(alog_ref, a_s)
    z = z_ref[...]
    grad = gb_ref[...]
    sig = 1.0 / (1.0 + jnp.exp(-z))
    g_s[...] = grad * (z * sig)
    gz_ref[...] = (grad * ssm_ref[...].astype(jnp.float32) * (sig * (1.0 + z * (1.0 - sig)))).astype(jnp.bfloat16)
    rates = [a_s[n] for n in range(NSTATE)]

    def body(k, lead):
        at = row_at(steps - 1 - k)
        step = jnp.maximum(delta_ref[at, :], cut_ref[at, :])
        g = g_s[at, :]
        return [jnp.exp2(step * rates[n]) * (lead[n] + g * c_s[n, at, :]) for n in range(NSTATE)]

    zero = jnp.zeros((SUB, LANES), jnp.float32)
    lead = unrolled(0, steps, body, [zero] * NSTATE)
    for n in range(NSTATE):
        lead_ref[n] = lead[n]


def back_kernel(
    xs_ref, delta_ref, alog_ref, bc_ref, cut_ref, g_ref, skip_ref, held_ref, last_ref,
    gxs_ref, gpre_ref, galog_ref, gvec_ref, gbc_ref,
    b_s, c_s, gb_s, gc_s, a_s, dx_s, x_s, gx_s, gd_s, hd_s, dec_s,
):
    steps = delta_ref.shape[0] // SUB

    @pl.when(pl.program_id(0) == 0)
    def _():
        spread(bc_ref, b_s, 0)
        spread(bc_ref, c_s, NSTATE)
        gb_s[...] = jnp.zeros_like(gb_s)
        gc_s[...] = jnp.zeros_like(gc_s)

    decay_rates(alog_ref, a_s)
    xs = xs_ref[...].astype(jnp.float32)
    x_s[...] = xs
    dx_s[...] = delta_ref[...] * xs

    def ahead(j, state, base):
        at = row_at(base + j)
        step = jnp.maximum(delta_ref[at, :], cut_ref[at, :])
        dx = dx_s[at, :]
        g = g_ref[at, :]
        new = []
        for n in range(NSTATE):
            dec = jnp.exp2(step * a_s[n])
            hd = dec * state[n]
            dec_s[j, n] = dec
            hd_s[j, n] = hd
            h = hd + dx * b_s[n, at, :]
            gc_s[n, at, :] = gc_s[n, at, :] + g * h
            new.append(h)
        return new

    def behind(k, carry, base):
        coming, rate_grad = carry
        j = CHUNK - 1 - k
        at = row_at(base + j)
        delta = delta_ref[at, :]
        dx = dx_s[at, :]
        g = g_ref[at, :]
        next_coming, next_rate, with_b, with_a = [], [], [], []
        for n in range(NSTATE):
            lam = coming[n] + g * c_s[n, at, :]
            with_b.append(lam * b_s[n, at, :])
            gb_s[n, at, :] = gb_s[n, at, :] + lam * dx
            q = lam * hd_s[j, n]
            with_a.append(q * a_s[n])
            next_rate.append(rate_grad[n] + delta * q)
            next_coming.append(lam * dec_s[j, n])
        by_b = tree_sum(with_b)
        gx_s[at, :] = by_b * delta
        gd_s[at, :] = by_b * x_s[at, :] + LN2 * tree_sum(with_a)
        return (next_coming, next_rate)

    chunks = steps // CHUNK

    def chunk(i, carry):
        c = chunks - 1 - i
        base = c * CHUNK
        unrolled(0, CHUNK, functools.partial(ahead, base=base), [held_ref[c, n] for n in range(NSTATE)])
        return unrolled(0, CHUNK, functools.partial(behind, base=base), carry)

    zero = jnp.zeros((SUB, LANES), jnp.float32)
    _, rate_grad = lax.fori_loop(0, chunks, chunk, ([last_ref[n] for n in range(NSTATE)], [zero] * NSTATE))
    for n in range(NSTATE):
        galog_ref[n : n + 1, :] = LN2 * jnp.sum(rate_grad[n] * a_s[n], axis=0, keepdims=True)
    skip = skip_ref[...].astype(jnp.float32)
    grad_ssm = g_ref[...]
    gxs_ref[...] = gx_s[...] + grad_ssm * skip
    delta = delta_ref[...]
    slope = jnp.where(delta < 0.01, delta * (1.0 - 0.5 * delta * (1.0 - delta * (1.0 / 3.0))), 1.0 - jnp.exp(-delta))
    gpre = gd_s[...] * slope
    gpre_ref[...] = gpre.astype(jnp.bfloat16)
    gvec_ref[0:1, :] = jnp.sum(gpre, axis=0, keepdims=True)
    gvec_ref[1:2, :] = jnp.sum(grad_ssm * xs, axis=0, keepdims=True)
    gvec_ref[2:SUB, :] = jnp.zeros((SUB - 2, LANES), jnp.float32)

    @pl.when(pl.program_id(0) == pl.num_programs(0) - 1)
    def _():
        lane = lax.broadcasted_iota(jnp.int32, (LANES, LANES), 1)
        gbc_ref[...] = jnp.zeros_like(gbc_ref)

        def gather(n, carry):
            for part, first in ((gb_s, 0), (gc_s, NSTATE)):
                pick = jnp.where(lane == first + n, 1.0, 0.0).astype(jnp.bfloat16)
                gbc_ref[...] += dot(part[n].astype(jnp.bfloat16), pick, NN)
            return carry

        lax.fori_loop(0, NSTATE, gather, 0)


def col_spec(rows):
    return pl.BlockSpec((rows, LANES), lambda c: (0, c))


def full_spec(shape):
    return pl.BlockSpec(shape, lambda c: (0,) * len(shape))


def state_spec():
    return pl.BlockSpec((NSTATE, SUB, LANES), lambda c: (0, 0, c))


def params():
    return pltpu.CompilerParams(vmem_limit_bytes=VMEM)


def f32s(*shape):
    return jax.ShapeDtypeStruct(shape, jnp.float32)


def b16s(*shape):
    return jax.ShapeDtypeStruct(shape, jnp.bfloat16)


def vm(*shape):
    return pltpu.VMEM(shape, jnp.float32)


def cost(rows, width, per_value):
    work = rows * width * NSTATE
    return pl.CostEstimate(flops=work * 8, bytes_accessed=work * per_value, transcendentals=work)


def run_end(xs, din, dtw, dtb, alog, bc, cut):
    rows = xs.shape[0]
    return pl.pallas_call(
        end_kernel,
        grid=(DI // LANES,),
        in_specs=[
            col_spec(rows), full_spec(din.shape), pl.BlockSpec((LANES, DTR), lambda c: (c, 0)),
            col_spec(1), col_spec(NSTATE), full_spec(bc.shape), full_spec(cut.shape),
        ],
        out_specs=[col_spec(rows), state_spec(), col_spec(SUB)],
        out_shape=[f32s(rows, DI), f32s(NSTATE, SUB, DI), f32s(SUB, DI)],
        scratch_shapes=[vm(NSTATE, rows, LANES), vm(NSTATE, SUB, LANES), vm(rows, LANES)],
        compiler_params=params(),
        cost_estimate=cost(rows, DI, 4),
        name="end",
    )(xs, din, dtw, dtb, alog, bc, cut)


def run_out(xs, delta, alog, bc, cut, start, z, skip):
    rows = xs.shape[0]
    chunks = rows // SUB // CHUNK
    return pl.pallas_call(
        out_kernel,
        grid=(DI // LANES,),
        in_specs=[
            col_spec(rows), col_spec(rows), col_spec(NSTATE), full_spec(bc.shape), full_spec(cut.shape),
            state_spec(), col_spec(rows), col_spec(1),
        ],
        out_specs=[
            col_spec(rows), col_spec(rows),
            pl.BlockSpec((chunks, NSTATE, SUB, LANES), lambda c: (0, 0, 0, c)),
        ],
        out_shape=[b16s(rows, DI), b16s(rows, DI), f32s(chunks, NSTATE, SUB, DI)],
        scratch_shapes=[
            vm(NSTATE, rows, LANES), vm(NSTATE, rows, LANES), vm(NSTATE, SUB, LANES), vm(rows, LANES), vm(rows, LANES),
        ],
        compiler_params=params(),
        cost_estimate=cost(rows, DI, 5),
        name="out",
    )(xs, delta, alog, bc, cut, start, z, skip)


def run_first(delta, alog, bc, cut, gbranch, z, ssm):
    rows = delta.shape[0]
    return pl.pallas_call(
        first_kernel,
        grid=(DI // LANES,),
        in_specs=[
            col_spec(rows), col_spec(NSTATE), full_spec(bc.shape), full_spec(cut.shape), col_spec(rows), col_spec(rows),
            col_spec(rows),
        ],
        out_specs=[state_spec(), col_spec(rows), col_spec(rows)],
        out_shape=[f32s(NSTATE, SUB, DI), b16s(rows, DI), f32s(rows, DI)],
        scratch_shapes=[vm(NSTATE, rows, LANES), vm(NSTATE, SUB, LANES)],
        compiler_params=params(),
        cost_estimate=cost(rows, DI, 4),
        name="first",
    )(delta, alog, bc, cut, gbranch, z, ssm)


def run_back(xs, delta, alog, bc, cut, grad_ssm, skip, held, last, part):
    rows = xs.shape[0]
    chunks = rows // SUB // CHUNK
    big = (NSTATE, rows, LANES)
    row = (rows, LANES)
    width = DI // SPLITS
    first = part * (width // LANES)

    def col(count):
        return pl.BlockSpec((count, LANES), lambda c: (0, c + first))

    return pl.pallas_call(
        back_kernel,
        grid=(width // LANES,),
        in_specs=[
            col(rows), col(rows), col(NSTATE), full_spec(bc.shape), full_spec(cut.shape), col(rows), col(1),
            pl.BlockSpec((chunks, NSTATE, SUB, LANES), lambda c: (0, 0, 0, c + first)),
            pl.BlockSpec((NSTATE, SUB, LANES), lambda c: (0, 0, c + first)),
        ],
        out_specs=[col_spec(rows), col_spec(rows), col_spec(NSTATE), col_spec(SUB), full_spec(row)],
        out_shape=[f32s(rows, width), b16s(rows, width), f32s(NSTATE, width), f32s(SUB, width), f32s(*row)],
        scratch_shapes=[
            vm(*big), vm(*big), vm(*big), vm(*big), vm(NSTATE, SUB, LANES),
            vm(*row), vm(*row), vm(*row), vm(*row),
            vm(CHUNK, NSTATE, SUB, LANES), vm(CHUNK, NSTATE, SUB, LANES),
        ],
        compiler_params=params(),
        cost_estimate=cost(rows, width, 17),
        name="back",
    )(xs, delta, alog, bc, cut, grad_ssm, skip, held, last)


def conv_kernel(gxs_ref, gproj_ref, xproj_ref, ext_ref, taps_ref, bias_ref, same_ref, gext_ref, gvec_ref, acc_s):
    rows = gxs_ref.shape[0]
    halo = CONVK - 1
    taps = taps_ref[...]
    bias = bias_ref[...]
    pieces = []
    conv = bias
    for k in range(CONVK):
        piece = ext_ref[k * SUB : k * SUB + rows, :]
        if k < halo:
            piece = piece * same_ref[k]
        pieces.append(piece)
        conv = conv + taps[k : k + 1, :] * piece
    sig = 1.0 / (1.0 + jnp.exp(-conv))
    grad = gxs_ref[...] + dot(gproj_ref[...], xproj_ref[...], NT)
    grad = grad * (sig * (1.0 + conv * (1.0 - sig)))
    acc_s[...] = jnp.zeros_like(acc_s)
    for k in range(CONVK):
        gvec_ref[k : k + 1, :] = jnp.sum(grad * pieces[k], axis=0, keepdims=True)
        part = taps[k : k + 1, :] * grad
        if k < halo:
            part = part * same_ref[k]
        acc_s[k * SUB : k * SUB + rows, :] += part
    gvec_ref[CONVK : CONVK + 1, :] = jnp.sum(grad, axis=0, keepdims=True)
    gvec_ref[CONVK + 1 : SUB, :] = jnp.zeros((SUB - CONVK - 1, LANES), jnp.float32)
    gext_ref[...] = acc_s[...].astype(jnp.bfloat16)


def run_conv(gxs, gproj, xproj, ext, taps, bias, same, part):
    rows, width = gxs.shape
    long = ext.shape[0]
    first = part * (width // LANES)

    def col(count):
        return pl.BlockSpec((count, LANES), lambda c: (0, c + first))

    return pl.pallas_call(
        conv_kernel,
        grid=(width // LANES,),
        in_specs=[
            col_spec(rows), full_spec(gproj.shape), pl.BlockSpec((LANES, XW), lambda c: (c + first, 0)), col(long),
            col(CONVK), col(1), full_spec(same.shape),
        ],
        out_specs=[col_spec(long), col_spec(SUB)],
        out_shape=[b16s(long, width), f32s(SUB, width)],
        scratch_shapes=[vm(long, LANES)],
        compiler_params=params(),
        cost_estimate=pl.CostEstimate(flops=rows * width * 260, bytes_accessed=rows * width * 10, transcendentals=rows * width),
        name="conv",
    )(gxs, gproj, xproj, ext, taps, bias, same)


def gelu_pair(v):
    inner = 0.7978845608 * (v + 0.044715 * v * v * v)
    t = jnp.tanh(inner)
    value = 0.5 * v * (1.0 + t)
    slope = 0.5 * (1.0 + t) + 0.5 * v * (1.0 - t * t) * (0.7978845608 * (1.0 + 3.0 * 0.044715 * v * v))
    return value, slope


def expert_kernel(blocks, peers, split_last, final, *refs):
    count = blocks + (1 if split_last else 0)
    weights, refs = refs[:count], refs[count:]
    xs, gs, refs = refs[:peers], refs[peers : 2 * peers], refs[2 * peers :]
    if final:
        before, refs = refs[:2], refs[2:]
    out_refs, (upg_ref, downg_ref), refs = refs[:2], refs[2:4], refs[4:]
    x_s, g_s, up_s, down_s, hid_s, pre_s, acc_y, acc_g = refs
    cap = xs[0].shape[1]
    size = weights[0].shape[1]
    expert, half = pl.program_id(0), pl.program_id(1)

    @pl.when(half == 0)
    def _():
        for d in range(peers):
            at = slice(d * cap, (d + 1) * cap)
            piece = xs[d][0]
            x_s[at, :] = piece[:, :D]
            gate = jnp.sum(piece[:, D:].astype(jnp.float32), axis=1, keepdims=True)
            g_s[at, :] = (gate * gs[d][0].astype(jnp.float32)).astype(jnp.bfloat16)
        if final:
            acc_y[...] = before[0][0].astype(jnp.float32)
            acc_g[...] = before[1][0].astype(jnp.float32)
        else:
            acc_y[...] = jnp.zeros_like(acc_y)
            acc_g[...] = jnp.zeros_like(acc_g)

    def place(k, ref):
        at = slice(k * size, (k + 1) * size)
        up_s[at, :] = ref[0]
        down_s[at, :] = ref[1]

    for h in range(2):

        @pl.when(half == h)
        def _():
            for k in range(blocks // 2):
                block = h * (blocks // 2) + k
                if split_last and block == blocks - 1:
                    for e in range(2):
                        pl.when(expert == e)(functools.partial(place, k, weights[block + e]))
                else:
                    place(k, weights[block])

    rows = cap * peers
    tile = rows // 3
    cols = up_s.shape[0]

    def body(r, carry):
        at = pl.ds(pl.multiple_of(r * tile, tile), tile)
        value, slope = gelu_pair(dot(x_s[at, :], up_s[...], NT))
        hidden = value.astype(jnp.bfloat16)
        grad_pre = (slope * dot(g_s[at, :], down_s[...], NT)).astype(jnp.bfloat16)
        hid_s[at, :] = hidden
        pre_s[at, :] = grad_pre
        acc_y[at, :] += dot(hidden, down_s[...], NN)
        acc_g[at, :] += dot(grad_pre, up_s[...], NN)
        return carry

    lax.fori_loop(0, 3, body, 0)
    wide = cols // 3

    def grads(c, carry):
        at = pl.ds(pl.multiple_of(c * wide, wide), wide)
        upg_ref[0, at, :] = dot(pre_s[:, at], x_s[...], TN).astype(jnp.bfloat16)
        downg_ref[0, at, :] = dot(hid_s[:, at], g_s[...], TN).astype(jnp.bfloat16)
        return carry

    lax.fori_loop(0, 3, grads, 0)

    @pl.when(half == 1)
    def _():
        out_refs[0][0] = acc_y[...].astype(jnp.bfloat16)
        out_refs[1][0] = acc_g[...].astype(jnp.bfloat16)


def run_experts(weights, split_last, xs, gs, before):
    blocks = len(weights) - (1 if split_last else 0)
    peers = len(xs)
    count, cap = xs[0].shape[:2]
    size = weights[0].shape[1]
    rows, cols = peers * cap, blocks * size
    final = before is not None

    def pick(shape, **more):
        return pl.BlockSpec((1,) + shape, lambda e, h: (e, 0, 0), **more)

    once = dict(pipeline_mode=pl.Buffered(1))
    pair = pl.BlockSpec((2, size, D), lambda e, h: (e, 0, 0))
    half = pl.BlockSpec((2, size, D), lambda e, h: (0, 0, 0), **once)
    in_specs = [pair] * (blocks - 1 if split_last else blocks) + ([half] * 2 if split_last else [])
    in_specs += [pick(xs[0].shape[1:])] * peers + [pick(gs[0].shape[1:])] * peers
    in_specs += [pick((rows, D), **once)] * (2 if final else 0)
    low = functools.partial(pltpu.VMEM, dtype=jnp.bfloat16)
    work = 12 * count * rows * cols * D
    grads = pl.BlockSpec((1, cols // 2, D), lambda e, h: (e, h, 0))
    return pl.pallas_call(
        functools.partial(expert_kernel, blocks, peers, split_last, final),
        grid=(count, 2),
        in_specs=in_specs,
        out_specs=[pick((rows, D))] * 2 + [grads] * 2,
        out_shape=[b16s(count, rows, D)] * 2 + [b16s(count, cols, D)] * 2,
        scratch_shapes=[
            low((rows, D)), low((rows, D)), low((cols // 2, D)), low((cols // 2, D)),
            low((rows, cols // 2)), low((rows, cols // 2)), vm(rows, D), vm(rows, D),
        ],
        compiler_params=params(),
        cost_estimate=pl.CostEstimate(flops=work, bytes_accessed=count * (4 * cols + 8 * rows) * D * 2, transcendentals=count * rows * cols),
        name="experts",
    )(*weights, *xs, *gs, *(before or ()))


def halves_of(value, seqs):
    split = value.reshape(value.shape[:-2] + (seqs, HALVES, value.shape[-1]))
    return split[..., 0, :], split[..., 1, :]


def join_halves(first, second):
    both = jnp.stack([first, second], axis=-2)
    return both.reshape(both.shape[:-3] + (both.shape[-3] * HALVES, both.shape[-1]))


def chained(own, decay, steps):
    start = jnp.zeros_like(own)
    carry = own
    for k in range(lax.axis_size("seq") - 1):
        start = shifted(carry.astype(jnp.bfloat16), "seq", steps).astype(jnp.float32)
        carry = own + decay * start
    return start


def start_states(ends, sums, rates, seqs):
    end_0, end_1 = halves_of(ends, seqs)
    sum_0, sum_1 = halves_of(sums, seqs)
    decay_0 = jnp.exp(rates * sum_0)
    decay_1 = jnp.exp(rates * sum_1)
    start = chained(decay_1 * end_0 + end_1, decay_0 * decay_1, 1)
    return join_halves(start, decay_0 * start + end_0), (decay_0, decay_1)


def last_grads(leads, decays, seqs):
    decay_0, decay_1 = decays
    lead_0, lead_1 = halves_of(leads, seqs)
    last = chained(lead_0 + decay_0 * lead_1, decay_0 * decay_1, -1)
    return join_halves(lead_1 + decay_1 * last, last)


def ring(value, axis, step):
    count = lax.axis_size(axis)
    return lax.ppermute(value, axis, [(i, (i + step) % count) for i in range(count)])


def partner(value, axis, bits):
    count = lax.axis_size(axis)
    return lax.ppermute(value, axis, [(i, i ^ bits) for i in range(count)])


def held_for(first, *others):
    flat, tree = jax.tree.flatten((first,) + others)
    return jax.tree.unflatten(tree, lax.optimization_barrier(flat))


class Gather:
    def __init__(self, own):
        self.here, self.there = [own], []
        self.peers = lax.axis_size("seq")

    def step(self):
        at = len(self.there)
        block = self.here[at]
        if at < self.peers - 1:
            self.there.append(ring(block, "dp", 1))
            self.here.append(ring(block, "seq", 1))
        else:
            half = block.shape[0] // 2
            self.there.append([ring(block[:half], "dp", 1), ring(self.there[-1][half:], "seq", 1)])

    def hold(self, value):
        value, here, there = held_for(value, self.here[1:], self.there)
        self.here[1:], self.there = here, there
        return value

    def done(self):
        return len(self.there) == self.peers


class Reduce:
    def __init__(self, here, there, x_first):
        self.peers = lax.axis_size("seq")
        here = here.reshape(self.peers, -1, D)
        there = there.reshape(self.peers, -1, D)
        self.x_first, self.k, self.total = x_first, self.peers, None
        self.blocks = [(here[k], there[k]) for k in range(self.peers)]
        if x_first:
            self.moving = ring(there, "dp", 1)
        else:
            self.advance()

    def term(self, k):
        if self.x_first:
            return self.blocks[k][0].astype(jnp.float32) + self.other[k].astype(jnp.float32)
        return jnp.stack(self.blocks[k]).astype(jnp.float32)

    def advance(self):
        self.k -= 1
        self.total = self.term(self.k) if self.total is None else self.term(self.k) + self.moving.astype(jnp.float32)
        if self.k > 0:
            self.moving = ring(self.total.astype(jnp.bfloat16), "seq", -1)
        elif self.x_first:
            self.moving = None
        else:
            self.moving = ring(self.total[1].astype(jnp.bfloat16), "dp", 1)

    def step(self):
        if self.moving is None:
            return
        if self.x_first and self.total is None:
            self.other = self.moving
            self.advance()
        elif self.k > 0:
            self.advance()
        else:
            self.total = self.total[0] + self.moving.astype(jnp.float32)
            self.moving = None

    def finish(self):
        while self.moving is not None:
            self.step()
        return self.total


def settle(value, reduces):
    live = [r for r in reduces if r.moving is not None]
    value, moved = held_for(value, [r.moving for r in live])
    for r, m in zip(live, moved):
        r.moving = m
    return value


def hold_all(value, reduces):
    live = [r for r in reduces if r.moving is not None]
    value, moved = held_for(value, [r.moving for r in live])
    for r, m in zip(live, moved):
        r.moving = m
        r.step()
    return value


def halved(value, axis):
    index, bits = lax.axis_index(axis), lax.axis_size(axis) // 2
    while bits >= 1:
        pair = value.reshape((2, bits) + value.shape[1:])
        high = (index // bits) % 2 == 1
        keep = jnp.where(high, pair[1], pair[0])
        send = jnp.where(high, pair[0], pair[1])
        value = keep.astype(jnp.float32) + partner(send.astype(jnp.bfloat16), axis, bits).astype(jnp.float32)
        bits //= 2
    return value[0]


def sum_everywhere(value):
    for axis in ALL:
        bits = 1
        while bits < lax.axis_size(axis):
            value = value + partner(value, axis, bits)
            bits *= 2
    return value


def exchange(blocks):
    return [blocks[0]] + [partner(blocks[d], "expert", d) for d in range(1, len(blocks))]


def local(
    tokens, segment_ids, routes, keep_mask, out_grad, norm_one, in_proj, conv_weight, conv_bias, x_proj,
    dt_proj, dt_bias, a_log, d_skip, out_proj, norm_two, router, expert_up, expert_down,
):
    seqs, length = tokens.shape[:2]
    rows = seqs * length
    steps = length // HALVES
    halo = CONVK - 1
    capacity = seqs * max(2, length * 3 // 16)
    f32, b16 = jnp.float32, jnp.bfloat16
    own = in_proj.shape[1]

    small = jnp.concatenate(
        [x_proj, dt_proj.T, conv_weight.T, conv_bias[:, None], dt_bias[:, None], a_log.T, d_skip[:, None]], axis=1
    )
    used = small.shape[1]
    small = jnp.pad(small, ((0, 0), (0, PACK - used)))
    entry = lax.all_gather(jnp.concatenate([in_proj.T, small.reshape(-1, D)], axis=0), ALL, axis=0, tiled=False)
    in_full = entry[:, :own].reshape(2 * DI, D)
    small = entry[:, own:].reshape(DI, PACK)
    out_full = lax.all_gather(out_proj, ALL, axis=0, tiled=True)
    local_experts = expert_up.shape[0]
    shard = jnp.stack([m for e in range(local_experts) for m in (expert_up[e].T, expert_down[e])])
    shard, in_full = held_for(shard, in_full)
    gather = Gather(shard)
    gather.step()

    xproj_full = small[:, :XW]
    dtw = small[:, XW : XW + DTR]
    at = XW + DTR
    rest = small[:, at:used].T
    conv_w = rest[:CONVK].astype(f32)
    cbias = rest[CONVK : CONVK + 1].astype(f32)
    dtb = rest[CONVK + 1 : CONVK + 2]
    alog = rest[CONVK + 2 : CONVK + 2 + NSTATE]
    skip = rest[CONVK + 2 + NSTATE :]

    halo_tokens = shifted(tokens[:, length - halo :], "seq", 1)
    halo_segs = shifted(segment_ids[:, length - halo :].astype(f32), "seq", 1)
    inputs = to_ext_rows(tokens, halo_tokens).astype(f32)
    seg_ext = to_ext_rows(segment_ids.astype(f32), halo_segs)
    drop = to_rows(keep_mask).astype(f32)
    route = to_rows(routes[..., 0])
    grad_low = to_rows(out_grad)
    grad_final = grad_low.astype(f32)
    skip_rows = halo * SUB
    seg = seg_ext[skip_rows:]
    same = [(seg_ext[k * SUB : k * SUB + rows] == seg).astype(f32)[:, None] for k in range(halo)]
    same_wide = jnp.broadcast_to(jnp.stack(same), (halo, rows, LANES))
    cut = jnp.broadcast_to((1.0 - same[halo - 1]) * BIG, (rows, LANES))

    onehot = (route[:, None] == jnp.arange(EXPERTS, dtype=jnp.int32)).astype(f32)
    order = jnp.arange(rows)
    below = (order[None, :] < order[:, None]).astype(b16)
    rank = jnp.sum(dot(below, onehot.astype(b16), NN) * onehot, axis=-1).astype(jnp.int32)
    peers = lax.axis_size("expert")
    target = (route // local_experts) ^ lax.axis_index("expert")
    slot = (target * local_experts + route % local_experts) * capacity + rank
    placing = (jnp.arange(EXPERTS * capacity, dtype=jnp.int32)[:, None] == slot[None, :]).astype(b16)

    def dispatch(values):
        sent = dot(placing, values, NN, b16).reshape(peers, local_experts, capacity, values.shape[1])
        return exchange([sent[d] for d in range(peers)])

    gain_one = norm_one.astype(f32)
    inv_one = lax.rsqrt(jnp.mean(inputs * inputs, axis=-1, keepdims=True) + norm_eps)
    normed_one = (inputs * inv_one * gain_one).astype(b16)
    ext = dot(normed_one, in_full[:DI], NT)
    gate_z = dot(normed_one[skip_rows:], in_full[DI:], NT)
    conv_out = cbias + conv_w[halo] * ext[skip_rows:]
    for k in range(halo):
        conv_out = conv_out + conv_w[k] * (same[k] * ext[k * SUB : k * SUB + rows])
    xs = jax.nn.silu(conv_out).astype(b16)
    proj = dot(xs, xproj_full, NN)
    delta_in = proj[:, :DTR].astype(b16)
    bc = proj[:, DTR:]
    grad_arrived = dispatch(grad_low)
    delta, ends, sums = run_end(xs, delta_in, dtw, dtb, alog, bc, cut)
    ends, grad_arrived = held_for(gather.hold(ends), grad_arrived)
    rates = -jnp.exp(alog.astype(f32))[:, None, :]
    starts, decays = start_states(ends, sums, rates, seqs)
    starts = gather.hold(starts)
    gather.step()
    branch, ssm, held = run_out(xs, delta, alog, bc, cut, starts, gate_z, skip)
    tokens_rows = inputs[skip_rows:]
    first_sum = tokens_rows + dot(branch, out_full, NN)

    gain_two = norm_two.astype(f32)
    inv_two = lax.rsqrt(jnp.mean(first_sum * first_sum, axis=-1, keepdims=True) + norm_eps)
    normed_two = (first_sum * inv_two * gain_two).astype(b16)
    probs = jax.nn.softmax(dot(normed_two, router, NN), axis=-1)
    gate_raw = jnp.sum(probs * onehot, axis=-1)
    gate = gate_raw * drop
    gate_high = lax.reduce_precision(gate, 8, 7)
    gate_mid = lax.reduce_precision(gate - gate_high, 8, 7)
    gate_low = gate - gate_high - gate_mid
    gates = jnp.stack([gate_high, gate_mid, gate_low], axis=1).astype(b16)
    message = jnp.concatenate([normed_two, jnp.pad(gates, ((0, 0), (0, LANES - 3)))], axis=1)
    message = gather.hold(message)
    gather.step()
    arrived = dispatch(message)
    arrived = gather.hold(arrived)
    while not gather.done():
        gather.step()
    sum_y, sum_g, up_here, down_here = run_experts(gather.here, False, arrived, grad_arrived, None)
    sum_y = gather.hold(sum_y)
    sum_y, sum_g, up_there, down_there = run_experts(
        gather.there[:-1] + gather.there[-1], True, arrived, grad_arrived, (sum_y, sum_g)
    )
    weight_grads = []
    for e in range(local_experts):
        weight_grads += [(up_here[e], up_there[e]), (down_here[e], down_there[e])]
    count = len(weight_grads)
    reduces = [Reduce(g[0], g[1], i < count - 1) for i, g in enumerate(weight_grads)]

    def send_back(parts):
        parts = parts.reshape(local_experts, peers, capacity, D)
        return exchange([parts[:, d] for d in range(peers)])

    returned_y = send_back(sum_y)
    returned_g = send_back(sum_g)

    def collect(parts):
        back_rows = jnp.stack(parts).reshape(EXPERTS * capacity, D)
        return dot(placing, back_rows, TN)

    expert_rows = collect(returned_y)
    grad_back = collect(hold_all(returned_g, reduces[-1:]))
    output = (first_sum + gate[:, None] * expert_rows).astype(b16)

    grad_gate = jnp.sum(grad_final * expert_rows, axis=-1) * drop
    grad_logits = (grad_gate * gate_raw)[:, None] * (onehot - probs)
    logits_low = grad_logits.astype(b16)
    router_grad = dot(normed_two, logits_low, TN)
    grad_two = grad_back + dot(logits_low, router, NT)
    gain_two_grad = jnp.sum(grad_two * (first_sum * inv_two), axis=0)
    scaled = grad_two * gain_two
    grad_first = (
        grad_final + inv_two * scaled
        - first_sum * (inv_two * inv_two * inv_two * jnp.mean(scaled * first_sum, axis=-1, keepdims=True))
    )
    grad_first = hold_all(grad_first, reduces[-1:])
    first_low = grad_first.astype(b16)
    out_grad_part = dot(branch, first_low, TN, b16)
    grad_branch = dot(first_low, out_full, NT)
    grad_branch, out_grad_part = held_for(grad_branch, out_grad_part)
    grad_branch = hold_all(grad_branch, reduces[:1])

    leads, grad_z, grad_ssm = run_first(delta, alog, bc, cut, grad_branch, gate_z, ssm)
    leads = settle(leads, [reduces[0], reduces[1], reduces[-1]])
    last = last_grads(leads, decays, seqs)
    last, out_grad_part = held_for(last, out_grad_part)
    out_sum = lax.psum_scatter(out_grad_part, ALL, scatter_dimension=0, tiled=True)
    gate_part = dot(grad_z, normed_one[skip_rows:], TN, b16)
    grad_normed_z = dot(grad_z, in_full[DI:], NN)
    grad_ssm, gate_part, grad_normed_z = held_for(grad_ssm, gate_part, grad_normed_z)
    gate_own = lax.psum_scatter(gate_part, ("seq", "expert"), scatter_dimension=0, tiled=True)
    grad_delta_in, gbc, parts = 0.0, 0.0, []
    width = DI // SPLITS
    for part in range(SPLITS):
        if part == 1:
            last, out_sum = held_for(last, out_sum)
        last = hold_all(last, reduces[: 2 + part] + reduces[-1:] if 2 + part < count else reduces)
        gxs, gpre, galog, gvec, gbc_part = run_back(xs, delta, alog, bc, cut, grad_ssm, skip, held, last, part)
        grad_delta_in = grad_delta_in + dot(gpre, dtw[part * width : (part + 1) * width], NN)
        gbc = gbc + gbc_part[:, : 2 * NSTATE]
        dtproj_part = dot(gpre, delta_in, TN)
        last, gxs, dtproj_part, grad_delta_in, gbc, galog, gvec = held_for(
            last, gxs, dtproj_part, grad_delta_in, gbc, galog, gvec
        )
        parts.append((gxs, dtproj_part, galog, gvec))
    grad_proj = jnp.concatenate([grad_delta_in, gbc], axis=1).astype(b16)
    grad_proj, gate_own = held_for(hold_all(grad_proj, reduces), gate_own)
    xproj_grad = dot(xs, grad_proj, TN)
    zeros = jnp.zeros((CONVK + 1, DI), f32)
    vecs = jnp.concatenate([p[3] for p in parts], axis=1)
    small_grad = jnp.concatenate(
        [
            xproj_grad,
            jnp.concatenate([p[1] for p in parts], axis=0),
            zeros.T,
            vecs[0][:, None],
            jnp.concatenate([p[2] for p in parts], axis=1).T,
            vecs[1][:, None],
        ],
        axis=1,
    ).astype(b16)
    small_grad = jnp.pad(small_grad, ((0, 0), (0, PACK - used)))
    small_grad, grad_proj = held_for(small_grad, grad_proj)
    small_sum = small_grad.reshape(lax.axis_size("dp"), lax.axis_size("seq"), peers, own // 2, PACK)
    small_sum = halved(small_sum, "dp")
    small_sum = halved(small_sum.swapaxes(0, 1), "expert")
    small_sum = halved(small_sum, "seq")
    gexts, conv_parts, conv_grads = [], [], []
    for part in range(SPLITS):
        gext, gvec = run_conv(parts[part][0], grad_proj, xproj_full, ext, conv_w, cbias, same_wide, part)
        if part == SPLITS - 1:
            gext = hold_all(gext, reduces)
        conv_parts.append(dot(gext, normed_one, TN, b16))
        gexts.append(gext)
        conv_grads.append(gvec)
    conv_all, gexts = held_for(jnp.concatenate(conv_parts, axis=0), gexts)
    grad_normed = sum(dot(gexts[k], in_full[k * width : (k + 1) * width], NN) for k in range(SPLITS))
    conv_own = lax.psum_scatter(conv_all, ("seq", "expert"), scatter_dimension=0, tiled=True)
    is_gate = lax.axis_index("dp") == 1
    in_sum = jnp.where(is_gate, gate_own, conv_own).astype(f32)
    in_sum = in_sum + ring(jnp.where(is_gate, conv_own, gate_own), "dp", 1).astype(f32)

    over = grad_normed[:skip_rows].reshape(halo, seqs, HALVES, D)
    from_next = shifted(over[:, :, 0], "seq", -1)
    edge = jnp.stack([over[:, :, 1], from_next], axis=2).reshape(skip_rows, D)
    grad_normed = grad_normed[skip_rows:] + grad_normed_z
    grad_normed = grad_normed + jnp.pad(edge, ((rows - skip_rows, 0), (0, 0)))
    inv_rows = inv_one[skip_rows:]
    gain_one_grad = jnp.sum(grad_normed * (tokens_rows * inv_rows), axis=0)
    scaled_one = grad_normed * gain_one
    grad_tokens = (
        grad_first + inv_rows * scaled_one
        - tokens_rows * (inv_rows * inv_rows * inv_rows * jnp.mean(scaled_one * tokens_rows, axis=-1, keepdims=True))
    )
    conv_grad = jnp.concatenate(conv_grads, axis=1)[: CONVK + 1]
    flat = jnp.concatenate([gain_one_grad, gain_two_grad, router_grad.reshape(-1), conv_grad.reshape(-1)])
    flat = sum_everywhere(flat.reshape(-1, LANES)).reshape(-1)
    gain_one_sum, gain_two_sum = flat[:D], flat[D : 2 * D]
    router_sum = flat[2 * D : (2 + EXPERTS) * D].reshape(D, EXPERTS)
    conv_sum = flat[(2 + EXPERTS) * D :].reshape(CONVK + 1, DI)
    place = (lax.axis_index("dp") * lax.axis_size("seq") + lax.axis_index("seq")) * peers + lax.axis_index("expert")
    channels = own // 2
    conv_sum = lax.dynamic_slice_in_dim(conv_sum, place * channels, channels, axis=1)

    small_sum = small_sum.T
    return (
        from_rows(output, seqs),
        from_rows(grad_tokens, seqs),
        gain_one_sum,
        in_sum.T,
        conv_sum[:CONVK],
        conv_sum[CONVK],
        small_sum[:XW].T,
        small_sum[XW : XW + DTR],
        small_sum[at + CONVK + 1],
        small_sum[at + CONVK + 2 : at + CONVK + 2 + NSTATE],
        small_sum[used - 1],
        out_sum.astype(f32),
        gain_two_sum,
        router_sum,
        jnp.stack([r.finish().T for r in reduces[0::2]]),
        jnp.stack([r.finish() for r in reduces[1::2]]),
    )


def solution(mesh):
    batch = ("dp", "expert")
    split = ("dp", "seq")
    return jax.shard_map(
        local,
        mesh=mesh,
        in_specs=(
            P(batch, "seq", None),
            P(batch, "seq"),
            P(batch, "seq", None),
            P(batch, "seq"),
            P(batch, "seq", None),
            P(),
            P(None, ALL),
            P(None, ALL),
            P(ALL),
            P(ALL, None),
            P(None, ALL),
            P(ALL),
            P(None, ALL),
            P(ALL),
            P(ALL, None),
            P(),
            P(),
            P("expert", None, split),
            P("expert", split, None),
        ),
        out_specs=(
            P(batch, "seq", None),
            P(batch, "seq", None),
            P(),
            P(None, ALL),
            P(None, ALL),
            P(ALL),
            P(ALL, None),
            P(None, ALL),
            P(ALL),
            P(None, ALL),
            P(ALL),
            P(ALL, None),
            P(),
            P(),
            P("expert", None, split),
            P("expert", split, None),
        ),
        check_vma=False,
    )
```

```python
import functools

import jax
import jax.numpy as jnp
from jax import lax
from jax.experimental import pallas as pl
from jax.experimental.pallas import tpu as pltpu
from jax.sharding import PartitionSpec as P

D = 1152
DI = 2304
NSTATE = 16
DTR = 72
CONVK = 4
EXPERTS = 8
XW = DTR + 2 * NSTATE
HALVES = 2
LANES = 128
LN2 = 0.6931471805599453
SPLITS = 3
SUB = 8
PACK = 256
CHUNK = 16
BIG = 1e30
VMEM = 60 * 1024 * 1024

norm_eps = 1e-05
ALL = ("dp", "seq", "expert")


def shifted(value, axis, steps):
    count = lax.axis_size(axis)
    first, last = (max(0, -steps), min(count, count - steps))
    return lax.ppermute(value, axis, [(source, source + steps) for source in range(first, last)])


def dot(left, right, dims, out=jnp.float32):
    return lax.dot_general(left, right, (dims, ((), ())), preferred_element_type=out)


NN = ((1,), (0,))
NT = ((1,), (1,))
TN = ((0,), (0,))


def to_rows(value):
    seqs, length = value.shape[:2]
    rest = value.shape[2:]
    split = value.reshape((seqs, HALVES, length // HALVES) + rest)
    return jnp.moveaxis(split, 2, 0).reshape((seqs * length,) + rest)


def from_rows(value, seqs):
    rest = value.shape[1:]
    length = value.shape[0] // seqs
    split = value.reshape((length // HALVES, seqs, HALVES) + rest)
    return jnp.moveaxis(split, 0, 2).reshape((seqs, length) + rest)


def to_ext_rows(value, halo):
    seqs, length = value.shape[:2]
    rest = value.shape[2:]
    part = length // HALVES
    ext = jnp.concatenate([halo, value], axis=1)
    split = jnp.stack([ext[:, h * part : h * part + part + CONVK - 1] for h in range(HALVES)], axis=1)
    return jnp.moveaxis(split, 2, 0).reshape(((part + CONVK - 1) * seqs * HALVES,) + rest)


def decay_rates(alog_ref, a_s):
    rates = -(1.0 / LN2) * jnp.exp(alog_ref[...].astype(jnp.float32))
    for n in range(NSTATE):
        a_s[n] = jnp.broadcast_to(rates[n : n + 1, :], (SUB, LANES))


def spread(src_ref, dst, first):
    src = src_ref[...]
    high = src.astype(jnp.bfloat16)
    both = jnp.concatenate([high, (src - high.astype(jnp.float32)).astype(jnp.bfloat16)], axis=1)
    line = lax.broadcasted_iota(jnp.int32, (4 * NSTATE, 2 * LANES), 0)
    shift = jnp.where(lax.broadcasted_iota(jnp.int32, (4 * NSTATE, 2 * LANES), 1) < LANES, 0, NSTATE // 2)

    def body(n, carry):
        wanted = shift + (first + n)
        pick = (line == wanted) | (line == wanted + 2 * NSTATE)
        wide = dot(both, jnp.where(pick, 1.0, 0.0).astype(jnp.bfloat16), NN)
        dst[n] = wide[:, :LANES]
        dst[n + NSTATE // 2] = wide[:, LANES:]
        return carry

    lax.fori_loop(0, NSTATE // 2, body, 0)


def tree_sum(parts):
    while len(parts) > 1:
        parts = [parts[i] + parts[i + 1] if i + 1 < len(parts) else parts[i] for i in range(0, len(parts), 2)]
    return parts[0]


UNROLL = 8


def unrolled(first, count, body, carry):
    def group(i, inner):
        for u in range(UNROLL):
            inner = body(first + i * UNROLL + u, inner)
        return inner

    return lax.fori_loop(0, count // UNROLL, group, carry)


def row_at(t):
    return pl.ds(pl.multiple_of(t * SUB, SUB), SUB)


def end_kernel(xs_ref, din_ref, dtw_ref, dtb_ref, alog_ref, bc_ref, cut_ref, delta_ref, end_ref, sum_ref, b_s, a_s, dx_s):
    steps = delta_ref.shape[0] // SUB

    @pl.when(pl.program_id(0) == 0)
    def _():
        spread(bc_ref, b_s, 0)

    decay_rates(alog_ref, a_s)
    pre = dot(din_ref[...], dtw_ref[...], NT) + dtb_ref[...].astype(jnp.float32)
    low = jnp.exp(-jnp.abs(pre))
    delta = jnp.maximum(pre, 0.0) + jnp.where(low < 0.01, low * (1.0 - low * (0.5 - low * (1.0 / 3.0))), jnp.log(1.0 + low))
    delta_ref[...] = delta
    dx_s[...] = delta * xs_ref[...].astype(jnp.float32)
    rates = [a_s[n] for n in range(NSTATE)]

    def body(t, carry):
        total, state = carry
        at = row_at(t)
        step = jnp.maximum(delta_ref[at, :], cut_ref[at, :])
        dx = dx_s[at, :]
        state = [jnp.exp2(step * rates[n]) * state[n] + dx * b_s[n, at, :] for n in range(NSTATE)]
        return (total + step, state)

    zero = jnp.zeros((SUB, LANES), jnp.float32)
    total, state = unrolled(0, steps, body, (zero, [zero] * NSTATE))
    sum_ref[...] = total
    for n in range(NSTATE):
        end_ref[n] = state[n]


def out_kernel(xs_ref, delta_ref, alog_ref, bc_ref, cut_ref, start_ref, z_ref, skip_ref, branch_ref, ssm_ref, held_ref, b_s, c_s, a_s, dx_s, y_s):
    steps = delta_ref.shape[0] // SUB

    @pl.when(pl.program_id(0) == 0)
    def _():
        spread(bc_ref, b_s, 0)
        spread(bc_ref, c_s, NSTATE)

    decay_rates(alog_ref, a_s)
    xs = xs_ref[...].astype(jnp.float32)
    dx_s[...] = delta_ref[...] * xs
    rates = [a_s[n] for n in range(NSTATE)]

    def body(t, state):
        at = row_at(t)
        step = jnp.maximum(delta_ref[at, :], cut_ref[at, :])
        dx = dx_s[at, :]
        state = [jnp.exp2(step * rates[n]) * state[n] + dx * b_s[n, at, :] for n in range(NSTATE)]
        y_s[at, :] = tree_sum([state[n] * c_s[n, at, :] for n in range(NSTATE)])
        return state

    def chunk(i, state):
        for n in range(NSTATE):
            held_ref[i, n] = state[n]
        return unrolled(i * CHUNK, CHUNK, body, state)

    lax.fori_loop(0, steps // CHUNK, chunk, [start_ref[n] for n in range(NSTATE)])
    ssm = y_s[...] + skip_ref[...].astype(jnp.float32) * xs
    z = z_ref[...]
    ssm_ref[...] = ssm.astype(jnp.bfloat16)
    branch_ref[...] = (ssm * (z / (1.0 + jnp.exp(-z)))).astype(jnp.bfloat16)


def first_kernel(delta_ref, alog_ref, bc_ref, cut_ref, gb_ref, z_ref, ssm_ref, lead_ref, gz_ref, g_s, c_s, a_s):
    steps = delta_ref.shape[0] // SUB

    @pl.when(pl.program_id(0) == 0)
    def _():
        spread(bc_ref, c_s, NSTATE)

    decay_rates(alog_ref, a_s)
    z = z_ref[...]
    grad = gb_ref[...]
    sig = 1.0 / (1.0 + jnp.exp(-z))
    g_s[...] = grad * (z * sig)
    gz_ref[...] = (grad * ssm_ref[...].astype(jnp.float32) * (sig * (1.0 + z * (1.0 - sig)))).astype(jnp.bfloat16)
    rates = [a_s[n] for n in range(NSTATE)]

    def body(k, lead):
        at = row_at(steps - 1 - k)
        step = jnp.maximum(delta_ref[at, :], cut_ref[at, :])
        g = g_s[at, :]
        return [jnp.exp2(step * rates[n]) * (lead[n] + g * c_s[n, at, :]) for n in range(NSTATE)]

    zero = jnp.zeros((SUB, LANES), jnp.float32)
    lead = unrolled(0, steps, body, [zero] * NSTATE)
    for n in range(NSTATE):
        lead_ref[n] = lead[n]


def back_kernel(
    xs_ref, delta_ref, alog_ref, bc_ref, cut_ref, g_ref, skip_ref, held_ref, last_ref,
    gxs_ref, gpre_ref, galog_ref, gvec_ref, gbc_ref,
    b_s, c_s, gb_s, gc_s, a_s, dx_s, x_s, gx_s, gd_s, hd_s, dec_s,
):
    steps = delta_ref.shape[0] // SUB

    @pl.when(pl.program_id(0) == 0)
    def _():
        spread(bc_ref, b_s, 0)
        spread(bc_ref, c_s, NSTATE)
        gb_s[...] = jnp.zeros_like(gb_s)
        gc_s[...] = jnp.zeros_like(gc_s)

    decay_rates(alog_ref, a_s)
    xs = xs_ref[...].astype(jnp.float32)
    x_s[...] = xs
    dx_s[...] = delta_ref[...] * xs

    rates = [a_s[n] for n in range(NSTATE)]

    def ahead(j, state, base):
        at = row_at(base + j)
        step = jnp.maximum(delta_ref[at, :], cut_ref[at, :])
        dx = dx_s[at, :]
        g = g_ref[at, :]
        new = []
        for n in range(NSTATE):
            dec = jnp.exp2(step * rates[n])
            hd = dec * state[n]
            dec_s[j, n] = dec
            hd_s[j, n] = hd
            h = hd + dx * b_s[n, at, :]
            gc_s[n, at, :] = gc_s[n, at, :] + g * h
            new.append(h)
        return new

    def behind(k, carry, base):
        coming, rate_grad = carry
        j = CHUNK - 1 - k
        at = row_at(base + j)
        delta = delta_ref[at, :]
        dx = dx_s[at, :]
        g = g_ref[at, :]
        next_coming, next_rate, with_b, with_a = [], [], [], []
        for n in range(NSTATE):
            lam = coming[n] + g * c_s[n, at, :]
            with_b.append(lam * b_s[n, at, :])
            gb_s[n, at, :] = gb_s[n, at, :] + lam * dx
            q = lam * hd_s[j, n]
            with_a.append(q * a_s[n])
            next_rate.append(rate_grad[n] + delta * q)
            next_coming.append(lam * dec_s[j, n])
        by_b = tree_sum(with_b)
        gx_s[at, :] = by_b * delta
        gd_s[at, :] = by_b * x_s[at, :] + LN2 * tree_sum(with_a)
        return (next_coming, next_rate)

    chunks = steps // CHUNK

    def chunk(i, carry):
        c = chunks - 1 - i
        base = c * CHUNK
        unrolled(0, CHUNK, functools.partial(ahead, base=base), [held_ref[c, n] for n in range(NSTATE)])
        return unrolled(0, CHUNK, functools.partial(behind, base=base), carry)

    zero = jnp.zeros((SUB, LANES), jnp.float32)
    _, rate_grad = lax.fori_loop(0, chunks, chunk, ([last_ref[n] for n in range(NSTATE)], [zero] * NSTATE))
    for n in range(NSTATE):
        galog_ref[n : n + 1, :] = LN2 * jnp.sum(rate_grad[n] * a_s[n], axis=0, keepdims=True)
    skip = skip_ref[...].astype(jnp.float32)
    grad_ssm = g_ref[...]
    gxs_ref[...] = gx_s[...] + grad_ssm * skip
    delta = delta_ref[...]
    slope = jnp.where(delta < 0.01, delta * (1.0 - 0.5 * delta * (1.0 - delta * (1.0 / 3.0))), 1.0 - jnp.exp(-delta))
    gpre = gd_s[...] * slope
    gpre_ref[...] = gpre.astype(jnp.bfloat16)
    gvec_ref[0:1, :] = jnp.sum(gpre, axis=0, keepdims=True)
    gvec_ref[1:2, :] = jnp.sum(grad_ssm * xs, axis=0, keepdims=True)
    gvec_ref[2:SUB, :] = jnp.zeros((SUB - 2, LANES), jnp.float32)

    @pl.when(pl.program_id(0) == pl.num_programs(0) - 1)
    def _():
        lane = lax.broadcasted_iota(jnp.int32, (2 * LANES, LANES), 1)
        line = lax.broadcasted_iota(jnp.int32, (2 * LANES, LANES), 0)
        gbc_ref[...] = jnp.zeros_like(gbc_ref)

        def gather(n, carry):
            pick = jnp.where(lane == jnp.where(line < LANES, n, NSTATE + n), 1.0, 0.0).astype(jnp.bfloat16)
            both = jnp.concatenate([gb_s[n].astype(jnp.bfloat16), gc_s[n].astype(jnp.bfloat16)], axis=1)
            gbc_ref[...] += dot(both, pick, NN)
            return carry

        lax.fori_loop(0, NSTATE, gather, 0)


def col_spec(rows):
    return pl.BlockSpec((rows, LANES), lambda c: (0, c))


def full_spec(shape):
    return pl.BlockSpec(shape, lambda c: (0,) * len(shape))


def state_spec():
    return pl.BlockSpec((NSTATE, SUB, LANES), lambda c: (0, 0, c))


def params():
    return pltpu.CompilerParams(vmem_limit_bytes=VMEM)


def f32s(*shape):
    return jax.ShapeDtypeStruct(shape, jnp.float32)


def b16s(*shape):
    return jax.ShapeDtypeStruct(shape, jnp.bfloat16)


def vm(*shape):
    return pltpu.VMEM(shape, jnp.float32)


def cost(rows, width, per_value):
    work = rows * width * NSTATE
    return pl.CostEstimate(flops=work * 8, bytes_accessed=work * per_value, transcendentals=work)


def run_end(xs, din, dtw, dtb, alog, bc, cut):
    rows = xs.shape[0]
    return pl.pallas_call(
        end_kernel,
        grid=(DI // LANES,),
        in_specs=[
            col_spec(rows), full_spec(din.shape), pl.BlockSpec((LANES, DTR), lambda c: (c, 0)),
            col_spec(1), col_spec(NSTATE), full_spec(bc.shape), full_spec(cut.shape),
        ],
        out_specs=[col_spec(rows), state_spec(), col_spec(SUB)],
        out_shape=[f32s(rows, DI), f32s(NSTATE, SUB, DI), f32s(SUB, DI)],
        scratch_shapes=[vm(NSTATE, rows, LANES), vm(NSTATE, SUB, LANES), vm(rows, LANES)],
        compiler_params=params(),
        cost_estimate=cost(rows, DI, 4),
        name="end",
    )(xs, din, dtw, dtb, alog, bc, cut)


def run_out(xs, delta, alog, bc, cut, start, z, skip):
    rows = xs.shape[0]
    chunks = rows // SUB // CHUNK
    return pl.pallas_call(
        out_kernel,
        grid=(DI // LANES,),
        in_specs=[
            col_spec(rows), col_spec(rows), col_spec(NSTATE), full_spec(bc.shape), full_spec(cut.shape),
            state_spec(), col_spec(rows), col_spec(1),
        ],
        out_specs=[
            col_spec(rows), col_spec(rows),
            pl.BlockSpec((chunks, NSTATE, SUB, LANES), lambda c: (0, 0, 0, c)),
        ],
        out_shape=[b16s(rows, DI), b16s(rows, DI), f32s(chunks, NSTATE, SUB, DI)],
        scratch_shapes=[
            vm(NSTATE, rows, LANES), vm(NSTATE, rows, LANES), vm(NSTATE, SUB, LANES), vm(rows, LANES), vm(rows, LANES),
        ],
        compiler_params=params(),
        cost_estimate=cost(rows, DI, 5),
        name="out",
    )(xs, delta, alog, bc, cut, start, z, skip)


def run_first(delta, alog, bc, cut, gbranch, z, ssm):
    rows = delta.shape[0]
    return pl.pallas_call(
        first_kernel,
        grid=(DI // LANES,),
        in_specs=[
            col_spec(rows), col_spec(NSTATE), full_spec(bc.shape), full_spec(cut.shape), col_spec(rows), col_spec(rows),
            col_spec(rows),
        ],
        out_specs=[state_spec(), col_spec(rows), col_spec(rows)],
        out_shape=[f32s(NSTATE, SUB, DI), b16s(rows, DI), f32s(rows, DI)],
        scratch_shapes=[vm(NSTATE, rows, LANES), vm(NSTATE, SUB, LANES)],
        compiler_params=params(),
        cost_estimate=cost(rows, DI, 4),
        name="first",
    )(delta, alog, bc, cut, gbranch, z, ssm)


def run_back(xs, delta, alog, bc, cut, grad_ssm, skip, held, last, part):
    rows = xs.shape[0]
    chunks = rows // SUB // CHUNK
    big = (NSTATE, rows, LANES)
    row = (rows, LANES)
    width = DI // SPLITS
    first = part * (width // LANES)

    def col(count):
        return pl.BlockSpec((count, LANES), lambda c: (0, c + first))

    return pl.pallas_call(
        back_kernel,
        grid=(width // LANES,),
        in_specs=[
            col(rows), col(rows), col(NSTATE), full_spec(bc.shape), full_spec(cut.shape), col(rows), col(1),
            pl.BlockSpec((chunks, NSTATE, SUB, LANES), lambda c: (0, 0, 0, c + first)),
            pl.BlockSpec((NSTATE, SUB, LANES), lambda c: (0, 0, c + first)),
        ],
        out_specs=[col_spec(rows), col_spec(rows), col_spec(NSTATE), col_spec(SUB), full_spec(row)],
        out_shape=[f32s(rows, width), b16s(rows, width), f32s(NSTATE, width), f32s(SUB, width), f32s(*row)],
        scratch_shapes=[
            vm(*big), vm(*big), vm(*big), vm(*big), vm(NSTATE, SUB, LANES),
            vm(*row), vm(*row), vm(*row), vm(*row),
            vm(CHUNK, NSTATE, SUB, LANES), vm(CHUNK, NSTATE, SUB, LANES),
        ],
        compiler_params=params(),
        cost_estimate=cost(rows, width, 17),
        name="back",
    )(xs, delta, alog, bc, cut, grad_ssm, skip, held, last)


def conv_kernel(gxs_ref, gproj_ref, xproj_ref, ext_ref, taps_ref, bias_ref, same_ref, gext_ref, gvec_ref, acc_s):
    rows = gxs_ref.shape[0]
    halo = CONVK - 1
    taps = taps_ref[...]
    bias = bias_ref[...]
    pieces = []
    conv = bias
    for k in range(CONVK):
        piece = ext_ref[k * SUB : k * SUB + rows, :]
        if k < halo:
            piece = piece * same_ref[k]
        pieces.append(piece)
        conv = conv + taps[k : k + 1, :] * piece
    sig = 1.0 / (1.0 + jnp.exp(-conv))
    grad = gxs_ref[...] + dot(gproj_ref[...], xproj_ref[...], NT)
    grad = grad * (sig * (1.0 + conv * (1.0 - sig)))
    acc_s[...] = jnp.zeros_like(acc_s)
    for k in range(CONVK):
        gvec_ref[k : k + 1, :] = jnp.sum(grad * pieces[k], axis=0, keepdims=True)
        part = taps[k : k + 1, :] * grad
        if k < halo:
            part = part * same_ref[k]
        acc_s[k * SUB : k * SUB + rows, :] += part
    gvec_ref[CONVK : CONVK + 1, :] = jnp.sum(grad, axis=0, keepdims=True)
    gvec_ref[CONVK + 1 : SUB, :] = jnp.zeros((SUB - CONVK - 1, LANES), jnp.float32)
    gext_ref[...] = acc_s[...].astype(jnp.bfloat16)


def run_conv(gxs, gproj, xproj, ext, taps, bias, same, part):
    rows, width = gxs.shape
    long = ext.shape[0]
    first = part * (width // LANES)

    def col(count):
        return pl.BlockSpec((count, LANES), lambda c: (0, c + first))

    return pl.pallas_call(
        conv_kernel,
        grid=(width // LANES,),
        in_specs=[
            col_spec(rows), full_spec(gproj.shape), pl.BlockSpec((LANES, XW), lambda c: (c + first, 0)), col(long),
            col(CONVK), col(1), full_spec(same.shape),
        ],
        out_specs=[col_spec(long), col_spec(SUB)],
        out_shape=[b16s(long, width), f32s(SUB, width)],
        scratch_shapes=[vm(long, LANES)],
        compiler_params=params(),
        cost_estimate=pl.CostEstimate(flops=rows * width * 260, bytes_accessed=rows * width * 10, transcendentals=rows * width),
        name="conv",
    )(gxs, gproj, xproj, ext, taps, bias, same)


def gelu_pair(v):
    inner = 0.7978845608 * (v + 0.044715 * v * v * v)
    t = jnp.tanh(inner)
    value = 0.5 * v * (1.0 + t)
    slope = 0.5 * (1.0 + t) + 0.5 * v * (1.0 - t * t) * (0.7978845608 * (1.0 + 3.0 * 0.044715 * v * v))
    return value, slope


QUARTERS = 4


def expert_kernel(blocks, peers, *refs):
    weights, refs = refs[:blocks], refs[blocks:]
    xs, gs, refs = refs[:peers], refs[peers : 2 * peers], refs[2 * peers :]
    out_ref, x_ref, g_ref, hid_ref, pre_ref, up_s, down_s, acc_y, acc_g = refs
    cap = xs[0].shape[1]
    size = weights[0].shape[1]
    step = pl.program_id(0)

    @pl.when(step == 0)
    def _():
        for d in range(peers):
            at = slice(d * cap, (d + 1) * cap)
            piece = xs[d][0]
            x_ref[at, :] = piece[:, :D]
            gate = jnp.sum(piece[:, D:].astype(jnp.float32), axis=1, keepdims=True)
            g_ref[at, :] = (gate * gs[d][0].astype(jnp.float32)).astype(jnp.bfloat16)
        acc_y[...] = jnp.zeros_like(acc_y)
        acc_g[...] = jnp.zeros_like(acc_g)

    each = blocks // QUARTERS
    for h in range(QUARTERS):

        @pl.when(step == h)
        def _():
            for k in range(each):
                at = slice(k * size, (k + 1) * size)
                up_s[at, :] = weights[h * each + k][0]
                down_s[at, :] = weights[h * each + k][1]

    tile = cap * peers // 3

    def body(r, carry):
        at = pl.ds(pl.multiple_of(r * tile, tile), tile)
        value, slope = gelu_pair(dot(x_ref[at, :], up_s[...], NT))
        hidden = value.astype(jnp.bfloat16)
        grad_pre = (slope * dot(g_ref[at, :], down_s[...], NT)).astype(jnp.bfloat16)
        hid_ref[at, :] = hidden
        pre_ref[at, :] = grad_pre
        acc_y[at, :] += dot(hidden, down_s[...], NN)
        acc_g[at, :] += dot(grad_pre, up_s[...], NN)
        return carry

    lax.fori_loop(0, 3, body, 0)

    @pl.when(step == QUARTERS - 1)
    def _():
        out_ref[:, :D] = acc_y[...].astype(jnp.bfloat16)
        out_ref[:, D:] = acc_g[...].astype(jnp.bfloat16)


def run_expert(weights, xs, gs, e):
    blocks, peers = len(weights), len(xs)
    cap = xs[0].shape[1]
    size = weights[0].shape[1]
    rows, cols = peers * cap, blocks * size
    part = cols // QUARTERS
    once = dict(pipeline_mode=pl.Buffered(1))

    def pick(shape):
        return pl.BlockSpec((1,) + shape, lambda h: (e, 0, 0), **once)

    in_specs = [pl.BlockSpec((2, size, D), lambda h: (e, 0, 0), **once)] * blocks
    in_specs += [pick(xs[0].shape[1:])] * peers + [pick(gs[0].shape[1:])] * peers
    column = pl.BlockSpec((rows, part), lambda h: (0, h))
    return pl.pallas_call(
        functools.partial(expert_kernel, blocks, peers),
        grid=(QUARTERS,),
        in_specs=in_specs,
        out_specs=[full_spec((rows, 2 * D)), full_spec((rows, D)), full_spec((rows, D)), column, column],
        out_shape=[b16s(rows, 2 * D), b16s(rows, D), b16s(rows, D), b16s(rows, cols), b16s(rows, cols)],
        scratch_shapes=[
            pltpu.VMEM((part, D), jnp.bfloat16), pltpu.VMEM((part, D), jnp.bfloat16), vm(rows, D), vm(rows, D),
        ],
        compiler_params=params(),
        cost_estimate=pl.CostEstimate(flops=1000, bytes_accessed=1000, transcendentals=0),
        name="expert",
    )(*weights, *xs, *gs)


def weight_kernel(hid_ref, pre_ref, x_ref, g_ref, up_ref, down_ref):
    up_ref[...] = dot(pre_ref[...], x_ref[...], TN).astype(jnp.bfloat16)
    down_ref[...] = dot(hid_ref[...], g_ref[...], TN).astype(jnp.bfloat16)


def run_weight(hid, pre, x, g):
    rows, cols = hid.shape
    part = cols // 12
    column = pl.BlockSpec((rows, part), lambda c: (0, c))
    out = pl.BlockSpec((part, D), lambda c: (c, 0))
    return pl.pallas_call(
        weight_kernel,
        grid=(12,),
        in_specs=[column, column, full_spec((rows, D)), full_spec((rows, D))],
        out_specs=[out, out],
        out_shape=[b16s(cols, D), b16s(cols, D)],
        compiler_params=params(),
        cost_estimate=pl.CostEstimate(flops=1000, bytes_accessed=1000, transcendentals=0),
        name="weight",
    )(hid, pre, x, g)


def halves_of(value, seqs):
    split = value.reshape(value.shape[:-2] + (seqs, HALVES, value.shape[-1]))
    return split[..., 0, :], split[..., 1, :]


def join_halves(first, second):
    both = jnp.stack([first, second], axis=-2)
    return both.reshape(both.shape[:-3] + (both.shape[-3] * HALVES, both.shape[-1]))


def chained(own, decay, steps, beside):
    start = jnp.zeros_like(own)
    carry = own
    for k in range(lax.axis_size("seq") - 1):
        start = shifted(carry.astype(jnp.bfloat16), "seq", steps)
        if k < len(beside):
            start, beside[k] = held_for(start, beside[k])
        start = start.astype(jnp.float32)
        carry = own + decay * start
    return start


def start_states(ends, sums, rates, seqs, beside):
    end_0, end_1 = halves_of(ends, seqs)
    sum_0, sum_1 = halves_of(sums, seqs)
    decay_0 = jnp.exp(rates * sum_0)
    decay_1 = jnp.exp(rates * sum_1)
    start = chained(decay_1 * end_0 + end_1, decay_0 * decay_1, 1, beside)
    return join_halves(start, decay_0 * start + end_0), (decay_0, decay_1)


def last_grads(leads, decays, seqs, beside):
    decay_0, decay_1 = decays
    lead_0, lead_1 = halves_of(leads, seqs)
    last = chained(lead_0 + decay_0 * lead_1, decay_0 * decay_1, -1, beside)
    return join_halves(lead_1 + decay_1 * last, last)


def ring(value, axis, step):
    count = lax.axis_size(axis)
    return lax.ppermute(value, axis, [(i, (i + step) % count) for i in range(count)])


def partner(value, axis, bits):
    count = lax.axis_size(axis)
    return lax.ppermute(value, axis, [(i, i ^ bits) for i in range(count)])


def held_for(first, *others):
    flat, tree = jax.tree.flatten((first,) + others)
    return jax.tree.unflatten(tree, lax.optimization_barrier(flat))


class Gather:
    def __init__(self, own):
        self.here, self.there = [own], []
        self.peers = lax.axis_size("seq")

    def step(self):
        at = len(self.there)
        block = self.here[at]
        if at < self.peers - 1:
            self.there.append(ring(block, "dp", 1))
            self.here.append(ring(block, "seq", 1))
        else:
            half = block.shape[0] // 2
            self.there.append([ring(block[:half], "dp", 1), ring(self.there[-1][half:], "seq", 1)])

    def hold(self, value):
        value, here, there = held_for(value, self.here[1:], self.there)
        self.here[1:], self.there = here, there
        return value

    def done(self):
        return len(self.there) == self.peers


class Reduce:
    def __init__(self, here, there, x_first):
        self.peers = lax.axis_size("seq")
        here = here.reshape(self.peers, -1, D)
        there = there.reshape(self.peers, -1, D)
        self.x_first, self.k, self.total = x_first, self.peers, None
        self.blocks = [(here[k], there[k]) for k in range(self.peers)]
        if x_first:
            self.moving = ring(there, "dp", 1)
        else:
            self.advance()

    def term(self, k):
        if self.x_first:
            return self.blocks[k][0].astype(jnp.float32) + self.other[k].astype(jnp.float32)
        return jnp.stack(self.blocks[k]).astype(jnp.float32)

    def advance(self):
        self.k -= 1
        self.total = self.term(self.k) if self.total is None else self.term(self.k) + self.moving.astype(jnp.float32)
        if self.k > 0:
            self.moving = ring(self.total.astype(jnp.bfloat16), "seq", -1)
        elif self.x_first:
            self.moving = None
        else:
            self.moving = ring(self.total[1].astype(jnp.bfloat16), "dp", 1)

    def step(self):
        if self.moving is None:
            return
        if self.x_first and self.total is None:
            self.other = self.moving
            self.advance()
        elif self.k > 0:
            self.advance()
        else:
            self.total = self.total[0] + self.moving.astype(jnp.float32)
            self.moving = None

    def finish(self):
        while self.moving is not None:
            self.step()
        return self.total


def settle(value, reduces):
    live = [r for r in reduces if r.moving is not None]
    value, moved = held_for(value, [r.moving for r in live])
    for r, m in zip(live, moved):
        r.moving = m
    return value


def hold_all(value, reduces):
    live = [r for r in reduces if r.moving is not None]
    value, moved = held_for(value, [r.moving for r in live])
    for r, m in zip(live, moved):
        r.moving = m
        r.step()
    return value


class Halving:
    def __init__(self, value, axes, near_first):
        self.dims = [(axis, 1 << k) for axis in axes for k in reversed(range(lax.axis_size(axis).bit_length() - 1))]
        self.plan = [d for d in self.dims if near_first and d == ("expert", 1)]
        self.plan += [d for d in self.dims if d[0] == "expert" and d not in self.plan]
        self.plan += [d for d in self.dims if d not in self.plan]
        self.value = value.reshape((2,) * len(self.plan) + value.shape[1:])
        self.start()

    def start(self):
        axis, bit = self.plan.pop(0)
        dim = self.dims.index((axis, bit))
        self.dims.pop(dim)
        low, high = (lax.index_in_dim(self.value, k, dim, False) for k in range(2))
        upper = (lax.axis_index(axis) // bit) % 2 == 1
        self.keep = jnp.where(upper, high, low)
        self.moving = partner(jnp.where(upper, low, high).astype(jnp.bfloat16), axis, bit)

    def step(self):
        self.value = self.keep.astype(jnp.float32) + self.moving.astype(jnp.float32)
        self.moving = None
        if self.plan:
            self.start()

    def finish(self):
        while self.moving is not None:
            self.step()
        return self.value


def sum_everywhere(value):
    for axis in ALL:
        bits = 1
        while bits < lax.axis_size(axis):
            value = value + partner(value, axis, bits)
            bits *= 2
    return value


def exchange(blocks):
    return [blocks[0]] + [partner(blocks[d], "expert", d) for d in range(1, len(blocks))]


def local(
    tokens, segment_ids, routes, keep_mask, out_grad, norm_one, in_proj, conv_weight, conv_bias, x_proj,
    dt_proj, dt_bias, a_log, d_skip, out_proj, norm_two, router, expert_up, expert_down,
):
    seqs, length = tokens.shape[:2]
    rows = seqs * length
    steps = length // HALVES
    halo = CONVK - 1
    capacity = seqs * max(2, length * 3 // 16)
    f32, b16 = jnp.float32, jnp.bfloat16
    own = in_proj.shape[1]

    small = jnp.concatenate(
        [x_proj, dt_proj.T, conv_weight.T, conv_bias[:, None], dt_bias[:, None], a_log.T, d_skip[:, None]], axis=1
    )
    used = small.shape[1]
    small = jnp.pad(small, ((0, 0), (0, PACK - used)))
    entry = lax.all_gather(jnp.concatenate([in_proj.T, small.reshape(-1, D)], axis=0), ALL, axis=0, tiled=False)
    middle = entry.shape[0] // 2
    conv_full = entry[:middle, :own].reshape(DI, D)
    gate_full = entry[middle:, :own].reshape(DI, D)
    small = entry[:, own:].reshape(DI, PACK)
    out_full = lax.all_gather(out_proj, ALL, axis=0, tiled=True)
    local_experts = expert_up.shape[0]
    shard = jnp.stack([m for e in range(local_experts) for m in (expert_up[e].T, expert_down[e])])
    gather = Gather(shard)
    gather.step()
    conv_full = gather.hold(conv_full)
    gather.step()

    xproj_full = small[:, :XW]
    dtw = small[:, XW : XW + DTR]
    at = XW + DTR
    rest = small[:, at:used].T
    conv_w = rest[:CONVK].astype(f32)
    cbias = rest[CONVK : CONVK + 1].astype(f32)
    dtb = rest[CONVK + 1 : CONVK + 2]
    alog = rest[CONVK + 2 : CONVK + 2 + NSTATE]
    skip = rest[CONVK + 2 + NSTATE :]

    halo_tokens = shifted(tokens[:, length - halo :], "seq", 1)
    halo_segs = shifted(segment_ids[:, length - halo :].astype(f32), "seq", 1)
    inputs = to_ext_rows(tokens, halo_tokens).astype(f32)
    seg_ext = to_ext_rows(segment_ids.astype(f32), halo_segs)
    drop = to_rows(keep_mask).astype(f32)
    route = to_rows(routes[..., 0])
    grad_low = to_rows(out_grad)
    grad_final = grad_low.astype(f32)
    skip_rows = halo * SUB
    seg = seg_ext[skip_rows:]
    same = [(seg_ext[k * SUB : k * SUB + rows] == seg).astype(f32)[:, None] for k in range(halo)]
    same_wide = jnp.broadcast_to(jnp.stack(same), (halo, rows, LANES))
    cut = jnp.broadcast_to((1.0 - same[halo - 1]) * BIG, (rows, LANES))

    onehot = (route[:, None] == jnp.arange(EXPERTS, dtype=jnp.int32)).astype(f32)
    order = jnp.arange(rows)
    below = (order[None, :] < order[:, None]).astype(b16)
    rank = jnp.sum(dot(below, onehot.astype(b16), NN) * onehot, axis=-1).astype(jnp.int32)
    peers = lax.axis_size("expert")
    target = (route // local_experts) ^ lax.axis_index("expert")
    slot = (target * local_experts + route % local_experts) * capacity + rank
    placing = (jnp.arange(EXPERTS * capacity, dtype=jnp.int32)[:, None] == slot[None, :]).astype(b16)

    def dispatch(values):
        sent = dot(placing, values, NN, b16).reshape(peers, local_experts, capacity, values.shape[1])
        return exchange([sent[d] for d in range(peers)])

    gain_one = norm_one.astype(f32)
    inv_one = lax.rsqrt(jnp.mean(inputs * inputs, axis=-1, keepdims=True) + norm_eps)
    normed_one = (inputs * inv_one * gain_one).astype(b16)
    ext = dot(normed_one, conv_full, NT)
    gate_z = dot(normed_one[skip_rows:], gate_full, NT)
    conv_out = cbias + conv_w[halo] * ext[skip_rows:]
    for k in range(halo):
        conv_out = conv_out + conv_w[k] * (same[k] * ext[k * SUB : k * SUB + rows])
    xs = jax.nn.silu(conv_out).astype(b16)
    proj = dot(xs, xproj_full, NN)
    delta_in = proj[:, :DTR].astype(b16)
    bc = proj[:, DTR:]
    grad_arrived = dispatch(grad_low)
    delta, ends, sums = run_end(xs, delta_in, dtw, dtb, alog, bc, cut)
    ends, grad_arrived = held_for(gather.hold(ends), grad_arrived)
    rates = -jnp.exp(alog.astype(f32))[:, None, :]
    beside = [gate_z]
    starts, decays = start_states(ends, sums, rates, seqs, beside)
    gate_z = beside[0]
    starts = gather.hold(starts)
    gather.step()
    branch, ssm, held = run_out(xs, delta, alog, bc, cut, starts, gate_z, skip)
    tokens_rows = inputs[skip_rows:]
    first_sum = tokens_rows + dot(branch, out_full, NN)

    gain_two = norm_two.astype(f32)
    inv_two = lax.rsqrt(jnp.mean(first_sum * first_sum, axis=-1, keepdims=True) + norm_eps)
    normed_two = (first_sum * inv_two * gain_two).astype(b16)
    probs = jax.nn.softmax(dot(normed_two, router, NN), axis=-1)
    gate_raw = jnp.sum(probs * onehot, axis=-1)
    gate = gate_raw * drop
    gate_high = lax.reduce_precision(gate, 8, 7)
    gate_mid = lax.reduce_precision(gate - gate_high, 8, 7)
    gate_low = gate - gate_high - gate_mid
    gates = jnp.stack([gate_high, gate_mid, gate_low], axis=1).astype(b16)
    message = jnp.concatenate([normed_two, jnp.pad(gates, ((0, 0), (0, LANES - 3)))], axis=1)
    message = gather.hold(message)
    gather.step()
    while not gather.done():
        gather.step()
    arrived = gather.hold(dispatch(message))
    blocks = gather.here + gather.there[:-1] + [jnp.concatenate(gather.there[-1], axis=0)]
    returned, for_weights = [], []
    for e in range(local_experts):
        done, *rest = run_expert(blocks, arrived, grad_arrived, e)
        for_weights.append(rest)
        if e > 0:
            done, returned = held_for(done, returned)
        returned.append(exchange([part for part in done.reshape(peers, capacity, 2 * D)]))
    weight_grads = []
    for e in range(local_experts):
        x_rows, g_rows, hid, pre = for_weights[e]
        weight_grads += run_weight(hid, pre, x_rows, g_rows)
    returned[-1], weight_grads = held_for(returned[-1], weight_grads)
    count = len(weight_grads)
    middle = weight_grads[0].shape[0] // 2
    reduces = [Reduce(g[:middle], g[middle:], i < count - 1) for i, g in enumerate(weight_grads)]
    returned = [jnp.stack([returned[e][d] for e in range(local_experts)]) for d in range(peers)]

    back_rows = jnp.stack(returned).reshape(EXPERTS * capacity, 2 * D)
    combined = dot(placing, back_rows, TN)
    expert_rows, grad_back = combined[:, :D], combined[:, D:]
    output = (first_sum + gate[:, None] * expert_rows).astype(b16)

    grad_gate = jnp.sum(grad_final * expert_rows, axis=-1) * drop
    grad_logits = (grad_gate * gate_raw)[:, None] * (onehot - probs)
    logits_low = grad_logits.astype(b16)
    router_grad = dot(normed_two, logits_low, TN)
    grad_two = grad_back + dot(logits_low, router, NT)
    gain_two_grad = jnp.sum(grad_two * (first_sum * inv_two), axis=0)
    scaled = grad_two * gain_two
    grad_first = (
        grad_final + inv_two * scaled
        - first_sum * (inv_two * inv_two * inv_two * jnp.mean(scaled * first_sum, axis=-1, keepdims=True))
    )
    grad_first = hold_all(grad_first, reduces[-1:])
    first_low = grad_first.astype(b16)
    out_grad_part = dot(branch, first_low, TN, b16)
    grad_branch = dot(first_low, out_full, NT)
    grad_branch, out_grad_part = held_for(grad_branch, out_grad_part)
    grad_branch = hold_all(grad_branch, reduces[:1])

    leads, grad_z, grad_ssm = run_first(delta, alog, bc, cut, grad_branch, gate_z, ssm)
    leads = settle(leads, [reduces[0], reduces[1], reduces[-1]])
    gate_part = dot(grad_z, normed_one[skip_rows:], TN, b16)
    grad_normed_z = dot(grad_z, gate_full, NN)
    beside = [gate_part, grad_normed_z, router_grad]
    last = last_grads(leads, decays, seqs, beside)
    gate_part, grad_normed_z, router_grad = beside
    last, out_grad_part, gate_part = held_for(last, out_grad_part, gate_part)
    out_sum = lax.psum_scatter(out_grad_part, ALL, scatter_dimension=0, tiled=True)
    gate_own = lax.psum_scatter(gate_part, ("seq", "expert"), scatter_dimension=0, tiled=True)
    grad_delta_in, gbc, parts = 0.0, 0.0, []
    width = DI // SPLITS
    for part in range(SPLITS):
        if part == 1:
            last, out_sum = held_for(last, out_sum)
        last = hold_all(last, reduces[: 2 + part] + reduces[-1:] if 2 + part < count else reduces)
        gxs, gpre, galog, gvec, gbc_part = run_back(xs, delta, alog, bc, cut, grad_ssm, skip, held, last, part)
        grad_delta_in = grad_delta_in + dot(gpre, dtw[part * width : (part + 1) * width], NN)
        gbc = gbc + gbc_part[:, : 2 * NSTATE]
        dtproj_part = dot(gpre, delta_in, TN)
        last, gxs, dtproj_part, grad_delta_in, gbc, galog, gvec = held_for(
            last, gxs, dtproj_part, grad_delta_in, gbc, galog, gvec
        )
        parts.append((gxs, dtproj_part, galog, gvec))
    grad_proj = jnp.concatenate([grad_delta_in, gbc], axis=1).astype(b16)
    grad_proj, gate_own = held_for(hold_all(grad_proj, reduces), gate_own)
    xproj_grad = dot(xs, grad_proj, TN)
    zeros = jnp.zeros((CONVK + 1, DI), f32)
    vecs = jnp.concatenate([p[3] for p in parts], axis=1)
    small_grad = jnp.concatenate(
        [
            xproj_grad,
            jnp.concatenate([p[1] for p in parts], axis=0),
            zeros.T,
            vecs[0][:, None],
            jnp.concatenate([p[2] for p in parts], axis=1).T,
            vecs[1][:, None],
        ],
        axis=1,
    ).astype(b16)
    small_grad = jnp.pad(small_grad, ((0, 0), (0, PACK - used)))
    small_grad, grad_proj = held_for(small_grad, grad_proj)
    small_half = Halving(small_grad.reshape(-1, own // 2, PACK), ALL, True)
    gexts, conv_parts, conv_grads = [], [], []
    for part in range(SPLITS):
        gext, gvec = run_conv(parts[part][0], grad_proj, xproj_full, ext, conv_w, cbias, same_wide, part)
        if part == SPLITS - 1:
            gext = hold_all(gext, reduces)
        conv_parts.append(dot(gext, normed_one, TN, b16))
        gexts.append(gext)
        conv_grads.append(gvec)
    conv_all, gexts = held_for(jnp.concatenate(conv_parts, axis=0), gexts)
    third = D // 3
    conv_own = []
    for k in range(3):
        piece = conv_all[:, k * third : (k + 1) * third].reshape(-1, own, third)
        conv_own.append(Halving(piece, ("seq", "expert"), True))
    gexts = hold_all(gexts, conv_own + [small_half])
    grad_normed = sum(dot(gexts[k], conv_full[k * width : (k + 1) * width], NN) for k in range(SPLITS))
    grad_normed = hold_all(grad_normed, conv_own + [small_half])
    over = grad_normed[:skip_rows].reshape(halo, seqs, HALVES, D)
    from_next = shifted(over[:, :, 0], "seq", -1)
    edge = jnp.stack([over[:, :, 1], from_next], axis=2).reshape(skip_rows, D)
    grad_normed = grad_normed[skip_rows:] + grad_normed_z
    grad_normed = grad_normed + jnp.pad(edge, ((rows - skip_rows, 0), (0, 0)))
    inv_rows = inv_one[skip_rows:]
    gain_one_grad = jnp.sum(grad_normed * (tokens_rows * inv_rows), axis=0)
    scaled_one = grad_normed * gain_one
    grad_tokens = (
        grad_first + inv_rows * scaled_one
        - tokens_rows * (inv_rows * inv_rows * inv_rows * jnp.mean(scaled_one * tokens_rows, axis=-1, keepdims=True))
    )
    conv_grad = jnp.concatenate(conv_grads, axis=1)[: CONVK + 1]
    flat = jnp.concatenate([gain_one_grad, gain_two_grad, router_grad.reshape(-1), conv_grad.reshape(-1)])
    flat = hold_all(flat, conv_own + [small_half])
    flat = sum_everywhere(flat.reshape(-1, LANES)).reshape(-1)
    small_sum = small_half.finish()
    is_gate = lax.axis_index("dp") == 1
    gate_own = gate_own.astype(f32)
    conv_own = jnp.concatenate([part.finish() for part in conv_own], axis=1)
    in_sum = jnp.where(is_gate, gate_own, conv_own)
    in_sum = in_sum + ring(jnp.where(is_gate, conv_own, gate_own).astype(b16), "dp", 1).astype(f32)
    gain_one_sum, gain_two_sum = flat[:D], flat[D : 2 * D]
    router_sum = flat[2 * D : (2 + EXPERTS) * D].reshape(D, EXPERTS)
    conv_sum = flat[(2 + EXPERTS) * D :].reshape(CONVK + 1, DI)
    place = (lax.axis_index("dp") * lax.axis_size("seq") + lax.axis_index("seq")) * peers + lax.axis_index("expert")
    channels = own // 2
    conv_sum = lax.dynamic_slice_in_dim(conv_sum, place * channels, channels, axis=1)

    small_sum = small_sum.T
    return (
        from_rows(output, seqs),
        from_rows(grad_tokens, seqs),
        gain_one_sum,
        in_sum.T,
        conv_sum[:CONVK],
        conv_sum[CONVK],
        small_sum[:XW].T,
        small_sum[XW : XW + DTR],
        small_sum[at + CONVK + 1],
        small_sum[at + CONVK + 2 : at + CONVK + 2 + NSTATE],
        small_sum[used - 1],
        out_sum.astype(f32),
        gain_two_sum,
        router_sum,
        jnp.stack([r.finish().T for r in reduces[0::2]]),
        jnp.stack([r.finish() for r in reduces[1::2]]),
    )


def solution(mesh):
    batch = ("dp", "expert")
    split = ("dp", "seq")
    return jax.shard_map(
        local,
        mesh=mesh,
        in_specs=(
            P(batch, "seq", None),
            P(batch, "seq"),
            P(batch, "seq", None),
            P(batch, "seq"),
            P(batch, "seq", None),
            P(),
            P(None, ALL),
            P(None, ALL),
            P(ALL),
            P(ALL, None),
            P(None, ALL),
            P(ALL),
            P(None, ALL),
            P(ALL),
            P(ALL, None),
            P(),
            P(),
            P("expert", None, split),
            P("expert", split, None),
        ),
        out_specs=(
            P(batch, "seq", None),
            P(batch, "seq", None),
            P(),
            P(None, ALL),
            P(None, ALL),
            P(ALL),
            P(ALL, None),
            P(None, ALL),
            P(ALL),
            P(None, ALL),
            P(ALL),
            P(ALL, None),
            P(),
            P(),
            P("expert", None, split),
            P("expert", split, None),
        ),
        check_vma=False,
    )
```

```python
import functools

import jax
import jax.numpy as jnp
from jax import lax
from jax.experimental import pallas as pl
from jax.experimental.pallas import tpu as pltpu
from jax.sharding import PartitionSpec as P

D = 1152
DI = 2304
NSTATE = 16
DTR = 72
CONVK = 4
EXPERTS = 8
XW = DTR + 2 * NSTATE
HALVES = 2
LANES = 128
LN2 = 0.6931471805599453
SPLITS = 3
SUB = 8
PACK = 256
CHUNK = 16
BIG = 1e30
VMEM = 60 * 1024 * 1024

norm_eps = 1e-05
ALL = ("dp", "seq", "expert")


def shifted(value, axis, steps):
    count = lax.axis_size(axis)
    first, last = (max(0, -steps), min(count, count - steps))
    return lax.ppermute(value, axis, [(source, source + steps) for source in range(first, last)])


def dot(left, right, dims, out=jnp.float32):
    return lax.dot_general(left, right, (dims, ((), ())), preferred_element_type=out)


NN = ((1,), (0,))
NT = ((1,), (1,))
TN = ((0,), (0,))


def to_rows(value):
    seqs, length = value.shape[:2]
    rest = value.shape[2:]
    split = value.reshape((seqs, HALVES, length // HALVES) + rest)
    return jnp.moveaxis(split, 2, 0).reshape((seqs * length,) + rest)


def from_rows(value, seqs):
    rest = value.shape[1:]
    length = value.shape[0] // seqs
    split = value.reshape((length // HALVES, seqs, HALVES) + rest)
    return jnp.moveaxis(split, 0, 2).reshape((seqs, length) + rest)


def to_ext_rows(value, halo):
    seqs, length = value.shape[:2]
    rest = value.shape[2:]
    part = length // HALVES
    ext = jnp.concatenate([halo, value], axis=1)
    split = jnp.stack([ext[:, h * part : h * part + part + CONVK - 1] for h in range(HALVES)], axis=1)
    return jnp.moveaxis(split, 2, 0).reshape(((part + CONVK - 1) * seqs * HALVES,) + rest)


def decay_rates(alog_ref, a_s):
    rates = -(1.0 / LN2) * jnp.exp(alog_ref[...].astype(jnp.float32))
    for n in range(NSTATE):
        a_s[n] = jnp.broadcast_to(rates[n : n + 1, :], (SUB, LANES))


def spread(src_ref, dst, first):
    src = src_ref[...]
    high = src.astype(jnp.bfloat16)
    both = jnp.concatenate([high, (src - high.astype(jnp.float32)).astype(jnp.bfloat16)], axis=1)
    line = lax.broadcasted_iota(jnp.int32, (4 * NSTATE, 2 * LANES), 0)
    shift = jnp.where(lax.broadcasted_iota(jnp.int32, (4 * NSTATE, 2 * LANES), 1) < LANES, 0, NSTATE // 2)

    def body(n, carry):
        wanted = shift + (first + n)
        pick = (line == wanted) | (line == wanted + 2 * NSTATE)
        wide = dot(both, jnp.where(pick, 1.0, 0.0).astype(jnp.bfloat16), NN)
        dst[n] = wide[:, :LANES]
        dst[n + NSTATE // 2] = wide[:, LANES:]
        return carry

    lax.fori_loop(0, NSTATE // 2, body, 0)


def tree_sum(parts):
    while len(parts) > 1:
        parts = [parts[i] + parts[i + 1] if i + 1 < len(parts) else parts[i] for i in range(0, len(parts), 2)]
    return parts[0]


UNROLL = 8


def unrolled(first, count, body, carry):
    def group(i, inner):
        for u in range(UNROLL):
            inner = body(first + i * UNROLL + u, inner)
        return inner

    return lax.fori_loop(0, count // UNROLL, group, carry)


def row_at(t):
    return pl.ds(pl.multiple_of(t * SUB, SUB), SUB)


def end_kernel(xs_ref, din_ref, dtw_ref, dtb_ref, alog_ref, bc_ref, cut_ref, delta_ref, end_ref, sum_ref, b_s, a_s, dx_s):
    steps = delta_ref.shape[0] // SUB

    @pl.when(pl.program_id(0) == 0)
    def _():
        spread(bc_ref, b_s, 0)

    decay_rates(alog_ref, a_s)
    pre = dot(din_ref[...], dtw_ref[...], NT) + dtb_ref[...].astype(jnp.float32)
    low = jnp.exp(-jnp.abs(pre))
    delta = jnp.maximum(pre, 0.0) + jnp.where(low < 0.01, low * (1.0 - low * (0.5 - low * (1.0 / 3.0))), jnp.log(1.0 + low))
    delta_ref[...] = delta
    dx_s[...] = delta * xs_ref[...].astype(jnp.float32)
    rates = [a_s[n] for n in range(NSTATE)]

    def body(t, carry):
        total, state = carry
        at = row_at(t)
        step = jnp.maximum(delta_ref[at, :], cut_ref[at, :])
        dx = dx_s[at, :]
        state = [jnp.exp2(step * rates[n]) * state[n] + dx * b_s[n, at, :] for n in range(NSTATE)]
        return (total + step, state)

    zero = jnp.zeros((SUB, LANES), jnp.float32)
    total, state = unrolled(0, steps, body, (zero, [zero] * NSTATE))
    sum_ref[...] = total
    for n in range(NSTATE):
        end_ref[n] = state[n]


def out_kernel(xs_ref, delta_ref, alog_ref, bc_ref, cut_ref, start_ref, z_ref, skip_ref, branch_ref, ssm_ref, held_ref, b_s, c_s, a_s, dx_s, y_s):
    steps = delta_ref.shape[0] // SUB

    @pl.when(pl.program_id(0) == 0)
    def _():
        spread(bc_ref, b_s, 0)
        spread(bc_ref, c_s, NSTATE)

    decay_rates(alog_ref, a_s)
    xs = xs_ref[...].astype(jnp.float32)
    dx_s[...] = delta_ref[...] * xs
    rates = [a_s[n] for n in range(NSTATE)]

    def body(t, state):
        at = row_at(t)
        step = jnp.maximum(delta_ref[at, :], cut_ref[at, :])
        dx = dx_s[at, :]
        state = [jnp.exp2(step * rates[n]) * state[n] + dx * b_s[n, at, :] for n in range(NSTATE)]
        y_s[at, :] = tree_sum([state[n] * c_s[n, at, :] for n in range(NSTATE)])
        return state

    def chunk(i, state):
        for n in range(NSTATE):
            held_ref[i, n] = state[n]
        return unrolled(i * CHUNK, CHUNK, body, state)

    lax.fori_loop(0, steps // CHUNK, chunk, [start_ref[n] for n in range(NSTATE)])
    ssm = y_s[...] + skip_ref[...].astype(jnp.float32) * xs
    z = z_ref[...]
    ssm_ref[...] = ssm.astype(jnp.bfloat16)
    branch_ref[...] = (ssm * (z / (1.0 + jnp.exp(-z)))).astype(jnp.bfloat16)


def first_kernel(delta_ref, alog_ref, bc_ref, cut_ref, gb_ref, z_ref, ssm_ref, lead_ref, gz_ref, g_s, c_s, a_s):
    steps = delta_ref.shape[0] // SUB

    @pl.when(pl.program_id(0) == 0)
    def _():
        spread(bc_ref, c_s, NSTATE)

    decay_rates(alog_ref, a_s)
    z = z_ref[...]
    grad = gb_ref[...]
    sig = 1.0 / (1.0 + jnp.exp(-z))
    g_s[...] = grad * (z * sig)
    gz_ref[...] = (grad * ssm_ref[...].astype(jnp.float32) * (sig * (1.0 + z * (1.0 - sig)))).astype(jnp.bfloat16)
    rates = [a_s[n] for n in range(NSTATE)]

    def body(k, lead):
        at = row_at(steps - 1 - k)
        step = jnp.maximum(delta_ref[at, :], cut_ref[at, :])
        g = g_s[at, :]
        return [jnp.exp2(step * rates[n]) * (lead[n] + g * c_s[n, at, :]) for n in range(NSTATE)]

    zero = jnp.zeros((SUB, LANES), jnp.float32)
    lead = unrolled(0, steps, body, [zero] * NSTATE)
    for n in range(NSTATE):
        lead_ref[n] = lead[n]


def back_kernel(
    xs_ref, delta_ref, alog_ref, bc_ref, cut_ref, g_ref, skip_ref, held_ref, last_ref,
    gxs_ref, gpre_ref, galog_ref, gvec_ref, gbc_ref,
    b_s, c_s, gb_s, gc_s, a_s, dx_s, x_s, gx_s, gd_s, hd_s, dec_s,
):
    steps = delta_ref.shape[0] // SUB

    @pl.when(pl.program_id(0) == 0)
    def _():
        spread(bc_ref, b_s, 0)
        spread(bc_ref, c_s, NSTATE)
        gb_s[...] = jnp.zeros_like(gb_s)
        gc_s[...] = jnp.zeros_like(gc_s)

    decay_rates(alog_ref, a_s)
    xs = xs_ref[...].astype(jnp.float32)
    x_s[...] = xs
    dx_s[...] = delta_ref[...] * xs

    rates = [a_s[n] for n in range(NSTATE)]

    def ahead(j, state, base):
        at = row_at(base + j)
        step = jnp.maximum(delta_ref[at, :], cut_ref[at, :])
        dx = dx_s[at, :]
        g = g_ref[at, :]
        new = []
        for n in range(NSTATE):
            dec = jnp.exp2(step * rates[n])
            hd = dec * state[n]
            dec_s[j, n] = dec
            hd_s[j, n] = hd
            h = hd + dx * b_s[n, at, :]
            gc_s[n, at, :] = gc_s[n, at, :] + g * h
            new.append(h)
        return new

    def behind(k, carry, base):
        coming, rate_grad = carry
        j = CHUNK - 1 - k
        at = row_at(base + j)
        delta = delta_ref[at, :]
        dx = dx_s[at, :]
        g = g_ref[at, :]
        next_coming, next_rate, with_b, with_a = [], [], [], []
        for n in range(NSTATE):
            lam = coming[n] + g * c_s[n, at, :]
            with_b.append(lam * b_s[n, at, :])
            gb_s[n, at, :] = gb_s[n, at, :] + lam * dx
            q = lam * hd_s[j, n]
            with_a.append(q * a_s[n])
            next_rate.append(rate_grad[n] + delta * q)
            next_coming.append(lam * dec_s[j, n])
        by_b = tree_sum(with_b)
        gx_s[at, :] = by_b * delta
        gd_s[at, :] = by_b * x_s[at, :] + LN2 * tree_sum(with_a)
        return (next_coming, next_rate)

    chunks = steps // CHUNK

    def chunk(i, carry):
        c = chunks - 1 - i
        base = c * CHUNK
        unrolled(0, CHUNK, functools.partial(ahead, base=base), [held_ref[c, n] for n in range(NSTATE)])
        return unrolled(0, CHUNK, functools.partial(behind, base=base), carry)

    zero = jnp.zeros((SUB, LANES), jnp.float32)
    _, rate_grad = lax.fori_loop(0, chunks, chunk, ([last_ref[n] for n in range(NSTATE)], [zero] * NSTATE))
    for n in range(NSTATE):
        galog_ref[n : n + 1, :] = LN2 * jnp.sum(rate_grad[n] * a_s[n], axis=0, keepdims=True)
    skip = skip_ref[...].astype(jnp.float32)
    grad_ssm = g_ref[...]
    gxs_ref[...] = gx_s[...] + grad_ssm * skip
    delta = delta_ref[...]
    slope = jnp.where(delta < 0.01, delta * (1.0 - 0.5 * delta * (1.0 - delta * (1.0 / 3.0))), 1.0 - jnp.exp(-delta))
    gpre = gd_s[...] * slope
    gpre_ref[...] = gpre.astype(jnp.bfloat16)
    gvec_ref[0:1, :] = jnp.sum(gpre, axis=0, keepdims=True)
    gvec_ref[1:2, :] = jnp.sum(grad_ssm * xs, axis=0, keepdims=True)
    gvec_ref[2:SUB, :] = jnp.zeros((SUB - 2, LANES), jnp.float32)

    @pl.when(pl.program_id(0) == pl.num_programs(0) - 1)
    def _():
        lane = lax.broadcasted_iota(jnp.int32, (2 * LANES, LANES), 1)
        line = lax.broadcasted_iota(jnp.int32, (2 * LANES, LANES), 0)
        gbc_ref[...] = jnp.zeros_like(gbc_ref)

        def gather(n, carry):
            pick = jnp.where(lane == jnp.where(line < LANES, n, NSTATE + n), 1.0, 0.0).astype(jnp.bfloat16)
            both = jnp.concatenate([gb_s[n].astype(jnp.bfloat16), gc_s[n].astype(jnp.bfloat16)], axis=1)
            gbc_ref[...] += dot(both, pick, NN)
            return carry

        lax.fori_loop(0, NSTATE, gather, 0)


def col_spec(rows):
    return pl.BlockSpec((rows, LANES), lambda c: (0, c))


def full_spec(shape):
    return pl.BlockSpec(shape, lambda c: (0,) * len(shape))


def state_spec():
    return pl.BlockSpec((NSTATE, SUB, LANES), lambda c: (0, 0, c))


def params():
    return pltpu.CompilerParams(vmem_limit_bytes=VMEM)


def f32s(*shape):
    return jax.ShapeDtypeStruct(shape, jnp.float32)


def b16s(*shape):
    return jax.ShapeDtypeStruct(shape, jnp.bfloat16)


def vm(*shape):
    return pltpu.VMEM(shape, jnp.float32)


def cost(rows, width, per_value):
    work = rows * width * NSTATE
    return pl.CostEstimate(flops=work * 8, bytes_accessed=work * per_value, transcendentals=work)


def run_end(xs, din, dtw, dtb, alog, bc, cut):
    rows = xs.shape[0]
    return pl.pallas_call(
        end_kernel,
        grid=(DI // LANES,),
        in_specs=[
            col_spec(rows), full_spec(din.shape), pl.BlockSpec((LANES, DTR), lambda c: (c, 0)),
            col_spec(1), col_spec(NSTATE), full_spec(bc.shape), full_spec(cut.shape),
        ],
        out_specs=[col_spec(rows), state_spec(), col_spec(SUB)],
        out_shape=[f32s(rows, DI), f32s(NSTATE, SUB, DI), f32s(SUB, DI)],
        scratch_shapes=[vm(NSTATE, rows, LANES), vm(NSTATE, SUB, LANES), vm(rows, LANES)],
        compiler_params=params(),
        cost_estimate=cost(rows, DI, 4),
        name="end",
    )(xs, din, dtw, dtb, alog, bc, cut)


def run_out(xs, delta, alog, bc, cut, start, z, skip):
    rows = xs.shape[0]
    chunks = rows // SUB // CHUNK
    return pl.pallas_call(
        out_kernel,
        grid=(DI // LANES,),
        in_specs=[
            col_spec(rows), col_spec(rows), col_spec(NSTATE), full_spec(bc.shape), full_spec(cut.shape),
            state_spec(), col_spec(rows), col_spec(1),
        ],
        out_specs=[
            col_spec(rows), col_spec(rows),
            pl.BlockSpec((chunks, NSTATE, SUB, LANES), lambda c: (0, 0, 0, c)),
        ],
        out_shape=[b16s(rows, DI), b16s(rows, DI), f32s(chunks, NSTATE, SUB, DI)],
        scratch_shapes=[
            vm(NSTATE, rows, LANES), vm(NSTATE, rows, LANES), vm(NSTATE, SUB, LANES), vm(rows, LANES), vm(rows, LANES),
        ],
        compiler_params=params(),
        cost_estimate=cost(rows, DI, 5),
        name="out",
    )(xs, delta, alog, bc, cut, start, z, skip)


def run_first(delta, alog, bc, cut, gbranch, z, ssm):
    rows = delta.shape[0]
    return pl.pallas_call(
        first_kernel,
        grid=(DI // LANES,),
        in_specs=[
            col_spec(rows), col_spec(NSTATE), full_spec(bc.shape), full_spec(cut.shape), col_spec(rows), col_spec(rows),
            col_spec(rows),
        ],
        out_specs=[state_spec(), col_spec(rows), col_spec(rows)],
        out_shape=[f32s(NSTATE, SUB, DI), b16s(rows, DI), f32s(rows, DI)],
        scratch_shapes=[vm(NSTATE, rows, LANES), vm(NSTATE, SUB, LANES)],
        compiler_params=params(),
        cost_estimate=pl.CostEstimate(flops=1000, bytes_accessed=1000, transcendentals=0),
        name="first",
    )(delta, alog, bc, cut, gbranch, z, ssm)


def run_back(xs, delta, alog, bc, cut, grad_ssm, skip, held, last, part):
    rows = xs.shape[0]
    chunks = rows // SUB // CHUNK
    big = (NSTATE, rows, LANES)
    row = (rows, LANES)
    width = DI // SPLITS
    first = part * (width // LANES)

    def col(count):
        return pl.BlockSpec((count, LANES), lambda c: (0, c + first))

    return pl.pallas_call(
        back_kernel,
        grid=(width // LANES,),
        in_specs=[
            col(rows), col(rows), col(NSTATE), full_spec(bc.shape), full_spec(cut.shape), col(rows), col(1),
            pl.BlockSpec((chunks, NSTATE, SUB, LANES), lambda c: (0, 0, 0, c + first)),
            pl.BlockSpec((NSTATE, SUB, LANES), lambda c: (0, 0, c + first)),
        ],
        out_specs=[col_spec(rows), col_spec(rows), col_spec(NSTATE), col_spec(SUB), full_spec(row)],
        out_shape=[f32s(rows, width), b16s(rows, width), f32s(NSTATE, width), f32s(SUB, width), f32s(*row)],
        scratch_shapes=[
            vm(*big), vm(*big), vm(*big), vm(*big), vm(NSTATE, SUB, LANES),
            vm(*row), vm(*row), vm(*row), vm(*row),
            vm(CHUNK, NSTATE, SUB, LANES), vm(CHUNK, NSTATE, SUB, LANES),
        ],
        compiler_params=params(),
        cost_estimate=cost(rows, width, 17),
        name="back",
    )(xs, delta, alog, bc, cut, grad_ssm, skip, held, last)


def conv_kernel(gxs_ref, gproj_ref, xproj_ref, ext_ref, taps_ref, bias_ref, same_ref, gext_ref, gvec_ref, acc_s):
    rows = gxs_ref.shape[0]
    halo = CONVK - 1
    taps = taps_ref[...]
    bias = bias_ref[...]
    pieces = []
    conv = bias
    for k in range(CONVK):
        piece = ext_ref[k * SUB : k * SUB + rows, :]
        if k < halo:
            piece = piece * same_ref[k]
        pieces.append(piece)
        conv = conv + taps[k : k + 1, :] * piece
    sig = 1.0 / (1.0 + jnp.exp(-conv))
    grad = gxs_ref[...] + dot(gproj_ref[...], xproj_ref[...], NT)
    grad = grad * (sig * (1.0 + conv * (1.0 - sig)))
    acc_s[...] = jnp.zeros_like(acc_s)
    for k in range(CONVK):
        gvec_ref[k : k + 1, :] = jnp.sum(grad * pieces[k], axis=0, keepdims=True)
        part = taps[k : k + 1, :] * grad
        if k < halo:
            part = part * same_ref[k]
        acc_s[k * SUB : k * SUB + rows, :] += part
    gvec_ref[CONVK : CONVK + 1, :] = jnp.sum(grad, axis=0, keepdims=True)
    gvec_ref[CONVK + 1 : SUB, :] = jnp.zeros((SUB - CONVK - 1, LANES), jnp.float32)
    gext_ref[...] = acc_s[...].astype(jnp.bfloat16)


def run_conv(gxs, gproj, xproj, ext, taps, bias, same, part):
    rows, width = gxs.shape
    long = ext.shape[0]
    first = part * (width // LANES)

    def col(count):
        return pl.BlockSpec((count, LANES), lambda c: (0, c + first))

    return pl.pallas_call(
        conv_kernel,
        grid=(width // LANES,),
        in_specs=[
            col_spec(rows), full_spec(gproj.shape), pl.BlockSpec((LANES, XW), lambda c: (c + first, 0)), col(long),
            col(CONVK), col(1), full_spec(same.shape),
        ],
        out_specs=[col_spec(long), col_spec(SUB)],
        out_shape=[b16s(long, width), f32s(SUB, width)],
        scratch_shapes=[vm(long, LANES)],
        compiler_params=params(),
        cost_estimate=pl.CostEstimate(flops=rows * width * 260, bytes_accessed=rows * width * 10, transcendentals=rows * width),
        name="conv",
    )(gxs, gproj, xproj, ext, taps, bias, same)


def gelu_pair(v):
    inner = 0.7978845608 * (v + 0.044715 * v * v * v)
    t = jnp.tanh(inner)
    value = 0.5 * v * (1.0 + t)
    slope = 0.5 * (1.0 + t) + 0.5 * v * (1.0 - t * t) * (0.7978845608 * (1.0 + 3.0 * 0.044715 * v * v))
    return value, slope


PARTS = 2


def expert_kernel(blocks, peers, final, *refs):
    weights, refs = refs[:blocks], refs[blocks:]
    step = pl.program_id(0)
    if final:
        x_ref, g_ref, before, out_ref, hid_ref, pre_ref, up_s, down_s, acc_y, acc_g = refs

        @pl.when(step == 0)
        def _():
            acc_y[...] = before[:, :D].astype(jnp.float32)
            acc_g[...] = before[:, D:].astype(jnp.float32)

    else:
        xs, gs, refs = refs[:peers], refs[peers : 2 * peers], refs[2 * peers :]
        out_ref, x_ref, g_ref, hid_ref, pre_ref, up_s, down_s, acc_y, acc_g = refs
        cap = xs[0].shape[1]

        @pl.when(step == 0)
        def _():
            for d in range(peers):
                at = slice(d * cap, (d + 1) * cap)
                piece = xs[d][0]
                x_ref[at, :] = piece[:, :D]
                gate = jnp.sum(piece[:, D:].astype(jnp.float32), axis=1, keepdims=True)
                g_ref[at, :] = (gate * gs[d][0].astype(jnp.float32)).astype(jnp.bfloat16)
            acc_y[...] = jnp.zeros_like(acc_y)
            acc_g[...] = jnp.zeros_like(acc_g)

    size = weights[0].shape[1]
    each = blocks // PARTS
    for h in range(PARTS):

        @pl.when(step == h)
        def _():
            for k in range(each):
                at = slice(k * size, (k + 1) * size)
                up_s[at, :] = weights[h * each + k][0]
                down_s[at, :] = weights[h * each + k][1]

    tile = x_ref.shape[0] // 3

    def body(r, carry):
        at = pl.ds(pl.multiple_of(r * tile, tile), tile)
        value, slope = gelu_pair(dot(x_ref[at, :], up_s[...], NT))
        hidden = value.astype(jnp.bfloat16)
        grad_pre = (slope * dot(g_ref[at, :], down_s[...], NT)).astype(jnp.bfloat16)
        hid_ref[at, :] = hidden
        pre_ref[at, :] = grad_pre
        acc_y[at, :] += dot(hidden, down_s[...], NN)
        acc_g[at, :] += dot(grad_pre, up_s[...], NN)
        return carry

    lax.fori_loop(0, 3, body, 0)

    @pl.when(step == PARTS - 1)
    def _():
        out_ref[:, :D] = acc_y[...].astype(jnp.bfloat16)
        out_ref[:, D:] = acc_g[...].astype(jnp.bfloat16)


def run_expert(weights, e, xs, gs, before):
    blocks = len(weights)
    final = before is not None
    size = weights[0].shape[1]
    peers = 1 if final else len(xs)
    rows = xs.shape[0] if final else peers * xs[0].shape[1]
    cols = blocks * size
    part = cols // PARTS
    once = dict(pipeline_mode=pl.Buffered(1))

    def pick(shape):
        return pl.BlockSpec((1,) + shape, lambda h: (e, 0, 0), **once)

    in_specs = [pl.BlockSpec((2, size, D), lambda h: (e, 0, 0), **once)] * blocks
    column = pl.BlockSpec((rows, part), lambda h: (0, h))
    kept_specs, kept = [column, column], [b16s(rows, cols), b16s(rows, cols)]
    if final:
        operands = [xs, gs, before]
        in_specs += [full_spec(v.shape) for v in operands]
    else:
        operands = [*xs, *gs]
        in_specs += [pick(v.shape[1:]) for v in operands]
        kept_specs = [full_spec((rows, D))] * 2 + kept_specs
        kept = [b16s(rows, D)] * 2 + kept
    return pl.pallas_call(
        functools.partial(expert_kernel, blocks, peers, final),
        grid=(PARTS,),
        in_specs=in_specs,
        out_specs=[full_spec((rows, 2 * D))] + kept_specs,
        out_shape=[b16s(rows, 2 * D)] + kept,
        scratch_shapes=[
            pltpu.VMEM((part, D), jnp.bfloat16), pltpu.VMEM((part, D), jnp.bfloat16), vm(rows, D), vm(rows, D),
        ],
        compiler_params=params(),
        cost_estimate=pl.CostEstimate(flops=1000, bytes_accessed=1000, transcendentals=0),
        name="expert",
    )(*weights, *operands)


def weight_kernel(hid_ref, pre_ref, x_ref, g_ref, up_ref, down_ref):
    up_ref[...] = dot(pre_ref[...], x_ref[...], TN).astype(jnp.bfloat16)
    down_ref[...] = dot(hid_ref[...], g_ref[...], TN).astype(jnp.bfloat16)


def run_weight(hid, pre, x, g):
    rows, cols = hid.shape
    part = cols // 6
    column = pl.BlockSpec((rows, part), lambda c: (0, c))
    out = pl.BlockSpec((part, D), lambda c: (c, 0))
    return pl.pallas_call(
        weight_kernel,
        grid=(6,),
        in_specs=[column, column, full_spec((rows, D)), full_spec((rows, D))],
        out_specs=[out, out],
        out_shape=[b16s(cols, D), b16s(cols, D)],
        compiler_params=params(),
        cost_estimate=pl.CostEstimate(flops=1000, bytes_accessed=1000, transcendentals=0),
        name="weight",
    )(hid, pre, x, g)


def halves_of(value, seqs):
    split = value.reshape(value.shape[:-2] + (seqs, HALVES, value.shape[-1]))
    return split[..., 0, :], split[..., 1, :]


def join_halves(first, second):
    both = jnp.stack([first, second], axis=-2)
    return both.reshape(both.shape[:-3] + (both.shape[-3] * HALVES, both.shape[-1]))


def chained(own, decay, steps, beside):
    start = jnp.zeros_like(own)
    carry = own
    for k in range(lax.axis_size("seq") - 1):
        start = shifted(carry.astype(jnp.bfloat16), "seq", steps)
        if k < len(beside):
            start, beside[k] = held_for(start, beside[k])
        start = start.astype(jnp.float32)
        carry = own + decay * start
    return start


def start_states(ends, sums, rates, seqs, beside):
    end_0, end_1 = halves_of(ends, seqs)
    sum_0, sum_1 = halves_of(sums, seqs)
    decay_0 = jnp.exp(rates * sum_0)
    decay_1 = jnp.exp(rates * sum_1)
    start = chained(decay_1 * end_0 + end_1, decay_0 * decay_1, 1, beside)
    return join_halves(start, decay_0 * start + end_0), (decay_0, decay_1)


def last_grads(leads, decays, seqs, beside):
    decay_0, decay_1 = decays
    lead_0, lead_1 = halves_of(leads, seqs)
    last = chained(lead_0 + decay_0 * lead_1, decay_0 * decay_1, -1, beside)
    return join_halves(lead_1 + decay_1 * last, last)


def ring(value, axis, step):
    count = lax.axis_size(axis)
    return lax.ppermute(value, axis, [(i, (i + step) % count) for i in range(count)])


def partner(value, axis, bits):
    count = lax.axis_size(axis)
    return lax.ppermute(value, axis, [(i, i ^ bits) for i in range(count)])


def held_for(first, *others):
    flat, tree = jax.tree.flatten((first,) + others)
    return jax.tree.unflatten(tree, lax.optimization_barrier(flat))


class Gather:
    def __init__(self, own):
        self.here, self.there = [own], []
        self.peers = lax.axis_size("seq")

    def step(self):
        at = len(self.there)
        block = self.here[at]
        if at < self.peers - 1:
            self.there.append(ring(block, "dp", 1))
            self.here.append(ring(block, "seq", 1))
        else:
            half = block.shape[0] // 2
            self.there.append([ring(block[:half], "dp", 1), ring(self.there[-1][half:], "seq", 1)])

    def hold(self, value):
        value, here, there = held_for(value, self.here[1:], self.there)
        self.here[1:], self.there = here, there
        return value

    def done(self):
        return len(self.there) == self.peers


class Reduce:
    def __init__(self, here, there, x_first):
        self.peers = lax.axis_size("seq")
        here = here.reshape(self.peers, -1, D)
        there = there.reshape(self.peers, -1, D)
        self.x_first, self.k, self.total = x_first, self.peers, None
        self.blocks = [(here[k], there[k]) for k in range(self.peers)]
        if x_first:
            self.moving = ring(there, "dp", 1)
        else:
            self.advance()

    def term(self, k):
        if self.x_first:
            return self.blocks[k][0].astype(jnp.float32) + self.other[k].astype(jnp.float32)
        return jnp.stack(self.blocks[k]).astype(jnp.float32)

    def advance(self):
        self.k -= 1
        self.total = self.term(self.k) if self.total is None else self.term(self.k) + self.moving.astype(jnp.float32)
        if self.k > 0:
            self.moving = ring(self.total.astype(jnp.bfloat16), "seq", -1)
        elif self.x_first:
            self.moving = None
        else:
            self.moving = ring(self.total[1].astype(jnp.bfloat16), "dp", 1)

    def step(self):
        if self.moving is None:
            return
        if self.x_first and self.total is None:
            self.other = self.moving
            self.advance()
        elif self.k > 0:
            self.advance()
        else:
            self.total = self.total[0] + self.moving.astype(jnp.float32)
            self.moving = None

    def finish(self):
        while self.moving is not None:
            self.step()
        return self.total


def settle(value, reduces):
    live = [r for r in reduces if r.moving is not None]
    value, moved = held_for(value, [r.moving for r in live])
    for r, m in zip(live, moved):
        r.moving = m
    return value


def hold_all(value, reduces):
    live = [r for r in reduces if r.moving is not None]
    value, moved = held_for(value, [r.moving for r in live])
    for r, m in zip(live, moved):
        r.moving = m
        r.step()
    return value


class Halving:
    def __init__(self, value, axes, near_first):
        self.dims = [(axis, 1 << k) for axis in axes for k in reversed(range(lax.axis_size(axis).bit_length() - 1))]
        self.plan = [d for d in self.dims if near_first and d == ("expert", 1)]
        self.plan += [d for d in self.dims if d[0] == "expert" and d not in self.plan]
        self.plan += [d for d in self.dims if d not in self.plan]
        self.value = value.reshape((2,) * len(self.plan) + value.shape[1:])
        self.start()

    def start(self):
        axis, bit = self.plan.pop(0)
        dim = self.dims.index((axis, bit))
        self.dims.pop(dim)
        low, high = (lax.index_in_dim(self.value, k, dim, False) for k in range(2))
        upper = (lax.axis_index(axis) // bit) % 2 == 1
        self.keep = jnp.where(upper, high, low)
        self.moving = partner(jnp.where(upper, low, high).astype(jnp.bfloat16), axis, bit)

    def step(self):
        self.value = self.keep.astype(jnp.float32) + self.moving.astype(jnp.float32)
        self.moving = None
        if self.plan:
            self.start()

    def finish(self):
        while self.moving is not None:
            self.step()
        return self.value


def sum_everywhere(value):
    for axis in ALL:
        bits = 1
        while bits < lax.axis_size(axis):
            value = value + partner(value, axis, bits)
            bits *= 2
    return value


def exchange(blocks):
    return [blocks[0]] + [partner(blocks[d], "expert", d) for d in range(1, len(blocks))]


def local(
    tokens, segment_ids, routes, keep_mask, out_grad, norm_one, in_proj, conv_weight, conv_bias, x_proj,
    dt_proj, dt_bias, a_log, d_skip, out_proj, norm_two, router, expert_up, expert_down,
):
    seqs, length = tokens.shape[:2]
    rows = seqs * length
    steps = length // HALVES
    halo = CONVK - 1
    capacity = seqs * max(2, length * 3 // 16)
    f32, b16 = jnp.float32, jnp.bfloat16
    own = in_proj.shape[1]

    small = jnp.concatenate(
        [x_proj, dt_proj.T, conv_weight.T, conv_bias[:, None], dt_bias[:, None], a_log.T, d_skip[:, None]], axis=1
    )
    used = small.shape[1]
    small = jnp.pad(small, ((0, 0), (0, PACK - used)))
    entry = lax.all_gather(jnp.concatenate([in_proj.T, small.reshape(-1, D)], axis=0), ALL, axis=0, tiled=False)
    middle = entry.shape[0] // 2
    conv_full = entry[:middle, :own].reshape(DI, D)
    gate_full = entry[middle:, :own].reshape(DI, D)
    small = entry[:, own:].reshape(DI, PACK)
    out_full = lax.all_gather(out_proj, ALL, axis=0, tiled=True)
    local_experts = expert_up.shape[0]
    shard = jnp.stack([m for e in range(local_experts) for m in (expert_up[e].T, expert_down[e])])
    shard, conv_full = held_for(shard, conv_full)
    gather = Gather(shard)
    gather.step()

    xproj_full = small[:, :XW]
    dtw = small[:, XW : XW + DTR]
    at = XW + DTR
    rest = small[:, at:used].T
    conv_w = rest[:CONVK].astype(f32)
    cbias = rest[CONVK : CONVK + 1].astype(f32)
    dtb = rest[CONVK + 1 : CONVK + 2]
    alog = rest[CONVK + 2 : CONVK + 2 + NSTATE]
    skip = rest[CONVK + 2 + NSTATE :]

    halo_tokens = shifted(tokens[:, length - halo :], "seq", 1)
    halo_segs = shifted(segment_ids[:, length - halo :].astype(f32), "seq", 1)
    inputs = lax.optimization_barrier(to_ext_rows(tokens, halo_tokens)).astype(f32)
    seg_ext = to_ext_rows(segment_ids.astype(f32), halo_segs)
    drop = to_rows(keep_mask).astype(f32)
    route = to_rows(routes[..., 0])
    grad_low = lax.optimization_barrier(to_rows(out_grad))
    grad_final = grad_low.astype(f32)
    skip_rows = halo * SUB
    seg = seg_ext[skip_rows:]
    same = [(seg_ext[k * SUB : k * SUB + rows] == seg).astype(f32)[:, None] for k in range(halo)]
    same_wide = jnp.broadcast_to(jnp.stack(same), (halo, rows, LANES))
    cut = jnp.broadcast_to((1.0 - same[halo - 1]) * BIG, (rows, LANES))

    onehot = (route[:, None] == jnp.arange(EXPERTS, dtype=jnp.int32)).astype(f32)
    order = jnp.arange(rows)
    below = (order[None, :] < order[:, None]).astype(b16)
    rank = jnp.sum(dot(below, onehot.astype(b16), NN) * onehot, axis=-1).astype(jnp.int32)
    peers = lax.axis_size("expert")
    target = (route // local_experts) ^ lax.axis_index("expert")
    slot = (target * local_experts + route % local_experts) * capacity + rank
    placing = (jnp.arange(EXPERTS * capacity, dtype=jnp.int32)[:, None] == slot[None, :]).astype(b16)

    def dispatch(values):
        sent = dot(placing, values, NN, b16).reshape(peers, local_experts, capacity, values.shape[1])
        return exchange([sent[d] for d in range(peers)])

    gain_one = norm_one.astype(f32)
    inv_one = lax.rsqrt(jnp.mean(inputs * inputs, axis=-1, keepdims=True) + norm_eps)
    normed_one = (inputs * inv_one * gain_one).astype(b16)
    ext = dot(normed_one, conv_full, NT)
    gate_z = dot(normed_one[skip_rows:], gate_full, NT)
    conv_out = cbias + conv_w[halo] * ext[skip_rows:]
    for k in range(halo):
        conv_out = conv_out + conv_w[k] * (same[k] * ext[k * SUB : k * SUB + rows])
    xs = jax.nn.silu(conv_out).astype(b16)
    proj = dot(xs, xproj_full, NN)
    delta_in = proj[:, :DTR].astype(b16)
    bc = proj[:, DTR:]
    grad_arrived = dispatch(grad_low)
    delta, ends, sums = run_end(xs, delta_in, dtw, dtb, alog, bc, cut)
    ends, grad_arrived = held_for(gather.hold(ends), grad_arrived)
    rates = -jnp.exp(alog.astype(f32))[:, None, :]
    beside = [gate_z]
    starts, decays = start_states(ends, sums, rates, seqs, beside)
    gate_z = beside[0]
    starts = gather.hold(starts)
    gather.step()
    branch, ssm, held = run_out(xs, delta, alog, bc, cut, starts, gate_z, skip)
    tokens_rows = inputs[skip_rows:]
    first_sum = tokens_rows + dot(branch, out_full, NN)

    gain_two = norm_two.astype(f32)
    inv_two = lax.rsqrt(jnp.mean(first_sum * first_sum, axis=-1, keepdims=True) + norm_eps)
    normed_two = (first_sum * inv_two * gain_two).astype(b16)
    probs = jax.nn.softmax(dot(normed_two, router, NN), axis=-1)
    gate_raw = jnp.sum(probs * onehot, axis=-1)
    gate = gate_raw * drop
    gate_high = lax.reduce_precision(gate, 8, 7)
    gate_mid = lax.reduce_precision(gate - gate_high, 8, 7)
    gate_low = gate - gate_high - gate_mid
    gates = jnp.stack([gate_high, gate_mid, gate_low], axis=1).astype(b16)
    message = jnp.concatenate([normed_two, jnp.pad(gates, ((0, 0), (0, LANES - 3)))], axis=1)
    message = gather.hold(message)
    gather.step()
    arrived = gather.hold(dispatch(message))
    while not gather.done():
        gather.step()
    partial, for_weights = [], []
    for e in range(local_experts):
        done, *rest = run_expert(gather.here, e, arrived, grad_arrived, None)
        partial.append(done)
        for_weights.append(rest)
    partial = gather.hold(partial)
    theirs = gather.there[:-1] + [jnp.concatenate(gather.there[-1], axis=0)]
    returned = []
    for e in range(local_experts):
        done, *rest = run_expert(theirs, e, *for_weights[e][:2], partial[e])
        for_weights[e] += rest
        if e > 0:
            done, returned = held_for(done, returned)
        returned.append(exchange([part for part in done.reshape(peers, capacity, 2 * D)]))
    weight_grads = []
    for e in range(local_experts):
        x_rows, g_rows, *kept = for_weights[e]
        sides = [run_weight(kept[2 * k], kept[2 * k + 1], x_rows, g_rows) for k in range(2)]
        weight_grads += [(sides[0][m], sides[1][m]) for m in range(2)]
    returned[-1], weight_grads = held_for(returned[-1], weight_grads)
    count = len(weight_grads)
    reduces = [Reduce(g[0], g[1], i < count - 1) for i, g in enumerate(weight_grads)]
    returned = [jnp.stack([returned[e][d] for e in range(local_experts)]) for d in range(peers)]

    back_rows = jnp.stack(returned).reshape(EXPERTS * capacity, 2 * D)
    combined = dot(placing, back_rows, TN)
    expert_rows, grad_back = combined[:, :D], combined[:, D:]
    output = (first_sum + gate[:, None] * expert_rows).astype(b16)

    grad_gate = jnp.sum(grad_final * expert_rows, axis=-1) * drop
    grad_logits = (grad_gate * gate_raw)[:, None] * (onehot - probs)
    logits_low = grad_logits.astype(b16)
    router_grad = dot(normed_two, logits_low, TN)
    grad_two = grad_back + dot(logits_low, router, NT)
    gain_two_grad = jnp.sum(grad_two * (first_sum * inv_two), axis=0)
    scaled = grad_two * gain_two
    grad_first = (
        grad_final + inv_two * scaled
        - first_sum * (inv_two * inv_two * inv_two * jnp.mean(scaled * first_sum, axis=-1, keepdims=True))
    )
    first_low = grad_first.astype(b16)
    out_grad_part = dot(branch, first_low, TN, b16)
    grad_branch = dot(first_low, out_full, NT)
    grad_branch, out_grad_part = held_for(grad_branch, out_grad_part)
    grad_branch = hold_all(grad_branch, reduces[-1:])

    leads, grad_z, grad_ssm = run_first(delta, alog, bc, cut, grad_branch, gate_z, ssm)
    leads = settle(leads, [reduces[0], reduces[-1]])
    gate_part = dot(grad_z, normed_one[skip_rows:], TN, b16)
    grad_normed_z = dot(grad_z, gate_full, NN)
    beside = [gate_part, grad_normed_z, router_grad]
    last = last_grads(leads, decays, seqs, beside)
    gate_part, grad_normed_z, router_grad = beside
    last, out_grad_part, gate_part = held_for(last, out_grad_part, gate_part)
    out_sum = lax.psum_scatter(out_grad_part, ALL, scatter_dimension=0, tiled=True)
    gate_own = lax.psum_scatter(gate_part, ("seq", "expert"), scatter_dimension=0, tiled=True)
    grad_delta_in, gbc, parts = 0.0, 0.0, []
    width = DI // SPLITS
    for part in range(SPLITS):
        if part == SPLITS - 1:
            last, out_sum = held_for(last, out_sum)
        last = hold_all(last, reduces[: 1 + part] + reduces[-1:] if 1 + part < count else reduces)
        gxs, gpre, galog, gvec, gbc_part = run_back(xs, delta, alog, bc, cut, grad_ssm, skip, held, last, part)
        grad_delta_in = grad_delta_in + dot(gpre, dtw[part * width : (part + 1) * width], NN)
        gbc = gbc + gbc_part[:, : 2 * NSTATE]
        dtproj_part = dot(gpre, delta_in, TN)
        last, gxs, dtproj_part, grad_delta_in, gbc, galog, gvec = held_for(
            last, gxs, dtproj_part, grad_delta_in, gbc, galog, gvec
        )
        parts.append((gxs, dtproj_part, galog, gvec))
    grad_proj = jnp.concatenate([grad_delta_in, gbc], axis=1).astype(b16)
    grad_proj, gate_own = held_for(hold_all(grad_proj, reduces), gate_own)
    xproj_grad = dot(xs, grad_proj, TN)
    zeros = jnp.zeros((CONVK + 1, DI), f32)
    vecs = jnp.concatenate([p[3] for p in parts], axis=1)
    small_grad = jnp.concatenate(
        [
            xproj_grad,
            jnp.concatenate([p[1] for p in parts], axis=0),
            zeros.T,
            vecs[0][:, None],
            jnp.concatenate([p[2] for p in parts], axis=1).T,
            vecs[1][:, None],
        ],
        axis=1,
    ).astype(b16)
    small_grad = jnp.pad(small_grad, ((0, 0), (0, PACK - used)))
    small_grad, grad_proj = held_for(small_grad, grad_proj)
    small_half = Halving(small_grad.reshape(-1, own // 2, PACK), ALL, True)
    gexts, conv_parts, conv_grads = [], [], []
    for part in range(SPLITS):
        gext, gvec = run_conv(parts[part][0], grad_proj, xproj_full, ext, conv_w, cbias, same_wide, part)
        if part == SPLITS - 1:
            gext = hold_all(gext, reduces)
        conv_parts.append(dot(gext, normed_one, TN, b16))
        gexts.append(gext)
        conv_grads.append(gvec)
    conv_all, gexts = held_for(jnp.concatenate(conv_parts, axis=0), gexts)
    conv_own = lax.psum_scatter(conv_all, ("seq", "expert"), scatter_dimension=0, tiled=True).astype(f32)
    grad_normed = sum(dot(gexts[k], conv_full[k * width : (k + 1) * width], NN) for k in range(SPLITS))
    over = grad_normed[:skip_rows].reshape(halo, seqs, HALVES, D)
    from_next = shifted(over[:, :, 0], "seq", -1)
    edge = jnp.stack([over[:, :, 1], from_next], axis=2).reshape(skip_rows, D)
    grad_normed = grad_normed[skip_rows:] + grad_normed_z
    grad_normed = grad_normed + jnp.pad(edge, ((rows - skip_rows, 0), (0, 0)))
    inv_rows = inv_one[skip_rows:]
    gain_one_grad = jnp.sum(grad_normed * (tokens_rows * inv_rows), axis=0)
    scaled_one = grad_normed * gain_one
    grad_tokens = (
        grad_first + inv_rows * scaled_one
        - tokens_rows * (inv_rows * inv_rows * inv_rows * jnp.mean(scaled_one * tokens_rows, axis=-1, keepdims=True))
    )
    conv_grad = jnp.concatenate(conv_grads, axis=1)[: CONVK + 1]
    flat = jnp.concatenate([gain_one_grad, gain_two_grad, router_grad.reshape(-1), conv_grad.reshape(-1)])
    flat = sum_everywhere(flat.reshape(-1, LANES)).reshape(-1)
    small_sum = small_half.finish()
    is_gate = lax.axis_index("dp") == 1
    gate_own = gate_own.astype(f32)
    in_sum = jnp.where(is_gate, gate_own, conv_own)
    in_sum = in_sum + ring(jnp.where(is_gate, conv_own, gate_own).astype(b16), "dp", 1).astype(f32)
    gain_one_sum, gain_two_sum = flat[:D], flat[D : 2 * D]
    router_sum = flat[2 * D : (2 + EXPERTS) * D].reshape(D, EXPERTS)
    conv_sum = flat[(2 + EXPERTS) * D :].reshape(CONVK + 1, DI)
    place = (lax.axis_index("dp") * lax.axis_size("seq") + lax.axis_index("seq")) * peers + lax.axis_index("expert")
    channels = own // 2
    conv_sum = lax.dynamic_slice_in_dim(conv_sum, place * channels, channels, axis=1)

    small_sum = small_sum.T
    return (
        from_rows(output, seqs),
        from_rows(grad_tokens, seqs),
        gain_one_sum,
        in_sum.T,
        conv_sum[:CONVK],
        conv_sum[CONVK],
        small_sum[:XW].T,
        small_sum[XW : XW + DTR],
        small_sum[at + CONVK + 1],
        small_sum[at + CONVK + 2 : at + CONVK + 2 + NSTATE],
        small_sum[used - 1],
        out_sum.astype(f32),
        gain_two_sum,
        router_sum,
        jnp.stack([r.finish().T for r in reduces[0::2]]),
        jnp.stack([r.finish() for r in reduces[1::2]]),
    )


def solution(mesh):
    batch = ("dp", "expert")
    split = ("dp", "seq")
    return jax.shard_map(
        local,
        mesh=mesh,
        in_specs=(
            P(batch, "seq", None),
            P(batch, "seq"),
            P(batch, "seq", None),
            P(batch, "seq"),
            P(batch, "seq", None),
            P(),
            P(None, ALL),
            P(None, ALL),
            P(ALL),
            P(ALL, None),
            P(None, ALL),
            P(ALL),
            P(None, ALL),
            P(ALL),
            P(ALL, None),
            P(),
            P(),
            P("expert", None, split),
            P("expert", split, None),
        ),
        out_specs=(
            P(batch, "seq", None),
            P(batch, "seq", None),
            P(),
            P(None, ALL),
            P(None, ALL),
            P(ALL),
            P(ALL, None),
            P(None, ALL),
            P(ALL),
            P(None, ALL),
            P(ALL),
            P(ALL, None),
            P(),
            P(),
            P("expert", None, split),
            P("expert", split, None),
        ),
        check_vma=False,
    )
```

```python
import functools

import jax
import jax.numpy as jnp
from jax import lax
from jax.experimental import pallas as pl
from jax.experimental.pallas import tpu as pltpu
from jax.sharding import PartitionSpec as P

D = 1152
DI = 2304
NSTATE = 16
DTR = 72
CONVK = 4
EXPERTS = 8
XW = DTR + 2 * NSTATE
HALVES = 2
LANES = 128
LN2 = 0.6931471805599453
SPLITS = 3
SUB = 8
PACK = 256
CHUNK = 16
BIG = 1e30
VMEM = 60 * 1024 * 1024

norm_eps = 1e-05
ALL = ("dp", "seq", "expert")


def shifted(value, axis, steps):
    count = lax.axis_size(axis)
    first, last = (max(0, -steps), min(count, count - steps))
    return lax.ppermute(value, axis, [(source, source + steps) for source in range(first, last)])


def dot(left, right, dims, out=jnp.float32):
    return lax.dot_general(left, right, (dims, ((), ())), preferred_element_type=out)


NN = ((1,), (0,))
NT = ((1,), (1,))
TN = ((0,), (0,))


def to_rows(value):
    seqs, length = value.shape[:2]
    rest = value.shape[2:]
    split = value.reshape((seqs, HALVES, length // HALVES) + rest)
    return jnp.moveaxis(split, 2, 0).reshape((seqs * length,) + rest)


def from_rows(value, seqs):
    rest = value.shape[1:]
    length = value.shape[0] // seqs
    split = value.reshape((length // HALVES, seqs, HALVES) + rest)
    return jnp.moveaxis(split, 0, 2).reshape((seqs, length) + rest)


def to_ext_rows(value, halo):
    seqs, length = value.shape[:2]
    rest = value.shape[2:]
    part = length // HALVES
    ext = jnp.concatenate([halo, value], axis=1)
    split = jnp.stack([ext[:, h * part : h * part + part + CONVK - 1] for h in range(HALVES)], axis=1)
    return jnp.moveaxis(split, 2, 0).reshape(((part + CONVK - 1) * seqs * HALVES,) + rest)


def decay_rates(alog_ref, a_s):
    rates = -(1.0 / LN2) * jnp.exp(alog_ref[...].astype(jnp.float32))
    for n in range(NSTATE):
        a_s[n] = jnp.broadcast_to(rates[n : n + 1, :], (SUB, LANES))


def spread(src_ref, dst, first):
    src = src_ref[...]
    high = src.astype(jnp.bfloat16)
    both = jnp.concatenate([high, (src - high.astype(jnp.float32)).astype(jnp.bfloat16)], axis=1)
    line = lax.broadcasted_iota(jnp.int32, (4 * NSTATE, 2 * LANES), 0)
    shift = jnp.where(lax.broadcasted_iota(jnp.int32, (4 * NSTATE, 2 * LANES), 1) < LANES, 0, NSTATE // 2)

    def body(n, carry):
        wanted = shift + (first + n)
        pick = (line == wanted) | (line == wanted + 2 * NSTATE)
        wide = dot(both, jnp.where(pick, 1.0, 0.0).astype(jnp.bfloat16), NN)
        dst[n] = wide[:, :LANES]
        dst[n + NSTATE // 2] = wide[:, LANES:]
        return carry

    lax.fori_loop(0, NSTATE // 2, body, 0)


def tree_sum(parts):
    while len(parts) > 1:
        parts = [parts[i] + parts[i + 1] if i + 1 < len(parts) else parts[i] for i in range(0, len(parts), 2)]
    return parts[0]


UNROLL = 8


def unrolled(first, count, body, carry):
    def group(i, inner):
        for u in range(UNROLL):
            inner = body(first + i * UNROLL + u, inner)
        return inner

    return lax.fori_loop(0, count // UNROLL, group, carry)


def row_at(t):
    return pl.ds(pl.multiple_of(t * SUB, SUB), SUB)


def end_kernel(xs_ref, din_ref, dtw_ref, dtb_ref, alog_ref, bc_ref, cut_ref, delta_ref, end_ref, sum_ref, b_s, a_s, dx_s):
    steps = delta_ref.shape[0] // SUB

    @pl.when(pl.program_id(0) == 0)
    def _():
        spread(bc_ref, b_s, 0)

    decay_rates(alog_ref, a_s)
    pre = dot(din_ref[...], dtw_ref[...], NT) + dtb_ref[...].astype(jnp.float32)
    low = jnp.exp(-jnp.abs(pre))
    delta = jnp.maximum(pre, 0.0) + jnp.where(low < 0.01, low * (1.0 - low * (0.5 - low * (1.0 / 3.0))), jnp.log(1.0 + low))
    delta_ref[...] = delta
    dx_s[...] = delta * xs_ref[...].astype(jnp.float32)
    rates = [a_s[n] for n in range(NSTATE)]

    def body(t, carry):
        total, state = carry
        at = row_at(t)
        step = jnp.maximum(delta_ref[at, :], cut_ref[at, :])
        dx = dx_s[at, :]
        state = [jnp.exp2(step * rates[n]) * state[n] + dx * b_s[n, at, :] for n in range(NSTATE)]
        return (total + step, state)

    zero = jnp.zeros((SUB, LANES), jnp.float32)
    total, state = unrolled(0, steps, body, (zero, [zero] * NSTATE))
    sum_ref[...] = total
    for n in range(NSTATE):
        end_ref[n] = state[n]


def out_kernel(xs_ref, delta_ref, alog_ref, bc_ref, cut_ref, start_ref, z_ref, skip_ref, branch_ref, ssm_ref, held_ref, b_s, c_s, a_s, dx_s, y_s):
    steps = delta_ref.shape[0] // SUB

    @pl.when(pl.program_id(0) == 0)
    def _():
        spread(bc_ref, b_s, 0)
        spread(bc_ref, c_s, NSTATE)

    decay_rates(alog_ref, a_s)
    xs = xs_ref[...].astype(jnp.float32)
    dx_s[...] = delta_ref[...] * xs
    rates = [a_s[n] for n in range(NSTATE)]

    def body(t, state):
        at = row_at(t)
        step = jnp.maximum(delta_ref[at, :], cut_ref[at, :])
        dx = dx_s[at, :]
        state = [jnp.exp2(step * rates[n]) * state[n] + dx * b_s[n, at, :] for n in range(NSTATE)]
        y_s[at, :] = tree_sum([state[n] * c_s[n, at, :] for n in range(NSTATE)])
        return state

    def chunk(i, state):
        for n in range(NSTATE):
            held_ref[i, n] = state[n]
        return unrolled(i * CHUNK, CHUNK, body, state)

    lax.fori_loop(0, steps // CHUNK, chunk, [start_ref[n] for n in range(NSTATE)])
    ssm = y_s[...] + skip_ref[...].astype(jnp.float32) * xs
    z = z_ref[...]
    ssm_ref[...] = ssm.astype(jnp.bfloat16)
    branch_ref[...] = (ssm * (z / (1.0 + jnp.exp(-z)))).astype(jnp.bfloat16)


def first_kernel(delta_ref, alog_ref, bc_ref, cut_ref, gb_ref, z_ref, ssm_ref, lead_ref, gz_ref, g_s, c_s, a_s):
    steps = delta_ref.shape[0] // SUB

    @pl.when(pl.program_id(0) == 0)
    def _():
        spread(bc_ref, c_s, NSTATE)

    decay_rates(alog_ref, a_s)
    z = z_ref[...]
    grad = gb_ref[...]
    sig = 1.0 / (1.0 + jnp.exp(-z))
    g_s[...] = grad * (z * sig)
    gz_ref[...] = (grad * ssm_ref[...].astype(jnp.float32) * (sig * (1.0 + z * (1.0 - sig)))).astype(jnp.bfloat16)
    rates = [a_s[n] for n in range(NSTATE)]

    def body(k, lead):
        at = row_at(steps - 1 - k)
        step = jnp.maximum(delta_ref[at, :], cut_ref[at, :])
        g = g_s[at, :]
        return [jnp.exp2(step * rates[n]) * (lead[n] + g * c_s[n, at, :]) for n in range(NSTATE)]

    zero = jnp.zeros((SUB, LANES), jnp.float32)
    lead = unrolled(0, steps, body, [zero] * NSTATE)
    for n in range(NSTATE):
        lead_ref[n] = lead[n]


def back_kernel(
    xs_ref, delta_ref, alog_ref, bc_ref, cut_ref, g_ref, skip_ref, held_ref, last_ref,
    gxs_ref, gpre_ref, galog_ref, gvec_ref, gbc_ref,
    b_s, c_s, gb_s, gc_s, a_s, dx_s, x_s, gx_s, gd_s, hd_s, dec_s,
):
    steps = delta_ref.shape[0] // SUB

    @pl.when(pl.program_id(0) == 0)
    def _():
        spread(bc_ref, b_s, 0)
        spread(bc_ref, c_s, NSTATE)
        gb_s[...] = jnp.zeros_like(gb_s)
        gc_s[...] = jnp.zeros_like(gc_s)

    decay_rates(alog_ref, a_s)
    xs = xs_ref[...].astype(jnp.float32)
    x_s[...] = xs
    dx_s[...] = delta_ref[...] * xs

    rates = [a_s[n] for n in range(NSTATE)]

    def ahead(j, state, base):
        at = row_at(base + j)
        step = jnp.maximum(delta_ref[at, :], cut_ref[at, :])
        dx = dx_s[at, :]
        g = g_ref[at, :]
        new = []
        for n in range(NSTATE):
            dec = jnp.exp2(step * rates[n])
            hd = dec * state[n]
            dec_s[j, n] = dec
            hd_s[j, n] = hd
            h = hd + dx * b_s[n, at, :]
            gc_s[n, at, :] = gc_s[n, at, :] + g * h
            new.append(h)
        return new

    def behind(k, carry, base):
        coming, rate_grad = carry
        j = CHUNK - 1 - k
        at = row_at(base + j)
        delta = delta_ref[at, :]
        dx = dx_s[at, :]
        g = g_ref[at, :]
        next_coming, next_rate, with_b, with_a = [], [], [], []
        for n in range(NSTATE):
            lam = coming[n] + g * c_s[n, at, :]
            with_b.append(lam * b_s[n, at, :])
            gb_s[n, at, :] = gb_s[n, at, :] + lam * dx
            q = lam * hd_s[j, n]
            with_a.append(q * a_s[n])
            next_rate.append(rate_grad[n] + delta * q)
            next_coming.append(lam * dec_s[j, n])
        by_b = tree_sum(with_b)
        gx_s[at, :] = by_b * delta
        gd_s[at, :] = by_b * x_s[at, :] + LN2 * tree_sum(with_a)
        return (next_coming, next_rate)

    chunks = steps // CHUNK

    def chunk(i, carry):
        c = chunks - 1 - i
        base = c * CHUNK
        unrolled(0, CHUNK, functools.partial(ahead, base=base), [held_ref[c, n] for n in range(NSTATE)])
        return unrolled(0, CHUNK, functools.partial(behind, base=base), carry)

    zero = jnp.zeros((SUB, LANES), jnp.float32)
    _, rate_grad = lax.fori_loop(0, chunks, chunk, ([last_ref[n] for n in range(NSTATE)], [zero] * NSTATE))
    for n in range(NSTATE):
        galog_ref[n : n + 1, :] = LN2 * jnp.sum(rate_grad[n] * a_s[n], axis=0, keepdims=True)
    skip = skip_ref[...].astype(jnp.float32)
    grad_ssm = g_ref[...]
    gxs_ref[...] = gx_s[...] + grad_ssm * skip
    delta = delta_ref[...]
    slope = jnp.where(delta < 0.01, delta * (1.0 - 0.5 * delta * (1.0 - delta * (1.0 / 3.0))), 1.0 - jnp.exp(-delta))
    gpre = gd_s[...] * slope
    gpre_ref[...] = gpre.astype(jnp.bfloat16)
    gvec_ref[0:1, :] = jnp.sum(gpre, axis=0, keepdims=True)
    gvec_ref[1:2, :] = jnp.sum(grad_ssm * xs, axis=0, keepdims=True)
    gvec_ref[2:SUB, :] = jnp.zeros((SUB - 2, LANES), jnp.float32)

    @pl.when(pl.program_id(0) == pl.num_programs(0) - 1)
    def _():
        lane = lax.broadcasted_iota(jnp.int32, (2 * LANES, LANES), 1)
        line = lax.broadcasted_iota(jnp.int32, (2 * LANES, LANES), 0)
        gbc_ref[...] = jnp.zeros_like(gbc_ref)

        def gather(n, carry):
            pick = jnp.where(lane == jnp.where(line < LANES, n, NSTATE + n), 1.0, 0.0).astype(jnp.bfloat16)
            both = jnp.concatenate([gb_s[n].astype(jnp.bfloat16), gc_s[n].astype(jnp.bfloat16)], axis=1)
            gbc_ref[...] += dot(both, pick, NN)
            return carry

        lax.fori_loop(0, NSTATE, gather, 0)


def col_spec(rows):
    return pl.BlockSpec((rows, LANES), lambda c: (0, c))


def full_spec(shape):
    return pl.BlockSpec(shape, lambda c: (0,) * len(shape))


def state_spec():
    return pl.BlockSpec((NSTATE, SUB, LANES), lambda c: (0, 0, c))


def params():
    return pltpu.CompilerParams(vmem_limit_bytes=VMEM)


def f32s(*shape):
    return jax.ShapeDtypeStruct(shape, jnp.float32)


def b16s(*shape):
    return jax.ShapeDtypeStruct(shape, jnp.bfloat16)


def vm(*shape):
    return pltpu.VMEM(shape, jnp.float32)


def cost(rows, width, per_value):
    work = rows * width * NSTATE
    return pl.CostEstimate(flops=work * 8, bytes_accessed=work * per_value, transcendentals=work)


def run_end(xs, din, dtw, dtb, alog, bc, cut):
    rows = xs.shape[0]
    return pl.pallas_call(
        end_kernel,
        grid=(DI // LANES,),
        in_specs=[
            col_spec(rows), full_spec(din.shape), pl.BlockSpec((LANES, DTR), lambda c: (c, 0)),
            col_spec(1), col_spec(NSTATE), full_spec(bc.shape), full_spec(cut.shape),
        ],
        out_specs=[col_spec(rows), state_spec(), col_spec(SUB)],
        out_shape=[f32s(rows, DI), f32s(NSTATE, SUB, DI), f32s(SUB, DI)],
        scratch_shapes=[vm(NSTATE, rows, LANES), vm(NSTATE, SUB, LANES), vm(rows, LANES)],
        compiler_params=params(),
        cost_estimate=cost(rows, DI, 4),
        name="end",
    )(xs, din, dtw, dtb, alog, bc, cut)


def run_out(xs, delta, alog, bc, cut, start, z, skip):
    rows = xs.shape[0]
    chunks = rows // SUB // CHUNK
    return pl.pallas_call(
        out_kernel,
        grid=(DI // LANES,),
        in_specs=[
            col_spec(rows), col_spec(rows), col_spec(NSTATE), full_spec(bc.shape), full_spec(cut.shape),
            state_spec(), col_spec(rows), col_spec(1),
        ],
        out_specs=[
            col_spec(rows), col_spec(rows),
            pl.BlockSpec((chunks, NSTATE, SUB, LANES), lambda c: (0, 0, 0, c)),
        ],
        out_shape=[b16s(rows, DI), b16s(rows, DI), f32s(chunks, NSTATE, SUB, DI)],
        scratch_shapes=[
            vm(NSTATE, rows, LANES), vm(NSTATE, rows, LANES), vm(NSTATE, SUB, LANES), vm(rows, LANES), vm(rows, LANES),
        ],
        compiler_params=params(),
        cost_estimate=cost(rows, DI, 5),
        name="out",
    )(xs, delta, alog, bc, cut, start, z, skip)


def run_first(delta, alog, bc, cut, gbranch, z, ssm):
    rows = delta.shape[0]
    return pl.pallas_call(
        first_kernel,
        grid=(DI // LANES,),
        in_specs=[
            col_spec(rows), col_spec(NSTATE), full_spec(bc.shape), full_spec(cut.shape), col_spec(rows), col_spec(rows),
            col_spec(rows),
        ],
        out_specs=[state_spec(), col_spec(rows), col_spec(rows)],
        out_shape=[f32s(NSTATE, SUB, DI), b16s(rows, DI), f32s(rows, DI)],
        scratch_shapes=[vm(NSTATE, rows, LANES), vm(NSTATE, SUB, LANES)],
        compiler_params=params(),
        cost_estimate=pl.CostEstimate(flops=1000, bytes_accessed=1000, transcendentals=0),
        name="first",
    )(delta, alog, bc, cut, gbranch, z, ssm)


def run_back(xs, delta, alog, bc, cut, grad_ssm, skip, held, last, part):
    rows = xs.shape[0]
    chunks = rows // SUB // CHUNK
    big = (NSTATE, rows, LANES)
    row = (rows, LANES)
    width = DI // SPLITS
    first = part * (width // LANES)

    def col(count):
        return pl.BlockSpec((count, LANES), lambda c: (0, c + first))

    return pl.pallas_call(
        back_kernel,
        grid=(width // LANES,),
        in_specs=[
            col(rows), col(rows), col(NSTATE), full_spec(bc.shape), full_spec(cut.shape), col(rows), col(1),
            pl.BlockSpec((chunks, NSTATE, SUB, LANES), lambda c: (0, 0, 0, c + first)),
            pl.BlockSpec((NSTATE, SUB, LANES), lambda c: (0, 0, c + first)),
        ],
        out_specs=[col_spec(rows), col_spec(rows), col_spec(NSTATE), col_spec(SUB), full_spec(row)],
        out_shape=[f32s(rows, width), b16s(rows, width), f32s(NSTATE, width), f32s(SUB, width), f32s(*row)],
        scratch_shapes=[
            vm(*big), vm(*big), vm(*big), vm(*big), vm(NSTATE, SUB, LANES),
            vm(*row), vm(*row), vm(*row), vm(*row),
            vm(CHUNK, NSTATE, SUB, LANES), vm(CHUNK, NSTATE, SUB, LANES),
        ],
        compiler_params=params(),
        cost_estimate=cost(rows, width, 17),
        name="back",
    )(xs, delta, alog, bc, cut, grad_ssm, skip, held, last)


def conv_kernel(gxs_ref, gproj_ref, xproj_ref, ext_ref, taps_ref, bias_ref, same_ref, gext_ref, gvec_ref, acc_s):
    rows = gxs_ref.shape[0]
    halo = CONVK - 1
    taps = taps_ref[...]
    bias = bias_ref[...]
    pieces = []
    conv = bias
    for k in range(CONVK):
        piece = ext_ref[k * SUB : k * SUB + rows, :]
        if k < halo:
            piece = piece * same_ref[k]
        pieces.append(piece)
        conv = conv + taps[k : k + 1, :] * piece
    sig = 1.0 / (1.0 + jnp.exp(-conv))
    grad = gxs_ref[...] + dot(gproj_ref[...], xproj_ref[...], NT)
    grad = grad * (sig * (1.0 + conv * (1.0 - sig)))
    acc_s[...] = jnp.zeros_like(acc_s)
    for k in range(CONVK):
        gvec_ref[k : k + 1, :] = jnp.sum(grad * pieces[k], axis=0, keepdims=True)
        part = taps[k : k + 1, :] * grad
        if k < halo:
            part = part * same_ref[k]
        acc_s[k * SUB : k * SUB + rows, :] += part
    gvec_ref[CONVK : CONVK + 1, :] = jnp.sum(grad, axis=0, keepdims=True)
    gvec_ref[CONVK + 1 : SUB, :] = jnp.zeros((SUB - CONVK - 1, LANES), jnp.float32)
    gext_ref[...] = acc_s[...].astype(jnp.bfloat16)


def run_conv(gxs, gproj, xproj, ext, taps, bias, same, part):
    rows, width = gxs.shape
    long = ext.shape[0]
    first = part * (width // LANES)

    def col(count):
        return pl.BlockSpec((count, LANES), lambda c: (0, c + first))

    return pl.pallas_call(
        conv_kernel,
        grid=(width // LANES,),
        in_specs=[
            col_spec(rows), full_spec(gproj.shape), pl.BlockSpec((LANES, XW), lambda c: (c + first, 0)), col(long),
            col(CONVK), col(1), full_spec(same.shape),
        ],
        out_specs=[col_spec(long), col_spec(SUB)],
        out_shape=[b16s(long, width), f32s(SUB, width)],
        scratch_shapes=[vm(long, LANES)],
        compiler_params=params(),
        cost_estimate=pl.CostEstimate(flops=rows * width * 260, bytes_accessed=rows * width * 10, transcendentals=rows * width),
        name="conv",
    )(gxs, gproj, xproj, ext, taps, bias, same)


def gelu_pair(v):
    inner = 0.7978845608 * (v + 0.044715 * v * v * v)
    t = jnp.tanh(inner)
    value = 0.5 * v * (1.0 + t)
    slope = 0.5 * (1.0 + t) + 0.5 * v * (1.0 - t * t) * (0.7978845608 * (1.0 + 3.0 * 0.044715 * v * v))
    return value, slope


PARTS = 2


def expert_kernel(blocks, peers, final, *refs):
    weights, refs = refs[:blocks], refs[blocks:]
    step = pl.program_id(0)
    if final:
        x_ref, g_ref, before, out_ref, hid_ref, pre_ref, up_s, down_s, acc_y, acc_g = refs

        @pl.when(step == 0)
        def _():
            acc_y[...] = before[:, :D].astype(jnp.float32)
            acc_g[...] = before[:, D:].astype(jnp.float32)

    else:
        xs, gs, refs = refs[:peers], refs[peers : 2 * peers], refs[2 * peers :]
        out_ref, x_ref, g_ref, hid_ref, pre_ref, up_s, down_s, acc_y, acc_g = refs
        cap = xs[0].shape[1]

        @pl.when(step == 0)
        def _():
            for d in range(peers):
                at = slice(d * cap, (d + 1) * cap)
                piece = xs[d][0]
                x_ref[at, :] = piece[:, :D]
                gate = jnp.sum(piece[:, D:].astype(jnp.float32), axis=1, keepdims=True)
                g_ref[at, :] = (gate * gs[d][0].astype(jnp.float32)).astype(jnp.bfloat16)
            acc_y[...] = jnp.zeros_like(acc_y)
            acc_g[...] = jnp.zeros_like(acc_g)

    size = weights[0].shape[1]
    each = blocks // PARTS
    for h in range(PARTS):

        @pl.when(step == h)
        def _():
            for k in range(each):
                at = slice(k * size, (k + 1) * size)
                up_s[at, :] = weights[h * each + k][0]
                down_s[at, :] = weights[h * each + k][1]

    tile = x_ref.shape[0] // 3

    def body(r, carry):
        at = pl.ds(pl.multiple_of(r * tile, tile), tile)
        value, slope = gelu_pair(dot(x_ref[at, :], up_s[...], NT))
        hidden = value.astype(jnp.bfloat16)
        grad_pre = (slope * dot(g_ref[at, :], down_s[...], NT)).astype(jnp.bfloat16)
        hid_ref[at, :] = hidden
        pre_ref[at, :] = grad_pre
        acc_y[at, :] += dot(hidden, down_s[...], NN)
        acc_g[at, :] += dot(grad_pre, up_s[...], NN)
        return carry

    lax.fori_loop(0, 3, body, 0)

    @pl.when(step == PARTS - 1)
    def _():
        out_ref[:, :D] = acc_y[...].astype(jnp.bfloat16)
        out_ref[:, D:] = acc_g[...].astype(jnp.bfloat16)


def run_expert(weights, e, xs, gs, before):
    blocks = len(weights)
    final = before is not None
    size = weights[0].shape[1]
    peers = 1 if final else len(xs)
    rows = xs.shape[0] if final else peers * xs[0].shape[1]
    cols = blocks * size
    part = cols // PARTS
    once = dict(pipeline_mode=pl.Buffered(1))

    def pick(shape):
        return pl.BlockSpec((1,) + shape, lambda h: (e, 0, 0), **once)

    in_specs = [pl.BlockSpec((2, size, D), lambda h: (e, 0, 0), **once)] * blocks
    column = pl.BlockSpec((rows, part), lambda h: (0, h))
    kept_specs, kept = [column, column], [b16s(rows, cols), b16s(rows, cols)]
    if final:
        operands = [xs, gs, before]
        in_specs += [full_spec(v.shape) for v in operands]
    else:
        operands = [*xs, *gs]
        in_specs += [pick(v.shape[1:]) for v in operands]
        kept_specs = [full_spec((rows, D))] * 2 + kept_specs
        kept = [b16s(rows, D)] * 2 + kept
    return pl.pallas_call(
        functools.partial(expert_kernel, blocks, peers, final),
        grid=(PARTS,),
        in_specs=in_specs,
        out_specs=[full_spec((rows, 2 * D))] + kept_specs,
        out_shape=[b16s(rows, 2 * D)] + kept,
        scratch_shapes=[
            pltpu.VMEM((part, D), jnp.bfloat16), pltpu.VMEM((part, D), jnp.bfloat16), vm(rows, D), vm(rows, D),
        ],
        compiler_params=params(),
        cost_estimate=pl.CostEstimate(flops=1000, bytes_accessed=1000, transcendentals=0),
        name="expert",
    )(*weights, *operands)


def weight_kernel(hid_ref, pre_ref, x_ref, g_ref, up_ref, down_ref):
    up_ref[...] = dot(pre_ref[...], x_ref[...], TN).astype(jnp.bfloat16)
    down_ref[...] = dot(hid_ref[...], g_ref[...], TN).astype(jnp.bfloat16)


def run_weight(hid, pre, x, g):
    rows, cols = hid.shape
    part = cols // 6
    column = pl.BlockSpec((rows, part), lambda c: (0, c))
    out = pl.BlockSpec((part, D), lambda c: (c, 0))
    return pl.pallas_call(
        weight_kernel,
        grid=(6,),
        in_specs=[column, column, full_spec((rows, D)), full_spec((rows, D))],
        out_specs=[out, out],
        out_shape=[b16s(cols, D), b16s(cols, D)],
        compiler_params=params(),
        cost_estimate=pl.CostEstimate(flops=1000, bytes_accessed=1000, transcendentals=0),
        name="weight",
    )(hid, pre, x, g)


def halves_of(value, seqs):
    split = value.reshape(value.shape[:-2] + (seqs, HALVES, value.shape[-1]))
    return split[..., 0, :], split[..., 1, :]


def join_halves(first, second):
    both = jnp.stack([first, second], axis=-2)
    return both.reshape(both.shape[:-3] + (both.shape[-3] * HALVES, both.shape[-1]))


def chained(own, decay, steps, beside):
    start = jnp.zeros_like(own)
    carry = own
    for k in range(lax.axis_size("seq") - 1):
        start = shifted(carry.astype(jnp.bfloat16), "seq", steps)
        if k < len(beside):
            start, beside[k] = held_for(start, beside[k])
        start = start.astype(jnp.float32)
        carry = own + decay * start
    return start


def start_states(ends, sums, rates, seqs, beside):
    end_0, end_1 = halves_of(ends, seqs)
    sum_0, sum_1 = halves_of(sums, seqs)
    decay_0 = jnp.exp(rates * sum_0)
    decay_1 = jnp.exp(rates * sum_1)
    start = chained(decay_1 * end_0 + end_1, decay_0 * decay_1, 1, beside)
    return join_halves(start, decay_0 * start + end_0), (decay_0, decay_1)


def last_grads(leads, decays, seqs, beside):
    decay_0, decay_1 = decays
    lead_0, lead_1 = halves_of(leads, seqs)
    last = chained(lead_0 + decay_0 * lead_1, decay_0 * decay_1, -1, beside)
    return join_halves(lead_1 + decay_1 * last, last)


def ring(value, axis, step):
    count = lax.axis_size(axis)
    return lax.ppermute(value, axis, [(i, (i + step) % count) for i in range(count)])


def partner(value, axis, bits):
    count = lax.axis_size(axis)
    return lax.ppermute(value, axis, [(i, i ^ bits) for i in range(count)])


def held_for(first, *others):
    flat, tree = jax.tree.flatten((first,) + others)
    return jax.tree.unflatten(tree, lax.optimization_barrier(flat))


class Gather:
    def __init__(self, own):
        self.here, self.there = [own], []
        self.peers = lax.axis_size("seq")

    def step(self):
        at = len(self.there)
        block = self.here[at]
        if at < self.peers - 1:
            self.there.append(ring(block, "dp", 1))
            self.here.append(ring(block, "seq", 1))
        else:
            half = block.shape[0] // 2
            self.there.append([ring(block[:half], "dp", 1), ring(self.there[-1][half:], "seq", 1)])

    def hold(self, value):
        value, here, there = held_for(value, self.here[1:], self.there)
        self.here[1:], self.there = here, there
        return value

    def done(self):
        return len(self.there) == self.peers


class Reduce:
    def __init__(self, here, there, x_first):
        self.peers = lax.axis_size("seq")
        here = here.reshape(self.peers, -1, D)
        there = there.reshape(self.peers, -1, D)
        self.x_first, self.k, self.total = x_first, self.peers, None
        self.blocks = [(here[k], there[k]) for k in range(self.peers)]
        if x_first:
            self.moving = ring(there, "dp", 1)
        else:
            self.advance()

    def term(self, k):
        if self.x_first:
            return self.blocks[k][0].astype(jnp.float32) + self.other[k].astype(jnp.float32)
        return jnp.stack(self.blocks[k]).astype(jnp.float32)

    def advance(self):
        self.k -= 1
        self.total = self.term(self.k) if self.total is None else self.term(self.k) + self.moving.astype(jnp.float32)
        if self.k > 0:
            self.moving = ring(self.total.astype(jnp.bfloat16), "seq", -1)
        elif self.x_first:
            self.moving = None
        else:
            self.moving = ring(self.total[1].astype(jnp.bfloat16), "dp", 1)

    def step(self):
        if self.moving is None:
            return
        if self.x_first and self.total is None:
            self.other = self.moving
            self.advance()
        elif self.k > 0:
            self.advance()
        else:
            self.total = self.total[0] + self.moving.astype(jnp.float32)
            self.moving = None

    def finish(self):
        while self.moving is not None:
            self.step()
        return self.total


def settle(value, reduces):
    live = [r for r in reduces if r.moving is not None]
    value, moved = held_for(value, [r.moving for r in live])
    for r, m in zip(live, moved):
        r.moving = m
    return value


def hold_all(value, reduces):
    live = [r for r in reduces if r.moving is not None]
    value, moved = held_for(value, [r.moving for r in live])
    for r, m in zip(live, moved):
        r.moving = m
        r.step()
    return value


class Halving:
    def __init__(self, value, axes, near_first):
        self.dims = [(axis, 1 << k) for axis in axes for k in reversed(range(lax.axis_size(axis).bit_length() - 1))]
        self.plan = [d for d in self.dims if near_first and d == ("expert", 1)]
        self.plan += [d for d in self.dims if d[0] == "expert" and d not in self.plan]
        self.plan += [d for d in self.dims if d not in self.plan]
        self.value = value.reshape((2,) * len(self.plan) + value.shape[1:])
        self.start()

    def start(self):
        axis, bit = self.plan.pop(0)
        dim = self.dims.index((axis, bit))
        self.dims.pop(dim)
        low, high = (lax.index_in_dim(self.value, k, dim, False) for k in range(2))
        upper = (lax.axis_index(axis) // bit) % 2 == 1
        self.keep = jnp.where(upper, high, low)
        self.moving = partner(jnp.where(upper, low, high).astype(jnp.bfloat16), axis, bit)

    def step(self):
        self.value = self.keep.astype(jnp.float32) + self.moving.astype(jnp.float32)
        self.moving = None
        if self.plan:
            self.start()

    def finish(self):
        while self.moving is not None:
            self.step()
        return self.value


def sum_everywhere(value):
    for axis in ALL:
        bits = 1
        while bits < lax.axis_size(axis):
            value = value + partner(value, axis, bits)
            bits *= 2
    return value


def exchange(blocks):
    return [blocks[0]] + [partner(blocks[d], "expert", d) for d in range(1, len(blocks))]


def local(
    tokens, segment_ids, routes, keep_mask, out_grad, norm_one, in_proj, conv_weight, conv_bias, x_proj,
    dt_proj, dt_bias, a_log, d_skip, out_proj, norm_two, router, expert_up, expert_down,
):
    seqs, length = tokens.shape[:2]
    rows = seqs * length
    steps = length // HALVES
    halo = CONVK - 1
    capacity = seqs * max(2, length * 3 // 16)
    f32, b16 = jnp.float32, jnp.bfloat16
    own = in_proj.shape[1]

    small = jnp.concatenate(
        [x_proj, dt_proj.T, conv_weight.T, conv_bias[:, None], dt_bias[:, None], a_log.T, d_skip[:, None]], axis=1
    )
    used = small.shape[1]
    small = jnp.pad(small, ((0, 0), (0, PACK - used)))
    entry = lax.all_gather(jnp.concatenate([in_proj.T, small.reshape(-1, D)], axis=0), ALL, axis=0, tiled=False)
    shard = jnp.stack([m for e in range(expert_up.shape[0]) for m in (expert_up[e].T, expert_down[e])])
    shard, entry = held_for(shard, entry)
    middle = entry.shape[0] // 2
    conv_full = entry[:middle, :own].reshape(DI, D)
    gate_full = entry[middle:, :own].reshape(DI, D)
    small = entry[:, own:].reshape(DI, PACK)
    out_full = lax.all_gather(out_proj, ALL, axis=0, tiled=True)
    local_experts = expert_up.shape[0]
    gather = Gather(shard)
    gather.step()

    xproj_full = small[:, :XW]
    dtw = small[:, XW : XW + DTR]
    at = XW + DTR
    rest = small[:, at:used].T
    conv_w = rest[:CONVK].astype(f32)
    cbias = rest[CONVK : CONVK + 1].astype(f32)
    dtb = rest[CONVK + 1 : CONVK + 2]
    alog = rest[CONVK + 2 : CONVK + 2 + NSTATE]
    skip = rest[CONVK + 2 + NSTATE :]

    halo_tokens = shifted(tokens[:, length - halo :], "seq", 1)
    halo_segs = shifted(segment_ids[:, length - halo :].astype(f32), "seq", 1)
    inputs = lax.optimization_barrier(to_ext_rows(tokens, halo_tokens)).astype(f32)
    seg_ext = to_ext_rows(segment_ids.astype(f32), halo_segs)
    drop = to_rows(keep_mask).astype(f32)
    route = to_rows(routes[..., 0])
    grad_low = lax.optimization_barrier(to_rows(out_grad))
    grad_final = grad_low.astype(f32)
    skip_rows = halo * SUB
    seg = seg_ext[skip_rows:]
    same = [(seg_ext[k * SUB : k * SUB + rows] == seg).astype(f32)[:, None] for k in range(halo)]
    same_wide = jnp.broadcast_to(jnp.stack(same), (halo, rows, LANES))
    cut = jnp.broadcast_to((1.0 - same[halo - 1]) * BIG, (rows, LANES))

    onehot = (route[:, None] == jnp.arange(EXPERTS, dtype=jnp.int32)).astype(f32)
    order = jnp.arange(rows)
    below = (order[None, :] < order[:, None]).astype(b16)
    rank = jnp.sum(dot(below, onehot.astype(b16), NN) * onehot, axis=-1).astype(jnp.int32)
    peers = lax.axis_size("expert")
    target = (route // local_experts) ^ lax.axis_index("expert")
    slot = (target * local_experts + route % local_experts) * capacity + rank
    placing = (jnp.arange(EXPERTS * capacity, dtype=jnp.int32)[:, None] == slot[None, :]).astype(b16)

    def dispatch(values):
        sent = dot(placing, values, NN, b16).reshape(peers, local_experts, capacity, values.shape[1])
        return exchange([sent[d] for d in range(peers)])

    gain_one = norm_one.astype(f32)
    inv_one = lax.rsqrt(jnp.mean(inputs * inputs, axis=-1, keepdims=True) + norm_eps)
    normed_one = (inputs * inv_one * gain_one).astype(b16)
    ext = dot(normed_one, conv_full, NT)
    gate_z = dot(normed_one[skip_rows:], gate_full, NT)
    conv_out = cbias + conv_w[halo] * ext[skip_rows:]
    for k in range(halo):
        conv_out = conv_out + conv_w[k] * (same[k] * ext[k * SUB : k * SUB + rows])
    xs = jax.nn.silu(conv_out).astype(b16)
    proj = dot(xs, xproj_full, NN)
    delta_in = proj[:, :DTR].astype(b16)
    bc = proj[:, DTR:]
    grad_arrived = dispatch(grad_low)
    delta, ends, sums = run_end(xs, delta_in, dtw, dtb, alog, bc, cut)
    ends, grad_arrived = held_for(gather.hold(ends), grad_arrived)
    rates = -jnp.exp(alog.astype(f32))[:, None, :]
    beside = [gate_z]
    starts, decays = start_states(ends, sums, rates, seqs, beside)
    gate_z = beside[0]
    starts = gather.hold(starts)
    gather.step()
    branch, ssm, held = run_out(xs, delta, alog, bc, cut, starts, gate_z, skip)
    tokens_rows = inputs[skip_rows:]
    first_sum = tokens_rows + dot(branch, out_full, NN)

    gain_two = norm_two.astype(f32)
    inv_two = lax.rsqrt(jnp.mean(first_sum * first_sum, axis=-1, keepdims=True) + norm_eps)
    normed_two = (first_sum * inv_two * gain_two).astype(b16)
    probs = jax.nn.softmax(dot(normed_two, router, NN), axis=-1)
    gate_raw = jnp.sum(probs * onehot, axis=-1)
    gate = gate_raw * drop
    gate_high = lax.reduce_precision(gate, 8, 7)
    gate_mid = lax.reduce_precision(gate - gate_high, 8, 7)
    gate_low = gate - gate_high - gate_mid
    gates = jnp.stack([gate_high, gate_mid, gate_low], axis=1).astype(b16)
    message = jnp.concatenate([normed_two, jnp.pad(gates, ((0, 0), (0, LANES - 3)))], axis=1)
    message = gather.hold(message)
    gather.step()
    arrived = gather.hold(dispatch(message))
    while not gather.done():
        gather.step()
    partial, for_weights = [], []
    for e in range(local_experts):
        done, *rest = run_expert(gather.here, e, arrived, grad_arrived, None)
        partial.append(done)
        for_weights.append(rest)
    partial = gather.hold(partial)
    theirs = gather.there[:-1] + [jnp.concatenate(gather.there[-1], axis=0)]
    returned = []
    for e in range(local_experts):
        done, *rest = run_expert(theirs, e, *for_weights[e][:2], partial[e])
        for_weights[e] += rest
        if e > 0:
            for_weights[e], returned = held_for(for_weights[e], returned)
        returned.append(exchange([part for part in done.reshape(peers, capacity, 2 * D)]))
    weight_grads = []
    for e in range(local_experts):
        x_rows, g_rows, *kept = for_weights[e]
        sides = [run_weight(kept[2 * k], kept[2 * k + 1], x_rows, g_rows) for k in range(2)]
        weight_grads += [(sides[0][m], sides[1][m]) for m in range(2)]
    returned[-1], weight_grads = held_for(returned[-1], weight_grads)
    count = len(weight_grads)
    reduces = [Reduce(g[0], g[1], i < count - 1) for i, g in enumerate(weight_grads)]
    returned = [jnp.stack([returned[e][d] for e in range(local_experts)]) for d in range(peers)]

    back_rows = jnp.stack(returned).reshape(EXPERTS * capacity, 2 * D)
    combined = dot(placing, back_rows, TN)
    expert_rows, grad_back = combined[:, :D], combined[:, D:]
    output = (first_sum + gate[:, None] * expert_rows).astype(b16)

    grad_gate = jnp.sum(grad_final * expert_rows, axis=-1) * drop
    grad_logits = (grad_gate * gate_raw)[:, None] * (onehot - probs)
    logits_low = grad_logits.astype(b16)
    router_grad = dot(normed_two, logits_low, TN)
    grad_two = grad_back + dot(logits_low, router, NT)
    gain_two_grad = jnp.sum(grad_two * (first_sum * inv_two), axis=0)
    scaled = grad_two * gain_two
    grad_first = (
        grad_final + inv_two * scaled
        - first_sum * (inv_two * inv_two * inv_two * jnp.mean(scaled * first_sum, axis=-1, keepdims=True))
    )
    first_low = grad_first.astype(b16)
    out_grad_part = dot(branch, first_low, TN, b16)
    grad_branch = dot(first_low, out_full, NT)
    grad_branch, out_grad_part = held_for(grad_branch, out_grad_part)
    grad_branch = hold_all(grad_branch, reduces[-1:])

    leads, grad_z, grad_ssm = run_first(delta, alog, bc, cut, grad_branch, gate_z, ssm)
    leads = settle(leads, [reduces[0], reduces[-1]])
    gate_part = dot(grad_z, normed_one[skip_rows:], TN, b16)
    grad_normed_z = dot(grad_z, gate_full, NN)
    beside = [gate_part, grad_normed_z, router_grad]
    last = last_grads(leads, decays, seqs, beside)
    gate_part, grad_normed_z, router_grad = beside
    last, out_grad_part, gate_part = held_for(last, out_grad_part, gate_part)
    out_sum = lax.psum_scatter(out_grad_part, ALL, scatter_dimension=0, tiled=True)
    gate_own = lax.psum_scatter(gate_part, ("seq", "expert"), scatter_dimension=0, tiled=True)
    grad_delta_in, gbc, parts = 0.0, 0.0, []
    width = DI // SPLITS
    for part in range(SPLITS):
        if part == SPLITS - 1:
            last, out_sum = held_for(last, out_sum)
        last = hold_all(last, reduces[: 1 + part] + reduces[-1:] if 1 + part < count else reduces)
        gxs, gpre, galog, gvec, gbc_part = run_back(xs, delta, alog, bc, cut, grad_ssm, skip, held, last, part)
        grad_delta_in = grad_delta_in + dot(gpre, dtw[part * width : (part + 1) * width], NN)
        gbc = gbc + gbc_part[:, : 2 * NSTATE]
        dtproj_part = dot(gpre, delta_in, TN)
        last, gxs, dtproj_part, grad_delta_in, gbc, galog, gvec = held_for(
            last, gxs, dtproj_part, grad_delta_in, gbc, galog, gvec
        )
        parts.append((gxs, dtproj_part, galog, gvec))
    grad_proj = jnp.concatenate([grad_delta_in, gbc], axis=1).astype(b16)
    grad_proj = hold_all(grad_proj, reduces)
    xproj_grad = dot(xs, grad_proj, TN)
    zeros = jnp.zeros((CONVK + 1, DI), f32)
    vecs = jnp.concatenate([p[3] for p in parts], axis=1)
    small_grad = jnp.concatenate(
        [
            xproj_grad,
            jnp.concatenate([p[1] for p in parts], axis=0),
            zeros.T,
            vecs[0][:, None],
            jnp.concatenate([p[2] for p in parts], axis=1).T,
            vecs[1][:, None],
        ],
        axis=1,
    ).astype(b16)
    small_grad = jnp.pad(small_grad, ((0, 0), (0, PACK - used)))
    small_grad, grad_proj = held_for(small_grad, grad_proj)
    small_half = Halving(small_grad.reshape(-1, own // 2, PACK), ALL, True)
    gexts, conv_parts, conv_grads = [], [], []
    for part in range(SPLITS):
        gext, gvec = run_conv(parts[part][0], grad_proj, xproj_full, ext, conv_w, cbias, same_wide, part)
        conv_parts.append(dot(gext, normed_one, TN, b16))
        gexts.append(gext)
        conv_grads.append(gvec)
    conv_all, gexts, gate_own = held_for(jnp.concatenate(conv_parts, axis=0), gexts, gate_own)
    conv_own = lax.psum_scatter(conv_all, ("seq", "expert"), scatter_dimension=0, tiled=True).astype(f32)
    gexts = hold_all(gexts, reduces)
    grad_normed = sum(dot(gexts[k], conv_full[k * width : (k + 1) * width], NN) for k in range(SPLITS))
    over = grad_normed[:skip_rows].reshape(halo, seqs, HALVES, D)
    from_next = shifted(over[:, :, 0], "seq", -1)
    edge = jnp.stack([over[:, :, 1], from_next], axis=2).reshape(skip_rows, D)
    grad_normed = grad_normed[skip_rows:] + grad_normed_z
    grad_normed = grad_normed + jnp.pad(edge, ((rows - skip_rows, 0), (0, 0)))
    inv_rows = inv_one[skip_rows:]
    gain_one_grad = jnp.sum(grad_normed * (tokens_rows * inv_rows), axis=0)
    scaled_one = grad_normed * gain_one
    grad_tokens = (
        grad_first + inv_rows * scaled_one
        - tokens_rows * (inv_rows * inv_rows * inv_rows * jnp.mean(scaled_one * tokens_rows, axis=-1, keepdims=True))
    )
    conv_grad = jnp.concatenate(conv_grads, axis=1)[: CONVK + 1]
    flat = jnp.concatenate([gain_one_grad, gain_two_grad, router_grad.reshape(-1), conv_grad.reshape(-1)])
    flat = sum_everywhere(flat.reshape(-1, LANES)).reshape(-1)
    small_sum = small_half.finish()
    is_gate = lax.axis_index("dp") == 1
    gate_own = gate_own.astype(f32)
    in_sum = jnp.where(is_gate, gate_own, conv_own)
    in_sum = in_sum + ring(jnp.where(is_gate, conv_own, gate_own).astype(b16), "dp", 1).astype(f32)
    gain_one_sum, gain_two_sum = flat[:D], flat[D : 2 * D]
    router_sum = flat[2 * D : (2 + EXPERTS) * D].reshape(D, EXPERTS)
    conv_sum = flat[(2 + EXPERTS) * D :].reshape(CONVK + 1, DI)
    place = (lax.axis_index("dp") * lax.axis_size("seq") + lax.axis_index("seq")) * peers + lax.axis_index("expert")
    channels = own // 2
    conv_sum = lax.dynamic_slice_in_dim(conv_sum, place * channels, channels, axis=1)

    small_sum = small_sum.T
    return (
        from_rows(output, seqs),
        from_rows(grad_tokens, seqs),
        gain_one_sum,
        in_sum.T,
        conv_sum[:CONVK],
        conv_sum[CONVK],
        small_sum[:XW].T,
        small_sum[XW : XW + DTR],
        small_sum[at + CONVK + 1],
        small_sum[at + CONVK + 2 : at + CONVK + 2 + NSTATE],
        small_sum[used - 1],
        out_sum.astype(f32),
        gain_two_sum,
        router_sum,
        jnp.stack([r.finish().T for r in reduces[0::2]]),
        jnp.stack([r.finish() for r in reduces[1::2]]),
    )


def solution(mesh):
    batch = ("dp", "expert")
    split = ("dp", "seq")
    return jax.shard_map(
        local,
        mesh=mesh,
        in_specs=(
            P(batch, "seq", None),
            P(batch, "seq"),
            P(batch, "seq", None),
            P(batch, "seq"),
            P(batch, "seq", None),
            P(),
            P(None, ALL),
            P(None, ALL),
            P(ALL),
            P(ALL, None),
            P(None, ALL),
            P(ALL),
            P(None, ALL),
            P(ALL),
            P(ALL, None),
            P(),
            P(),
            P("expert", None, split),
            P("expert", split, None),
        ),
        out_specs=(
            P(batch, "seq", None),
            P(batch, "seq", None),
            P(),
            P(None, ALL),
            P(None, ALL),
            P(ALL),
            P(ALL, None),
            P(None, ALL),
            P(ALL),
            P(None, ALL),
            P(ALL),
            P(ALL, None),
            P(),
            P(),
            P("expert", None, split),
            P("expert", split, None),
        ),
        check_vma=False,
    )
```

```python
import functools

import jax
import jax.numpy as jnp
from jax import lax
from jax.experimental import pallas as pl
from jax.experimental.pallas import tpu as pltpu
from jax.sharding import PartitionSpec as P

D = 1152
DI = 2304
NSTATE = 16
DTR = 72
CONVK = 4
EXPERTS = 8
XW = DTR + 2 * NSTATE
HALVES = 2
LANES = 128
LN2 = 0.6931471805599453
SPLITS = 3
SUB = 8
PACK = 256
CHUNK = 16
BIG = 1e30
VMEM = 60 * 1024 * 1024

norm_eps = 1e-05
ALL = ("dp", "seq", "expert")


def shifted(value, axis, steps):
    count = lax.axis_size(axis)
    first, last = (max(0, -steps), min(count, count - steps))
    return lax.ppermute(value, axis, [(source, source + steps) for source in range(first, last)])


def dot(left, right, dims, out=jnp.float32):
    return lax.dot_general(left, right, (dims, ((), ())), preferred_element_type=out)


NN = ((1,), (0,))
NT = ((1,), (1,))
TN = ((0,), (0,))


def to_rows(value):
    seqs, length = value.shape[:2]
    rest = value.shape[2:]
    split = value.reshape((seqs, HALVES, length // HALVES) + rest)
    return jnp.moveaxis(split, 2, 0).reshape((seqs * length,) + rest)


def from_rows_kernel(rows_ref, out_ref):
    steps = out_ref.shape[1]
    for s in range(SUB):
        out_ref[s] = rows_ref[pl.ds(s, steps, stride=SUB), :].astype(out_ref.dtype)


def from_rows(value, seqs, dtype):
    rows = value.shape[0]
    steps = rows // SUB
    out = pl.pallas_call(
        from_rows_kernel,
        grid=(D // LANES,),
        in_specs=[pl.BlockSpec((rows, LANES), lambda c: (0, c))],
        out_specs=pl.BlockSpec((SUB, steps, LANES), lambda c: (0, 0, c)),
        out_shape=jax.ShapeDtypeStruct((SUB, steps, D), dtype),
        name="positions",
    )(value)
    return out.reshape(seqs, HALVES * steps, D)


def to_ext_rows(value, halo):
    seqs, length = value.shape[:2]
    rest = value.shape[2:]
    part = length // HALVES
    ext = jnp.concatenate([halo, value], axis=1)
    split = jnp.stack([ext[:, h * part : h * part + part + CONVK - 1] for h in range(HALVES)], axis=1)
    return jnp.moveaxis(split, 2, 0).reshape(((part + CONVK - 1) * seqs * HALVES,) + rest)


def decay_rates(alog_ref, a_s):
    rates = -(1.0 / LN2) * jnp.exp(alog_ref[...].astype(jnp.float32))
    for n in range(NSTATE):
        a_s[n] = jnp.broadcast_to(rates[n : n + 1, :], (SUB, LANES))


def spread(src_ref, dst, first):
    src = src_ref[...]
    high = src.astype(jnp.bfloat16)
    both = jnp.concatenate([high, (src - high.astype(jnp.float32)).astype(jnp.bfloat16)], axis=1)
    line = lax.broadcasted_iota(jnp.int32, (4 * NSTATE, 2 * LANES), 0)
    shift = jnp.where(lax.broadcasted_iota(jnp.int32, (4 * NSTATE, 2 * LANES), 1) < LANES, 0, NSTATE // 2)

    def body(n, carry):
        wanted = shift + (first + n)
        pick = (line == wanted) | (line == wanted + 2 * NSTATE)
        wide = dot(both, jnp.where(pick, 1.0, 0.0).astype(jnp.bfloat16), NN)
        dst[n] = wide[:, :LANES]
        dst[n + NSTATE // 2] = wide[:, LANES:]
        return carry

    lax.fori_loop(0, NSTATE // 2, body, 0)


def tree_sum(parts):
    while len(parts) > 1:
        parts = [parts[i] + parts[i + 1] if i + 1 < len(parts) else parts[i] for i in range(0, len(parts), 2)]
    return parts[0]


UNROLL = 8


def unrolled(first, count, body, carry):
    def group(i, inner):
        for u in range(UNROLL):
            inner = body(first + i * UNROLL + u, inner)
        return inner

    return lax.fori_loop(0, count // UNROLL, group, carry)


def row_at(t):
    return pl.ds(pl.multiple_of(t * SUB, SUB), SUB)


def end_kernel(xs_ref, din_ref, dtw_ref, dtb_ref, alog_ref, bc_ref, cut_ref, delta_ref, end_ref, sum_ref, b_s, a_s, dx_s):
    steps = delta_ref.shape[0] // SUB

    @pl.when(pl.program_id(0) == 0)
    def _():
        spread(bc_ref, b_s, 0)

    decay_rates(alog_ref, a_s)
    pre = dot(din_ref[...], dtw_ref[...], NT) + dtb_ref[...].astype(jnp.float32)
    low = jnp.exp(-jnp.abs(pre))
    delta = jnp.maximum(pre, 0.0) + jnp.where(low < 0.01, low * (1.0 - low * (0.5 - low * (1.0 / 3.0))), jnp.log(1.0 + low))
    delta_ref[...] = delta
    dx_s[...] = delta * xs_ref[...].astype(jnp.float32)
    rates = [a_s[n] for n in range(NSTATE)]

    def body(t, carry):
        total, state = carry
        at = row_at(t)
        step = jnp.maximum(delta_ref[at, :], cut_ref[at, :])
        dx = dx_s[at, :]
        state = [jnp.exp2(step * rates[n]) * state[n] + dx * b_s[n, at, :] for n in range(NSTATE)]
        return (total + step, state)

    zero = jnp.zeros((SUB, LANES), jnp.float32)
    total, state = unrolled(0, steps, body, (zero, [zero] * NSTATE))
    sum_ref[...] = total
    for n in range(NSTATE):
        end_ref[n] = state[n]


def out_kernel(xs_ref, delta_ref, alog_ref, bc_ref, cut_ref, start_ref, z_ref, skip_ref, branch_ref, ssm_ref, held_ref, b_s, c_s, a_s, dx_s, y_s):
    steps = delta_ref.shape[0] // SUB

    @pl.when(pl.program_id(0) == 0)
    def _():
        spread(bc_ref, b_s, 0)
        spread(bc_ref, c_s, NSTATE)

    decay_rates(alog_ref, a_s)
    xs = xs_ref[...].astype(jnp.float32)
    dx_s[...] = delta_ref[...] * xs
    rates = [a_s[n] for n in range(NSTATE)]

    def body(t, state):
        at = row_at(t)
        step = jnp.maximum(delta_ref[at, :], cut_ref[at, :])
        dx = dx_s[at, :]
        state = [jnp.exp2(step * rates[n]) * state[n] + dx * b_s[n, at, :] for n in range(NSTATE)]
        y_s[at, :] = tree_sum([state[n] * c_s[n, at, :] for n in range(NSTATE)])
        return state

    def chunk(i, state):
        for n in range(NSTATE):
            held_ref[i, n] = state[n]
        return unrolled(i * CHUNK, CHUNK, body, state)

    lax.fori_loop(0, steps // CHUNK, chunk, [start_ref[n] for n in range(NSTATE)])
    ssm = y_s[...] + skip_ref[...].astype(jnp.float32) * xs
    z = z_ref[...]
    ssm_ref[...] = ssm.astype(jnp.bfloat16)
    branch_ref[...] = (ssm * (z / (1.0 + jnp.exp(-z)))).astype(jnp.bfloat16)


def first_kernel(delta_ref, alog_ref, bc_ref, cut_ref, gb_ref, z_ref, ssm_ref, lead_ref, gz_ref, g_s, c_s, a_s):
    steps = delta_ref.shape[0] // SUB

    @pl.when(pl.program_id(0) == 0)
    def _():
        spread(bc_ref, c_s, NSTATE)

    decay_rates(alog_ref, a_s)
    z = z_ref[...]
    grad = gb_ref[...]
    sig = 1.0 / (1.0 + jnp.exp(-z))
    g_s[...] = grad * (z * sig)
    gz_ref[...] = (grad * ssm_ref[...].astype(jnp.float32) * (sig * (1.0 + z * (1.0 - sig)))).astype(jnp.bfloat16)
    rates = [a_s[n] for n in range(NSTATE)]

    def body(k, lead):
        at = row_at(steps - 1 - k)
        step = jnp.maximum(delta_ref[at, :], cut_ref[at, :])
        g = g_s[at, :]
        return [jnp.exp2(step * rates[n]) * (lead[n] + g * c_s[n, at, :]) for n in range(NSTATE)]

    zero = jnp.zeros((SUB, LANES), jnp.float32)
    lead = unrolled(0, steps, body, [zero] * NSTATE)
    for n in range(NSTATE):
        lead_ref[n] = lead[n]


def back_kernel(
    xs_ref, delta_ref, alog_ref, bc_ref, cut_ref, g_ref, skip_ref, held_ref, last_ref,
    gxs_ref, gpre_ref, galog_ref, gvec_ref, gbc_ref,
    b_s, c_s, gb_s, gc_s, a_s, dx_s, x_s, gx_s, gd_s, hd_s, dec_s,
):
    steps = delta_ref.shape[0] // SUB

    @pl.when(pl.program_id(0) == 0)
    def _():
        spread(bc_ref, b_s, 0)
        spread(bc_ref, c_s, NSTATE)
        gb_s[...] = jnp.zeros_like(gb_s)
        gc_s[...] = jnp.zeros_like(gc_s)

    decay_rates(alog_ref, a_s)
    xs = xs_ref[...].astype(jnp.float32)
    x_s[...] = xs
    dx_s[...] = delta_ref[...] * xs

    rates = [a_s[n] for n in range(NSTATE)]

    def ahead(j, state, base):
        at = row_at(base + j)
        step = jnp.maximum(delta_ref[at, :], cut_ref[at, :])
        dx = dx_s[at, :]
        g = g_ref[at, :]
        new = []
        for n in range(NSTATE):
            dec = jnp.exp2(step * rates[n])
            hd = dec * state[n]
            dec_s[j, n] = dec
            hd_s[j, n] = hd
            h = hd + dx * b_s[n, at, :]
            gc_s[n, at, :] = gc_s[n, at, :] + g * h
            new.append(h)
        return new

    def behind(k, carry, base):
        coming, rate_grad = carry
        j = CHUNK - 1 - k
        at = row_at(base + j)
        delta = delta_ref[at, :]
        dx = dx_s[at, :]
        g = g_ref[at, :]
        next_coming, next_rate, with_b, with_a = [], [], [], []
        for n in range(NSTATE):
            lam = coming[n] + g * c_s[n, at, :]
            with_b.append(lam * b_s[n, at, :])
            gb_s[n, at, :] = gb_s[n, at, :] + lam * dx
            q = lam * hd_s[j, n]
            with_a.append(q * a_s[n])
            next_rate.append(rate_grad[n] + delta * q)
            next_coming.append(lam * dec_s[j, n])
        by_b = tree_sum(with_b)
        gx_s[at, :] = by_b * delta
        gd_s[at, :] = by_b * x_s[at, :] + LN2 * tree_sum(with_a)
        return (next_coming, next_rate)

    chunks = steps // CHUNK

    def chunk(i, carry):
        c = chunks - 1 - i
        base = c * CHUNK
        unrolled(0, CHUNK, functools.partial(ahead, base=base), [held_ref[c, n] for n in range(NSTATE)])
        return unrolled(0, CHUNK, functools.partial(behind, base=base), carry)

    zero = jnp.zeros((SUB, LANES), jnp.float32)
    _, rate_grad = lax.fori_loop(0, chunks, chunk, ([last_ref[n] for n in range(NSTATE)], [zero] * NSTATE))
    for n in range(NSTATE):
        galog_ref[n : n + 1, :] = LN2 * jnp.sum(rate_grad[n] * a_s[n], axis=0, keepdims=True)
    skip = skip_ref[...].astype(jnp.float32)
    grad_ssm = g_ref[...]
    gxs_ref[...] = gx_s[...] + grad_ssm * skip
    delta = delta_ref[...]
    slope = jnp.where(delta < 0.01, delta * (1.0 - 0.5 * delta * (1.0 - delta * (1.0 / 3.0))), 1.0 - jnp.exp(-delta))
    gpre = gd_s[...] * slope
    gpre_ref[...] = gpre.astype(jnp.bfloat16)
    gvec_ref[0:1, :] = jnp.sum(gpre, axis=0, keepdims=True)
    gvec_ref[1:2, :] = jnp.sum(grad_ssm * xs, axis=0, keepdims=True)
    gvec_ref[2:SUB, :] = jnp.zeros((SUB - 2, LANES), jnp.float32)

    @pl.when(pl.program_id(0) == pl.num_programs(0) - 1)
    def _():
        lane = lax.broadcasted_iota(jnp.int32, (2 * LANES, LANES), 1)
        line = lax.broadcasted_iota(jnp.int32, (2 * LANES, LANES), 0)
        gbc_ref[...] = jnp.zeros_like(gbc_ref)

        def gather(n, carry):
            pick = jnp.where(lane == jnp.where(line < LANES, n, NSTATE + n), 1.0, 0.0).astype(jnp.bfloat16)
            both = jnp.concatenate([gb_s[n].astype(jnp.bfloat16), gc_s[n].astype(jnp.bfloat16)], axis=1)
            gbc_ref[...] += dot(both, pick, NN)
            return carry

        lax.fori_loop(0, NSTATE, gather, 0)


def col_spec(rows):
    return pl.BlockSpec((rows, LANES), lambda c: (0, c))


def full_spec(shape):
    return pl.BlockSpec(shape, lambda c: (0,) * len(shape))


def state_spec():
    return pl.BlockSpec((NSTATE, SUB, LANES), lambda c: (0, 0, c))


def params():
    return pltpu.CompilerParams(vmem_limit_bytes=VMEM)


def f32s(*shape):
    return jax.ShapeDtypeStruct(shape, jnp.float32)


def b16s(*shape):
    return jax.ShapeDtypeStruct(shape, jnp.bfloat16)


def vm(*shape):
    return pltpu.VMEM(shape, jnp.float32)


def cost(rows, width, per_value):
    work = rows * width * NSTATE
    return pl.CostEstimate(flops=work * 8, bytes_accessed=work * per_value, transcendentals=work)


def run_end(xs, din, dtw, dtb, alog, bc, cut):
    rows = xs.shape[0]
    return pl.pallas_call(
        end_kernel,
        grid=(DI // LANES,),
        in_specs=[
            col_spec(rows), full_spec(din.shape), pl.BlockSpec((LANES, DTR), lambda c: (c, 0)),
            col_spec(1), col_spec(NSTATE), full_spec(bc.shape), full_spec(cut.shape),
        ],
        out_specs=[col_spec(rows), state_spec(), col_spec(SUB)],
        out_shape=[f32s(rows, DI), f32s(NSTATE, SUB, DI), f32s(SUB, DI)],
        scratch_shapes=[vm(NSTATE, rows, LANES), vm(NSTATE, SUB, LANES), vm(rows, LANES)],
        compiler_params=params(),
        cost_estimate=cost(rows, DI, 4),
        name="end",
    )(xs, din, dtw, dtb, alog, bc, cut)


def run_out(xs, delta, alog, bc, cut, start, z, skip):
    rows = xs.shape[0]
    chunks = rows // SUB // CHUNK
    return pl.pallas_call(
        out_kernel,
        grid=(DI // LANES,),
        in_specs=[
            col_spec(rows), col_spec(rows), col_spec(NSTATE), full_spec(bc.shape), full_spec(cut.shape),
            state_spec(), col_spec(rows), col_spec(1),
        ],
        out_specs=[
            col_spec(rows), col_spec(rows),
            pl.BlockSpec((chunks, NSTATE, SUB, LANES), lambda c: (0, 0, 0, c)),
        ],
        out_shape=[b16s(rows, DI), b16s(rows, DI), f32s(chunks, NSTATE, SUB, DI)],
        scratch_shapes=[
            vm(NSTATE, rows, LANES), vm(NSTATE, rows, LANES), vm(NSTATE, SUB, LANES), vm(rows, LANES), vm(rows, LANES),
        ],
        compiler_params=params(),
        cost_estimate=cost(rows, DI, 5),
        name="out",
    )(xs, delta, alog, bc, cut, start, z, skip)


def run_first(delta, alog, bc, cut, gbranch, z, ssm):
    rows = delta.shape[0]
    return pl.pallas_call(
        first_kernel,
        grid=(DI // LANES,),
        in_specs=[
            col_spec(rows), col_spec(NSTATE), full_spec(bc.shape), full_spec(cut.shape), col_spec(rows), col_spec(rows),
            col_spec(rows),
        ],
        out_specs=[state_spec(), col_spec(rows), col_spec(rows)],
        out_shape=[f32s(NSTATE, SUB, DI), b16s(rows, DI), f32s(rows, DI)],
        scratch_shapes=[vm(NSTATE, rows, LANES), vm(NSTATE, SUB, LANES)],
        compiler_params=params(),
        cost_estimate=pl.CostEstimate(flops=1000, bytes_accessed=1000, transcendentals=0),
        name="first",
    )(delta, alog, bc, cut, gbranch, z, ssm)


def run_back(xs, delta, alog, bc, cut, grad_ssm, skip, held, last, part):
    rows = xs.shape[0]
    chunks = rows // SUB // CHUNK
    big = (NSTATE, rows, LANES)
    row = (rows, LANES)
    width = DI // SPLITS
    first = part * (width // LANES)

    def col(count):
        return pl.BlockSpec((count, LANES), lambda c: (0, c + first))

    return pl.pallas_call(
        back_kernel,
        grid=(width // LANES,),
        in_specs=[
            col(rows), col(rows), col(NSTATE), full_spec(bc.shape), full_spec(cut.shape), col(rows), col(1),
            pl.BlockSpec((chunks, NSTATE, SUB, LANES), lambda c: (0, 0, 0, c + first)),
            pl.BlockSpec((NSTATE, SUB, LANES), lambda c: (0, 0, c + first)),
        ],
        out_specs=[col_spec(rows), col_spec(rows), col_spec(NSTATE), col_spec(SUB), full_spec(row)],
        out_shape=[f32s(rows, width), b16s(rows, width), f32s(NSTATE, width), f32s(SUB, width), f32s(*row)],
        scratch_shapes=[
            vm(*big), vm(*big), vm(*big), vm(*big), vm(NSTATE, SUB, LANES),
            vm(*row), vm(*row), vm(*row), vm(*row),
            vm(CHUNK, NSTATE, SUB, LANES), vm(CHUNK, NSTATE, SUB, LANES),
        ],
        compiler_params=params(),
        cost_estimate=cost(rows, width, 17),
        name="back",
    )(xs, delta, alog, bc, cut, grad_ssm, skip, held, last)


def conv_kernel(gxs_ref, gproj_ref, xproj_ref, ext_ref, taps_ref, bias_ref, same_ref, gext_ref, gvec_ref, acc_s):
    rows = gxs_ref.shape[0]
    halo = CONVK - 1
    taps = taps_ref[...]
    bias = bias_ref[...]
    pieces = []
    conv = bias
    for k in range(CONVK):
        piece = ext_ref[k * SUB : k * SUB + rows, :]
        if k < halo:
            piece = piece * same_ref[k]
        pieces.append(piece)
        conv = conv + taps[k : k + 1, :] * piece
    sig = 1.0 / (1.0 + jnp.exp(-conv))
    grad = gxs_ref[...] + dot(gproj_ref[...], xproj_ref[...], NT)
    grad = grad * (sig * (1.0 + conv * (1.0 - sig)))
    acc_s[...] = jnp.zeros_like(acc_s)
    for k in range(CONVK):
        gvec_ref[k : k + 1, :] = jnp.sum(grad * pieces[k], axis=0, keepdims=True)
        part = taps[k : k + 1, :] * grad
        if k < halo:
            part = part * same_ref[k]
        acc_s[k * SUB : k * SUB + rows, :] += part
    gvec_ref[CONVK : CONVK + 1, :] = jnp.sum(grad, axis=0, keepdims=True)
    gvec_ref[CONVK + 1 : SUB, :] = jnp.zeros((SUB - CONVK - 1, LANES), jnp.float32)
    gext_ref[...] = acc_s[...].astype(jnp.bfloat16)


def run_conv(gxs, gproj, xproj, ext, taps, bias, same, part):
    rows, width = gxs.shape
    long = ext.shape[0]
    first = part * (width // LANES)

    def col(count):
        return pl.BlockSpec((count, LANES), lambda c: (0, c + first))

    return pl.pallas_call(
        conv_kernel,
        grid=(width // LANES,),
        in_specs=[
            col_spec(rows), full_spec(gproj.shape), pl.BlockSpec((LANES, XW), lambda c: (c + first, 0)), col(long),
            col(CONVK), col(1), full_spec(same.shape),
        ],
        out_specs=[col_spec(long), col_spec(SUB)],
        out_shape=[b16s(long, width), f32s(SUB, width)],
        scratch_shapes=[vm(long, LANES)],
        compiler_params=params(),
        cost_estimate=pl.CostEstimate(flops=rows * width * 260, bytes_accessed=rows * width * 10, transcendentals=rows * width),
        name="conv",
    )(gxs, gproj, xproj, ext, taps, bias, same)


def gelu_pair(v):
    inner = 0.7978845608 * (v + 0.044715 * v * v * v)
    t = jnp.tanh(inner)
    value = 0.5 * v * (1.0 + t)
    slope = 0.5 * (1.0 + t) + 0.5 * v * (1.0 - t * t) * (0.7978845608 * (1.0 + 3.0 * 0.044715 * v * v))
    return value, slope


PARTS = 2


def expert_kernel(blocks, peers, final, *refs):
    weights, refs = refs[:blocks], refs[blocks:]
    step = pl.program_id(0)
    if final:
        x_ref, g_ref, before, out_ref, hid_ref, pre_ref, up_s, down_s, acc_y, acc_g = refs

        @pl.when(step == 0)
        def _():
            acc_y[...] = before[:, :D].astype(jnp.float32)
            acc_g[...] = before[:, D:].astype(jnp.float32)

    else:
        xs, gs, refs = refs[:peers], refs[peers : 2 * peers], refs[2 * peers :]
        out_ref, x_ref, g_ref, hid_ref, pre_ref, up_s, down_s, acc_y, acc_g = refs
        cap = xs[0].shape[1]

        @pl.when(step == 0)
        def _():
            for d in range(peers):
                at = slice(d * cap, (d + 1) * cap)
                piece = xs[d][0]
                x_ref[at, :] = piece[:, :D]
                gate = jnp.sum(piece[:, D:].astype(jnp.float32), axis=1, keepdims=True)
                g_ref[at, :] = (gate * gs[d][0].astype(jnp.float32)).astype(jnp.bfloat16)
            acc_y[...] = jnp.zeros_like(acc_y)
            acc_g[...] = jnp.zeros_like(acc_g)

    size = weights[0].shape[1]
    each = blocks // PARTS
    for h in range(PARTS):

        @pl.when(step == h)
        def _():
            for k in range(each):
                at = slice(k * size, (k + 1) * size)
                up_s[at, :] = weights[h * each + k][0]
                down_s[at, :] = weights[h * each + k][1]

    tile = x_ref.shape[0] // 3

    def body(r, carry):
        at = pl.ds(pl.multiple_of(r * tile, tile), tile)
        value, slope = gelu_pair(dot(x_ref[at, :], up_s[...], NT))
        hidden = value.astype(jnp.bfloat16)
        grad_pre = (slope * dot(g_ref[at, :], down_s[...], NT)).astype(jnp.bfloat16)
        hid_ref[at, :] = hidden
        pre_ref[at, :] = grad_pre
        acc_y[at, :] += dot(hidden, down_s[...], NN)
        acc_g[at, :] += dot(grad_pre, up_s[...], NN)
        return carry

    lax.fori_loop(0, 3, body, 0)

    @pl.when(step == PARTS - 1)
    def _():
        out_ref[:, :D] = acc_y[...].astype(jnp.bfloat16)
        out_ref[:, D:] = acc_g[...].astype(jnp.bfloat16)


def run_expert(weights, e, xs, gs, before):
    blocks = len(weights)
    final = before is not None
    size = weights[0].shape[1]
    peers = 1 if final else len(xs)
    rows = xs.shape[0] if final else peers * xs[0].shape[1]
    cols = blocks * size
    part = cols // PARTS
    once = dict(pipeline_mode=pl.Buffered(1))

    def pick(shape):
        return pl.BlockSpec((1,) + shape, lambda h: (e, 0, 0), **once)

    in_specs = [pl.BlockSpec((2, size, D), lambda h: (e, 0, 0), **once)] * blocks
    column = pl.BlockSpec((rows, part), lambda h: (0, h))
    kept_specs, kept = [column, column], [b16s(rows, cols), b16s(rows, cols)]
    if final:
        operands = [xs, gs, before]
        in_specs += [full_spec(v.shape) for v in operands]
    else:
        operands = [*xs, *gs]
        in_specs += [pick(v.shape[1:]) for v in operands]
        kept_specs = [full_spec((rows, D))] * 2 + kept_specs
        kept = [b16s(rows, D)] * 2 + kept
    return pl.pallas_call(
        functools.partial(expert_kernel, blocks, peers, final),
        grid=(PARTS,),
        in_specs=in_specs,
        out_specs=[full_spec((rows, 2 * D))] + kept_specs,
        out_shape=[b16s(rows, 2 * D)] + kept,
        scratch_shapes=[
            pltpu.VMEM((part, D), jnp.bfloat16), pltpu.VMEM((part, D), jnp.bfloat16), vm(rows, D), vm(rows, D),
        ],
        compiler_params=params(),
        cost_estimate=pl.CostEstimate(flops=1000, bytes_accessed=1000, transcendentals=0),
        name="expert",
    )(*weights, *operands)


def weight_kernel(hid_ref, pre_ref, x_ref, g_ref, up_ref, down_ref):
    up_ref[...] = dot(pre_ref[...], x_ref[...], TN).astype(jnp.bfloat16)
    down_ref[...] = dot(hid_ref[...], g_ref[...], TN).astype(jnp.bfloat16)


def run_weight(hid, pre, x, g):
    rows, cols = hid.shape
    part = cols // 6
    column = pl.BlockSpec((rows, part), lambda c: (0, c))
    out = pl.BlockSpec((part, D), lambda c: (c, 0))
    return pl.pallas_call(
        weight_kernel,
        grid=(6,),
        in_specs=[column, column, full_spec((rows, D)), full_spec((rows, D))],
        out_specs=[out, out],
        out_shape=[b16s(cols, D), b16s(cols, D)],
        compiler_params=params(),
        cost_estimate=pl.CostEstimate(flops=1000, bytes_accessed=1000, transcendentals=0),
        name="weight",
    )(hid, pre, x, g)


def halves_of(value, seqs):
    split = value.reshape(value.shape[:-2] + (seqs, HALVES, value.shape[-1]))
    return split[..., 0, :], split[..., 1, :]


def join_halves(first, second):
    both = jnp.stack([first, second], axis=-2)
    return both.reshape(both.shape[:-3] + (both.shape[-3] * HALVES, both.shape[-1]))


def chained(own, decay, steps, beside):
    start = jnp.zeros_like(own)
    carry = own
    for k in range(lax.axis_size("seq") - 1):
        start = shifted(carry.astype(jnp.bfloat16), "seq", steps)
        if k < len(beside):
            start, beside[k] = held_for(start, beside[k])
        start = start.astype(jnp.float32)
        carry = own + decay * start
    return start


def start_states(ends, sums, rates, seqs, beside):
    end_0, end_1 = halves_of(ends, seqs)
    sum_0, sum_1 = halves_of(sums, seqs)
    decay_0 = jnp.exp(rates * sum_0)
    decay_1 = jnp.exp(rates * sum_1)
    start = chained(decay_1 * end_0 + end_1, decay_0 * decay_1, 1, beside)
    return join_halves(start, decay_0 * start + end_0), (decay_0, decay_1)


def last_grads(leads, decays, seqs, beside):
    decay_0, decay_1 = decays
    lead_0, lead_1 = halves_of(leads, seqs)
    last = chained(lead_0 + decay_0 * lead_1, decay_0 * decay_1, -1, beside)
    return join_halves(lead_1 + decay_1 * last, last)


def ring(value, axis, step):
    count = lax.axis_size(axis)
    return lax.ppermute(value, axis, [(i, (i + step) % count) for i in range(count)])


def partner(value, axis, bits):
    count = lax.axis_size(axis)
    return lax.ppermute(value, axis, [(i, i ^ bits) for i in range(count)])


def held_for(first, *others):
    flat, tree = jax.tree.flatten((first,) + others)
    return jax.tree.unflatten(tree, lax.optimization_barrier(flat))


class Gather:
    def __init__(self, own):
        self.here, self.there = [own], []
        self.peers = lax.axis_size("seq")

    def step(self):
        at = len(self.there)
        block = self.here[at]
        if at < self.peers - 1:
            self.there.append(ring(block, "dp", 1))
            self.here.append(ring(block, "seq", 1))
        else:
            half = block.shape[0] // 2
            self.there.append([ring(block[:half], "dp", 1), ring(self.there[-1][half:], "seq", 1)])

    def hold(self, value):
        value, here, there = held_for(value, self.here[1:], self.there)
        self.here[1:], self.there = here, there
        return value

    def done(self):
        return len(self.there) == self.peers


class Reduce:
    def __init__(self, here, there, x_first):
        self.peers = lax.axis_size("seq")
        here = here.reshape(self.peers, -1, D)
        there = there.reshape(self.peers, -1, D)
        self.x_first, self.k, self.total = x_first, self.peers, None
        self.blocks = [(here[k], there[k]) for k in range(self.peers)]
        if x_first:
            self.moving = ring(there, "dp", 1)
        else:
            self.advance()

    def term(self, k):
        if self.x_first:
            return self.blocks[k][0].astype(jnp.float32) + self.other[k].astype(jnp.float32)
        return jnp.stack(self.blocks[k]).astype(jnp.float32)

    def advance(self):
        self.k -= 1
        self.total = self.term(self.k) if self.total is None else self.term(self.k) + self.moving.astype(jnp.float32)
        if self.k > 0:
            self.moving = ring(self.total.astype(jnp.bfloat16), "seq", -1)
        elif self.x_first:
            self.moving = None
        else:
            self.moving = ring(self.total[1].astype(jnp.bfloat16), "dp", 1)

    def step(self):
        if self.moving is None:
            return
        if self.x_first and self.total is None:
            self.other = self.moving
            self.advance()
        elif self.k > 0:
            self.advance()
        else:
            self.total = self.total[0] + self.moving.astype(jnp.float32)
            self.moving = None

    def finish(self):
        while self.moving is not None:
            self.step()
        return self.total


def settle(value, reduces):
    live = [r for r in reduces if r.moving is not None]
    value, moved = held_for(value, [r.moving for r in live])
    for r, m in zip(live, moved):
        r.moving = m
    return value


def hold_all(value, reduces):
    live = [r for r in reduces if r.moving is not None]
    value, moved = held_for(value, [r.moving for r in live])
    for r, m in zip(live, moved):
        r.moving = m
        r.step()
    return value


class Halving:
    def __init__(self, value, axes, near_first):
        self.dims = [(axis, 1 << k) for axis in axes for k in reversed(range(lax.axis_size(axis).bit_length() - 1))]
        self.plan = [d for d in self.dims if near_first and d == ("expert", 1)]
        self.plan += [d for d in self.dims if d[0] == "expert" and d not in self.plan]
        self.plan += [d for d in self.dims if d not in self.plan]
        self.value = value.reshape((2,) * len(self.plan) + value.shape[1:])
        self.start()

    def start(self):
        axis, bit = self.plan.pop(0)
        dim = self.dims.index((axis, bit))
        self.dims.pop(dim)
        low, high = (lax.index_in_dim(self.value, k, dim, False) for k in range(2))
        upper = (lax.axis_index(axis) // bit) % 2 == 1
        self.keep = jnp.where(upper, high, low)
        self.moving = partner(jnp.where(upper, low, high).astype(jnp.bfloat16), axis, bit)

    def step(self):
        self.value = self.keep.astype(jnp.float32) + self.moving.astype(jnp.float32)
        self.moving = None
        if self.plan:
            self.start()

    def finish(self):
        while self.moving is not None:
            self.step()
        return self.value


def sum_everywhere(value):
    for axis in ALL:
        size = lax.axis_size(axis)
        if size <= 4:
            value = tree_sum([value] + [partner(value, axis, d) for d in range(1, size)])
            continue
        bits = 1
        while bits < size:
            value = value + partner(value, axis, bits)
            bits *= 2
    return value


def exchange(blocks):
    return [blocks[0]] + [partner(blocks[d], "expert", d) for d in range(1, len(blocks))]


def local(
    tokens, segment_ids, routes, keep_mask, out_grad, norm_one, in_proj, conv_weight, conv_bias, x_proj,
    dt_proj, dt_bias, a_log, d_skip, out_proj, norm_two, router, expert_up, expert_down,
):
    seqs, length = tokens.shape[:2]
    rows = seqs * length
    steps = length // HALVES
    halo = CONVK - 1
    capacity = seqs * max(2, length * 3 // 16)
    f32, b16 = jnp.float32, jnp.bfloat16
    own = in_proj.shape[1]

    small = jnp.concatenate(
        [x_proj, dt_proj.T, conv_weight.T, conv_bias[:, None], dt_bias[:, None], a_log.T, d_skip[:, None]], axis=1
    )
    used = small.shape[1]
    small = jnp.pad(small, ((0, 0), (0, PACK - used)))
    entry = lax.all_gather(jnp.concatenate([in_proj.T, small.reshape(-1, D)], axis=0), ALL, axis=0, tiled=False)
    shard = jnp.stack([m for e in range(expert_up.shape[0]) for m in (expert_up[e].T, expert_down[e])])
    shard, entry = held_for(shard, entry)
    middle = entry.shape[0] // 2
    conv_full = entry[:middle, :own].reshape(DI, D)
    gate_full = entry[middle:, :own].reshape(DI, D)
    small = entry[:, own:].reshape(DI, PACK)
    out_full = lax.all_gather(out_proj, ALL, axis=0, tiled=True)
    local_experts = expert_up.shape[0]
    gather = Gather(shard)
    gather.step()

    xproj_full = small[:, :XW]
    dtw = small[:, XW : XW + DTR]
    at = XW + DTR
    rest = small[:, at:used].T
    conv_w = rest[:CONVK].astype(f32)
    cbias = rest[CONVK : CONVK + 1].astype(f32)
    dtb = rest[CONVK + 1 : CONVK + 2]
    alog = rest[CONVK + 2 : CONVK + 2 + NSTATE]
    skip = rest[CONVK + 2 + NSTATE :]

    halo_tokens = shifted(tokens[:, length - halo :], "seq", 1)
    halo_segs = shifted(segment_ids[:, length - halo :].astype(f32), "seq", 1)
    inputs = lax.optimization_barrier(to_ext_rows(tokens, halo_tokens)).astype(f32)
    seg_ext = to_ext_rows(segment_ids.astype(f32), halo_segs)
    drop = to_rows(keep_mask).astype(f32)
    route = to_rows(routes[..., 0])
    grad_low = lax.optimization_barrier(to_rows(out_grad))
    grad_final = grad_low.astype(f32)
    skip_rows = halo * SUB
    seg = seg_ext[skip_rows:]
    same = [(seg_ext[k * SUB : k * SUB + rows] == seg).astype(f32)[:, None] for k in range(halo)]
    same_wide = jnp.broadcast_to(jnp.stack(same), (halo, rows, LANES))
    cut = jnp.broadcast_to((1.0 - same[halo - 1]) * BIG, (rows, LANES))

    onehot = (route[:, None] == jnp.arange(EXPERTS, dtype=jnp.int32)).astype(f32)
    order = jnp.arange(rows)
    below = (order[None, :] < order[:, None]).astype(b16)
    rank = jnp.sum(dot(below, onehot.astype(b16), NN) * onehot, axis=-1).astype(jnp.int32)
    peers = lax.axis_size("expert")
    target = (route // local_experts) ^ lax.axis_index("expert")
    slot = (target * local_experts + route % local_experts) * capacity + rank
    placing = (jnp.arange(EXPERTS * capacity, dtype=jnp.int32)[:, None] == slot[None, :]).astype(b16)

    def dispatch(values):
        sent = dot(placing, values, NN, b16).reshape(peers, local_experts, capacity, values.shape[1])
        return exchange([sent[d] for d in range(peers)])

    gain_one = norm_one.astype(f32)
    inv_one = lax.rsqrt(jnp.mean(inputs * inputs, axis=-1, keepdims=True) + norm_eps)
    normed_one = (inputs * inv_one * gain_one).astype(b16)
    ext = dot(normed_one, conv_full, NT)
    gate_z = dot(normed_one[skip_rows:], gate_full, NT)
    conv_out = cbias + conv_w[halo] * ext[skip_rows:]
    for k in range(halo):
        conv_out = conv_out + conv_w[k] * (same[k] * ext[k * SUB : k * SUB + rows])
    xs = jax.nn.silu(conv_out).astype(b16)
    proj = dot(xs, xproj_full, NN)
    delta_in = proj[:, :DTR].astype(b16)
    bc = proj[:, DTR:]
    grad_arrived = dispatch(grad_low)
    delta, ends, sums = run_end(xs, delta_in, dtw, dtb, alog, bc, cut)
    ends, grad_arrived = held_for(gather.hold(ends), grad_arrived)
    rates = -jnp.exp(alog.astype(f32))[:, None, :]
    beside = [gate_z]
    starts, decays = start_states(ends, sums, rates, seqs, beside)
    gate_z = beside[0]
    starts = gather.hold(starts)
    gather.step()
    branch, ssm, held = run_out(xs, delta, alog, bc, cut, starts, gate_z, skip)
    tokens_rows = inputs[skip_rows:]
    first_sum = tokens_rows + dot(branch, out_full, NN)

    gain_two = norm_two.astype(f32)
    inv_two = lax.rsqrt(jnp.mean(first_sum * first_sum, axis=-1, keepdims=True) + norm_eps)
    normed_two = (first_sum * inv_two * gain_two).astype(b16)
    probs = jax.nn.softmax(dot(normed_two, router, NN), axis=-1)
    gate_raw = jnp.sum(probs * onehot, axis=-1)
    gate = gate_raw * drop
    gate_high = lax.reduce_precision(gate, 8, 7)
    gate_mid = lax.reduce_precision(gate - gate_high, 8, 7)
    gate_low = gate - gate_high - gate_mid
    gates = jnp.stack([gate_high, gate_mid, gate_low], axis=1).astype(b16)
    message = jnp.concatenate([normed_two, jnp.pad(gates, ((0, 0), (0, LANES - 3)))], axis=1)
    message = gather.hold(message)
    gather.step()
    arrived = gather.hold(dispatch(message))
    while not gather.done():
        gather.step()
    partial, for_weights = [], []
    for e in range(local_experts):
        done, *rest = run_expert(gather.here, e, arrived, grad_arrived, None)
        partial.append(done)
        for_weights.append(rest)
    partial = gather.hold(partial)
    theirs = gather.there[:-1] + [jnp.concatenate(gather.there[-1], axis=0)]
    returned = []
    for e in range(local_experts):
        done, *rest = run_expert(theirs, e, *for_weights[e][:2], partial[e])
        for_weights[e] += rest
        if e > 0:
            for_weights[e], returned = held_for(for_weights[e], returned)
        returned.append(exchange([part for part in done.reshape(peers, capacity, 2 * D)]))
    weight_grads = []
    for e in range(local_experts):
        x_rows, g_rows, *kept = for_weights[e]
        sides = [run_weight(kept[2 * k], kept[2 * k + 1], x_rows, g_rows) for k in range(2)]
        weight_grads += [(sides[0][m], sides[1][m]) for m in range(2)]
    returned[-1], weight_grads = held_for(returned[-1], weight_grads)
    count = len(weight_grads)
    reduces = [Reduce(g[0], g[1], i < count - 1) for i, g in enumerate(weight_grads)]
    returned = [jnp.stack([returned[e][d] for e in range(local_experts)]) for d in range(peers)]

    back_rows = jnp.stack(returned).reshape(EXPERTS * capacity, 2 * D)
    combined = dot(placing, back_rows, TN)
    expert_rows, grad_back = combined[:, :D], combined[:, D:]
    output = from_rows(first_sum + gate[:, None] * expert_rows, seqs, b16)

    grad_gate = jnp.sum(grad_final * expert_rows, axis=-1) * drop
    grad_logits = (grad_gate * gate_raw)[:, None] * (onehot - probs)
    logits_low = grad_logits.astype(b16)
    router_grad = dot(normed_two, logits_low, TN)
    grad_two = grad_back + dot(logits_low, router, NT)
    gain_two_grad = jnp.sum(grad_two * (first_sum * inv_two), axis=0)
    scaled = grad_two * gain_two
    grad_first = (
        grad_final + inv_two * scaled
        - first_sum * (inv_two * inv_two * inv_two * jnp.mean(scaled * first_sum, axis=-1, keepdims=True))
    )
    first_low = grad_first.astype(b16)
    out_grad_part = dot(branch, first_low, TN, b16)
    grad_branch = dot(first_low, out_full, NT)
    grad_branch, out_grad_part = held_for(grad_branch, out_grad_part)
    grad_branch = hold_all(grad_branch, reduces[-1:])

    leads, grad_z, grad_ssm = run_first(delta, alog, bc, cut, grad_branch, gate_z, ssm)
    leads = settle(leads, [reduces[0], reduces[-1]])
    gate_part = dot(grad_z, normed_one[skip_rows:], TN, b16)
    grad_normed_z = dot(grad_z, gate_full, NN)
    beside = [gate_part, grad_normed_z, router_grad]
    last = last_grads(leads, decays, seqs, beside)
    gate_part, grad_normed_z, router_grad = beside
    last, out_grad_part, gate_part = held_for(last, out_grad_part, gate_part)
    out_sum = lax.psum_scatter(out_grad_part, ALL, scatter_dimension=0, tiled=True)
    gate_own = lax.psum_scatter(gate_part, ("seq", "expert"), scatter_dimension=0, tiled=True)
    grad_delta_in, gbc, parts = 0.0, 0.0, []
    width = DI // SPLITS
    for part in range(SPLITS):
        if part == SPLITS - 1:
            last, out_sum = held_for(last, out_sum)
        last = hold_all(last, reduces[: 1 + part] + reduces[-1:] if 1 + part < count else reduces)
        gxs, gpre, galog, gvec, gbc_part = run_back(xs, delta, alog, bc, cut, grad_ssm, skip, held, last, part)
        grad_delta_in = grad_delta_in + dot(gpre, dtw[part * width : (part + 1) * width], NN)
        gbc = gbc + gbc_part[:, : 2 * NSTATE]
        dtproj_part = dot(gpre, delta_in, TN)
        last, gxs, dtproj_part, grad_delta_in, gbc, galog, gvec = held_for(
            last, gxs, dtproj_part, grad_delta_in, gbc, galog, gvec
        )
        parts.append((gxs, dtproj_part, galog, gvec))
    grad_proj = jnp.concatenate([grad_delta_in, gbc], axis=1).astype(b16)
    grad_proj = hold_all(grad_proj, reduces)
    xproj_grad = dot(xs, grad_proj, TN)
    zeros = jnp.zeros((CONVK + 1, DI), f32)
    vecs = jnp.concatenate([p[3] for p in parts], axis=1)
    small_grad = jnp.concatenate(
        [
            xproj_grad,
            jnp.concatenate([p[1] for p in parts], axis=0),
            zeros.T,
            vecs[0][:, None],
            jnp.concatenate([p[2] for p in parts], axis=1).T,
            vecs[1][:, None],
        ],
        axis=1,
    ).astype(b16)
    small_grad = jnp.pad(small_grad, ((0, 0), (0, PACK - used)))
    small_grad, grad_proj = held_for(small_grad, grad_proj)
    small_half = Halving(small_grad.reshape(-1, own // 2, PACK), ALL, True)
    gexts, conv_parts, conv_grads = [], [], []
    for part in range(SPLITS):
        gext, gvec = run_conv(parts[part][0], grad_proj, xproj_full, ext, conv_w, cbias, same_wide, part)
        conv_parts.append(dot(gext, normed_one, TN, b16))
        gexts.append(gext)
        conv_grads.append(gvec)
    conv_all, gexts, gate_own = held_for(jnp.concatenate(conv_parts, axis=0), gexts, gate_own)
    conv_own = lax.psum_scatter(conv_all, ("seq", "expert"), scatter_dimension=0, tiled=True).astype(f32)
    grad_normed = sum(dot(gexts[k], conv_full[k * width : (k + 1) * width], NN) for k in range(SPLITS))
    grad_normed = hold_all(grad_normed, reduces)
    over = grad_normed[:skip_rows].reshape(halo, seqs, HALVES, D)
    from_next = shifted(over[:, :, 0], "seq", -1)
    edge = jnp.stack([over[:, :, 1], from_next], axis=2).reshape(skip_rows, D)
    grad_normed = grad_normed[skip_rows:] + grad_normed_z
    grad_normed = grad_normed + jnp.pad(edge, ((rows - skip_rows, 0), (0, 0)))
    inv_rows = inv_one[skip_rows:]
    gain_one_grad = jnp.sum(grad_normed * (tokens_rows * inv_rows), axis=0)
    scaled_one = grad_normed * gain_one
    grad_tokens = (
        grad_first + inv_rows * scaled_one
        - tokens_rows * (inv_rows * inv_rows * inv_rows * jnp.mean(scaled_one * tokens_rows, axis=-1, keepdims=True))
    )
    conv_grad = jnp.concatenate(conv_grads, axis=1)[: CONVK + 1]
    flat = jnp.concatenate([gain_one_grad, gain_two_grad, router_grad.reshape(-1), conv_grad.reshape(-1)])
    flat = sum_everywhere(flat.reshape(-1, LANES)).reshape(-1)
    gain_one_sum, gain_two_sum = flat[:D], flat[D : 2 * D]
    small_sum = small_half.finish()
    is_gate = lax.axis_index("dp") == 1
    gate_own = gate_own.astype(f32)
    in_sum = jnp.where(is_gate, gate_own, conv_own)
    in_sum = in_sum + ring(jnp.where(is_gate, conv_own, gate_own).astype(b16), "dp", 1).astype(f32)
    router_sum = flat[2 * D : (2 + EXPERTS) * D].reshape(D, EXPERTS)
    conv_sum = flat[(2 + EXPERTS) * D :].reshape(CONVK + 1, DI)
    place = (lax.axis_index("dp") * lax.axis_size("seq") + lax.axis_index("seq")) * peers + lax.axis_index("expert")
    channels = own // 2
    conv_sum = lax.dynamic_slice_in_dim(conv_sum, place * channels, channels, axis=1)

    small_sum = small_sum.T
    return (
        output,
        from_rows(grad_tokens, seqs, f32),
        gain_one_sum,
        in_sum.T,
        conv_sum[:CONVK],
        conv_sum[CONVK],
        small_sum[:XW].T,
        small_sum[XW : XW + DTR],
        small_sum[at + CONVK + 1],
        small_sum[at + CONVK + 2 : at + CONVK + 2 + NSTATE],
        small_sum[used - 1],
        out_sum.astype(f32),
        gain_two_sum,
        router_sum,
        jnp.stack([r.finish().T for r in reduces[0::2]]),
        jnp.stack([r.finish() for r in reduces[1::2]]),
    )


def solution(mesh):
    batch = ("dp", "expert")
    split = ("dp", "seq")
    return jax.shard_map(
        local,
        mesh=mesh,
        in_specs=(
            P(batch, "seq", None),
            P(batch, "seq"),
            P(batch, "seq", None),
            P(batch, "seq"),
            P(batch, "seq", None),
            P(),
            P(None, ALL),
            P(None, ALL),
            P(ALL),
            P(ALL, None),
            P(None, ALL),
            P(ALL),
            P(None, ALL),
            P(ALL),
            P(ALL, None),
            P(),
            P(),
            P("expert", None, split),
            P("expert", split, None),
        ),
        out_specs=(
            P(batch, "seq", None),
            P(batch, "seq", None),
            P(),
            P(None, ALL),
            P(None, ALL),
            P(ALL),
            P(ALL, None),
            P(None, ALL),
            P(ALL),
            P(None, ALL),
            P(ALL),
            P(ALL, None),
            P(),
            P(),
            P("expert", None, split),
            P("expert", split, None),
        ),
        check_vma=False,
    )
```

```python
import functools

import jax
import jax.numpy as jnp
from jax import lax
from jax.experimental import pallas as pl
from jax.experimental.pallas import tpu as pltpu
from jax.sharding import PartitionSpec as P

D = 1152
DI = 2304
NSTATE = 16
DTR = 72
CONVK = 4
EXPERTS = 8
XW = DTR + 2 * NSTATE
HALVES = 2
LANES = 128
LN2 = 0.6931471805599453
SPLITS = 3
SUB = 8
PACK = 256
CHUNK = 16
BIG = 1e30
VMEM = 60 * 1024 * 1024

norm_eps = 1e-05
ALL = ("dp", "seq", "expert")


def shifted(value, axis, steps):
    count = lax.axis_size(axis)
    first, last = (max(0, -steps), min(count, count - steps))
    return lax.ppermute(value, axis, [(source, source + steps) for source in range(first, last)])


def dot(left, right, dims, out=jnp.float32):
    return lax.dot_general(left, right, (dims, ((), ())), preferred_element_type=out)


NN = ((1,), (0,))
NT = ((1,), (1,))
TN = ((0,), (0,))


def to_rows(value):
    seqs, length = value.shape[:2]
    rest = value.shape[2:]
    split = value.reshape((seqs, HALVES, length // HALVES) + rest)
    return jnp.moveaxis(split, 2, 0).reshape((seqs * length,) + rest)


def from_rows_kernel(rows_ref, out_ref):
    steps = out_ref.shape[1]
    for s in range(SUB):
        out_ref[s] = rows_ref[pl.ds(s, steps, stride=SUB), :].astype(out_ref.dtype)


def from_rows(value, seqs, dtype):
    rows = value.shape[0]
    steps = rows // SUB
    out = pl.pallas_call(
        from_rows_kernel,
        grid=(D // LANES,),
        in_specs=[pl.BlockSpec((rows, LANES), lambda c: (0, c))],
        out_specs=pl.BlockSpec((SUB, steps, LANES), lambda c: (0, 0, c)),
        out_shape=jax.ShapeDtypeStruct((SUB, steps, D), dtype),
        name="positions",
    )(value)
    return out.reshape(seqs, HALVES * steps, D)


def to_ext_rows(value, halo):
    seqs, length = value.shape[:2]
    rest = value.shape[2:]
    part = length // HALVES
    ext = jnp.concatenate([halo, value], axis=1)
    split = jnp.stack([ext[:, h * part : h * part + part + CONVK - 1] for h in range(HALVES)], axis=1)
    return jnp.moveaxis(split, 2, 0).reshape(((part + CONVK - 1) * seqs * HALVES,) + rest)


def decay_rates(alog_ref, a_s):
    rates = -(1.0 / LN2) * jnp.exp(alog_ref[...].astype(jnp.float32))
    for n in range(NSTATE):
        a_s[n] = jnp.broadcast_to(rates[n : n + 1, :], (SUB, LANES))


def spread(src_ref, dst, first):
    src = src_ref[...]
    high = src.astype(jnp.bfloat16)
    both = jnp.concatenate([high, (src - high.astype(jnp.float32)).astype(jnp.bfloat16)], axis=1)
    line = lax.broadcasted_iota(jnp.int32, (4 * NSTATE, 2 * LANES), 0)
    shift = jnp.where(lax.broadcasted_iota(jnp.int32, (4 * NSTATE, 2 * LANES), 1) < LANES, 0, NSTATE // 2)

    def body(n, carry):
        wanted = shift + (first + n)
        pick = (line == wanted) | (line == wanted + 2 * NSTATE)
        wide = dot(both, jnp.where(pick, 1.0, 0.0).astype(jnp.bfloat16), NN)
        dst[n] = wide[:, :LANES]
        dst[n + NSTATE // 2] = wide[:, LANES:]
        return carry

    lax.fori_loop(0, NSTATE // 2, body, 0)


def tree_sum(parts):
    while len(parts) > 1:
        parts = [parts[i] + parts[i + 1] if i + 1 < len(parts) else parts[i] for i in range(0, len(parts), 2)]
    return parts[0]


UNROLL = 8


def unrolled(first, count, body, carry):
    def group(i, inner):
        for u in range(UNROLL):
            inner = body(first + i * UNROLL + u, inner)
        return inner

    return lax.fori_loop(0, count // UNROLL, group, carry)


def row_at(t):
    return pl.ds(pl.multiple_of(t * SUB, SUB), SUB)


def end_kernel(xs_ref, din_ref, dtw_ref, dtb_ref, alog_ref, bc_ref, cut_ref, delta_ref, end_ref, sum_ref, b_s, a_s, dx_s):
    steps = delta_ref.shape[0] // SUB

    @pl.when(pl.program_id(0) == 0)
    def _():
        spread(bc_ref, b_s, 0)

    decay_rates(alog_ref, a_s)
    pre = dot(din_ref[...], dtw_ref[...], NT) + dtb_ref[...].astype(jnp.float32)
    low = jnp.exp(-jnp.abs(pre))
    delta = jnp.maximum(pre, 0.0) + jnp.where(low < 0.01, low * (1.0 - low * (0.5 - low * (1.0 / 3.0))), jnp.log(1.0 + low))
    delta_ref[...] = delta
    dx_s[...] = delta * xs_ref[...].astype(jnp.float32)
    rates = [a_s[n] for n in range(NSTATE)]

    def body(t, carry):
        total, state = carry
        at = row_at(t)
        step = jnp.maximum(delta_ref[at, :], cut_ref[at, :])
        dx = dx_s[at, :]
        state = [jnp.exp2(step * rates[n]) * state[n] + dx * b_s[n, at, :] for n in range(NSTATE)]
        return (total + step, state)

    zero = jnp.zeros((SUB, LANES), jnp.float32)
    total, state = unrolled(0, steps, body, (zero, [zero] * NSTATE))
    sum_ref[...] = total
    for n in range(NSTATE):
        end_ref[n] = state[n]


def out_kernel(xs_ref, delta_ref, alog_ref, bc_ref, cut_ref, start_ref, z_ref, skip_ref, branch_ref, ssm_ref, held_ref, b_s, c_s, a_s, dx_s, y_s):
    steps = delta_ref.shape[0] // SUB

    @pl.when(pl.program_id(0) == 0)
    def _():
        spread(bc_ref, b_s, 0)
        spread(bc_ref, c_s, NSTATE)

    decay_rates(alog_ref, a_s)
    xs = xs_ref[...].astype(jnp.float32)
    dx_s[...] = delta_ref[...] * xs
    rates = [a_s[n] for n in range(NSTATE)]

    def body(t, state):
        at = row_at(t)
        step = jnp.maximum(delta_ref[at, :], cut_ref[at, :])
        dx = dx_s[at, :]
        state = [jnp.exp2(step * rates[n]) * state[n] + dx * b_s[n, at, :] for n in range(NSTATE)]
        y_s[at, :] = tree_sum([state[n] * c_s[n, at, :] for n in range(NSTATE)])
        return state

    def chunk(i, state):
        for n in range(NSTATE):
            held_ref[i, n] = state[n]
        return unrolled(i * CHUNK, CHUNK, body, state)

    lax.fori_loop(0, steps // CHUNK, chunk, [start_ref[n] for n in range(NSTATE)])
    ssm = y_s[...] + skip_ref[...].astype(jnp.float32) * xs
    z = z_ref[...]
    ssm_ref[...] = ssm.astype(jnp.bfloat16)
    branch_ref[...] = (ssm * (z / (1.0 + jnp.exp(-z)))).astype(jnp.bfloat16)


def first_kernel(delta_ref, alog_ref, bc_ref, cut_ref, gb_ref, z_ref, ssm_ref, lead_ref, gz_ref, g_s, c_s, a_s):
    steps = delta_ref.shape[0] // SUB

    @pl.when(pl.program_id(0) == 0)
    def _():
        spread(bc_ref, c_s, NSTATE)

    decay_rates(alog_ref, a_s)
    z = z_ref[...]
    grad = gb_ref[...]
    sig = 1.0 / (1.0 + jnp.exp(-z))
    g_s[...] = grad * (z * sig)
    gz_ref[...] = (grad * ssm_ref[...].astype(jnp.float32) * (sig * (1.0 + z * (1.0 - sig)))).astype(jnp.bfloat16)
    rates = [a_s[n] for n in range(NSTATE)]

    def body(k, lead):
        at = row_at(steps - 1 - k)
        step = jnp.maximum(delta_ref[at, :], cut_ref[at, :])
        g = g_s[at, :]
        return [jnp.exp2(step * rates[n]) * (lead[n] + g * c_s[n, at, :]) for n in range(NSTATE)]

    zero = jnp.zeros((SUB, LANES), jnp.float32)
    lead = unrolled(0, steps, body, [zero] * NSTATE)
    for n in range(NSTATE):
        lead_ref[n] = lead[n]


def back_kernel(
    xs_ref, delta_ref, alog_ref, bc_ref, cut_ref, g_ref, skip_ref, held_ref, last_ref,
    gxs_ref, gpre_ref, galog_ref, gvec_ref, gbc_ref,
    b_s, c_s, gb_s, gc_s, a_s, dx_s, x_s, gx_s, gd_s, hd_s, dec_s,
):
    steps = delta_ref.shape[0] // SUB

    @pl.when(pl.program_id(0) == 0)
    def _():
        spread(bc_ref, b_s, 0)
        spread(bc_ref, c_s, NSTATE)
        gb_s[...] = jnp.zeros_like(gb_s)
        gc_s[...] = jnp.zeros_like(gc_s)

    decay_rates(alog_ref, a_s)
    xs = xs_ref[...].astype(jnp.float32)
    x_s[...] = xs
    dx_s[...] = delta_ref[...] * xs

    rates = [a_s[n] for n in range(NSTATE)]

    def ahead(j, state, base):
        at = row_at(base + j)
        step = jnp.maximum(delta_ref[at, :], cut_ref[at, :])
        dx = dx_s[at, :]
        g = g_ref[at, :]
        new = []
        for n in range(NSTATE):
            dec = jnp.exp2(step * rates[n])
            hd = dec * state[n]
            dec_s[j, n] = dec
            hd_s[j, n] = hd
            h = hd + dx * b_s[n, at, :]
            gc_s[n, at, :] = gc_s[n, at, :] + g * h
            new.append(h)
        return new

    def behind(k, carry, base):
        coming, rate_grad = carry
        j = CHUNK - 1 - k
        at = row_at(base + j)
        delta = delta_ref[at, :]
        dx = dx_s[at, :]
        g = g_ref[at, :]
        next_coming, next_rate, with_b, with_a = [], [], [], []
        for n in range(NSTATE):
            lam = coming[n] + g * c_s[n, at, :]
            with_b.append(lam * b_s[n, at, :])
            gb_s[n, at, :] = gb_s[n, at, :] + lam * dx
            q = lam * hd_s[j, n]
            with_a.append(q * a_s[n])
            next_rate.append(rate_grad[n] + delta * q)
            next_coming.append(lam * dec_s[j, n])
        by_b = tree_sum(with_b)
        gx_s[at, :] = by_b * delta
        gd_s[at, :] = by_b * x_s[at, :] + LN2 * tree_sum(with_a)
        return (next_coming, next_rate)

    chunks = steps // CHUNK

    def chunk(i, carry):
        c = chunks - 1 - i
        base = c * CHUNK
        unrolled(0, CHUNK, functools.partial(ahead, base=base), [held_ref[c, n] for n in range(NSTATE)])
        return unrolled(0, CHUNK, functools.partial(behind, base=base), carry)

    zero = jnp.zeros((SUB, LANES), jnp.float32)
    _, rate_grad = lax.fori_loop(0, chunks, chunk, ([last_ref[n] for n in range(NSTATE)], [zero] * NSTATE))
    for n in range(NSTATE):
        galog_ref[n : n + 1, :] = LN2 * jnp.sum(rate_grad[n] * a_s[n], axis=0, keepdims=True)
    skip = skip_ref[...].astype(jnp.float32)
    grad_ssm = g_ref[...]
    gxs_ref[...] = gx_s[...] + grad_ssm * skip
    delta = delta_ref[...]
    slope = jnp.where(delta < 0.01, delta * (1.0 - 0.5 * delta * (1.0 - delta * (1.0 / 3.0))), 1.0 - jnp.exp(-delta))
    gpre = gd_s[...] * slope
    gpre_ref[...] = gpre.astype(jnp.bfloat16)
    gvec_ref[0:1, :] = jnp.sum(gpre, axis=0, keepdims=True)
    gvec_ref[1:2, :] = jnp.sum(grad_ssm * xs, axis=0, keepdims=True)
    gvec_ref[2:SUB, :] = jnp.zeros((SUB - 2, LANES), jnp.float32)

    @pl.when(pl.program_id(0) == pl.num_programs(0) - 1)
    def _():
        lane = lax.broadcasted_iota(jnp.int32, (2 * LANES, LANES), 1)
        line = lax.broadcasted_iota(jnp.int32, (2 * LANES, LANES), 0)
        gbc_ref[...] = jnp.zeros_like(gbc_ref)

        def gather(n, carry):
            pick = jnp.where(lane == jnp.where(line < LANES, n, NSTATE + n), 1.0, 0.0).astype(jnp.bfloat16)
            both = jnp.concatenate([gb_s[n].astype(jnp.bfloat16), gc_s[n].astype(jnp.bfloat16)], axis=1)
            gbc_ref[...] += dot(both, pick, NN)
            return carry

        lax.fori_loop(0, NSTATE, gather, 0)


def col_spec(rows):
    return pl.BlockSpec((rows, LANES), lambda c: (0, c))


def full_spec(shape):
    return pl.BlockSpec(shape, lambda c: (0,) * len(shape))


def state_spec():
    return pl.BlockSpec((NSTATE, SUB, LANES), lambda c: (0, 0, c))


def params():
    return pltpu.CompilerParams(vmem_limit_bytes=VMEM)


def f32s(*shape):
    return jax.ShapeDtypeStruct(shape, jnp.float32)


def b16s(*shape):
    return jax.ShapeDtypeStruct(shape, jnp.bfloat16)


def vm(*shape):
    return pltpu.VMEM(shape, jnp.float32)


def cost(rows, width, per_value):
    work = rows * width * NSTATE
    return pl.CostEstimate(flops=work * 8, bytes_accessed=work * per_value, transcendentals=work)


def run_end(xs, din, dtw, dtb, alog, bc, cut):
    rows = xs.shape[0]
    return pl.pallas_call(
        end_kernel,
        grid=(DI // LANES,),
        in_specs=[
            col_spec(rows), full_spec(din.shape), pl.BlockSpec((LANES, DTR), lambda c: (c, 0)),
            col_spec(1), col_spec(NSTATE), full_spec(bc.shape), full_spec(cut.shape),
        ],
        out_specs=[col_spec(rows), state_spec(), col_spec(SUB)],
        out_shape=[f32s(rows, DI), f32s(NSTATE, SUB, DI), f32s(SUB, DI)],
        scratch_shapes=[vm(NSTATE, rows, LANES), vm(NSTATE, SUB, LANES), vm(rows, LANES)],
        compiler_params=params(),
        cost_estimate=cost(rows, DI, 4),
        name="end",
    )(xs, din, dtw, dtb, alog, bc, cut)


def run_out(xs, delta, alog, bc, cut, start, z, skip):
    rows = xs.shape[0]
    chunks = rows // SUB // CHUNK
    return pl.pallas_call(
        out_kernel,
        grid=(DI // LANES,),
        in_specs=[
            col_spec(rows), col_spec(rows), col_spec(NSTATE), full_spec(bc.shape), full_spec(cut.shape),
            state_spec(), col_spec(rows), col_spec(1),
        ],
        out_specs=[
            col_spec(rows), col_spec(rows),
            pl.BlockSpec((chunks, NSTATE, SUB, LANES), lambda c: (0, 0, 0, c)),
        ],
        out_shape=[b16s(rows, DI), b16s(rows, DI), f32s(chunks, NSTATE, SUB, DI)],
        scratch_shapes=[
            vm(NSTATE, rows, LANES), vm(NSTATE, rows, LANES), vm(NSTATE, SUB, LANES), vm(rows, LANES), vm(rows, LANES),
        ],
        compiler_params=params(),
        cost_estimate=cost(rows, DI, 5),
        name="out",
    )(xs, delta, alog, bc, cut, start, z, skip)


def run_first(delta, alog, bc, cut, gbranch, z, ssm):
    rows = delta.shape[0]
    return pl.pallas_call(
        first_kernel,
        grid=(DI // LANES,),
        in_specs=[
            col_spec(rows), col_spec(NSTATE), full_spec(bc.shape), full_spec(cut.shape), col_spec(rows), col_spec(rows),
            col_spec(rows),
        ],
        out_specs=[state_spec(), col_spec(rows), col_spec(rows)],
        out_shape=[f32s(NSTATE, SUB, DI), b16s(rows, DI), f32s(rows, DI)],
        scratch_shapes=[vm(NSTATE, rows, LANES), vm(NSTATE, SUB, LANES)],
        compiler_params=params(),
        cost_estimate=pl.CostEstimate(flops=1000, bytes_accessed=1000, transcendentals=0),
        name="first",
    )(delta, alog, bc, cut, gbranch, z, ssm)


def run_back(xs, delta, alog, bc, cut, grad_ssm, skip, held, last, part):
    rows = xs.shape[0]
    chunks = rows // SUB // CHUNK
    big = (NSTATE, rows, LANES)
    row = (rows, LANES)
    width = DI // SPLITS
    first = part * (width // LANES)

    def col(count):
        return pl.BlockSpec((count, LANES), lambda c: (0, c + first))

    return pl.pallas_call(
        back_kernel,
        grid=(width // LANES,),
        in_specs=[
            col(rows), col(rows), col(NSTATE), full_spec(bc.shape), full_spec(cut.shape), col(rows), col(1),
            pl.BlockSpec((chunks, NSTATE, SUB, LANES), lambda c: (0, 0, 0, c + first)),
            pl.BlockSpec((NSTATE, SUB, LANES), lambda c: (0, 0, c + first)),
        ],
        out_specs=[col_spec(rows), col_spec(rows), col_spec(NSTATE), col_spec(SUB), full_spec(row)],
        out_shape=[f32s(rows, width), b16s(rows, width), f32s(NSTATE, width), f32s(SUB, width), f32s(*row)],
        scratch_shapes=[
            vm(*big), vm(*big), vm(*big), vm(*big), vm(NSTATE, SUB, LANES),
            vm(*row), vm(*row), vm(*row), vm(*row),
            vm(CHUNK, NSTATE, SUB, LANES), vm(CHUNK, NSTATE, SUB, LANES),
        ],
        compiler_params=params(),
        cost_estimate=cost(rows, width, 17),
        name="back",
    )(xs, delta, alog, bc, cut, grad_ssm, skip, held, last)


def conv_kernel(gxs_ref, gproj_ref, xproj_ref, ext_ref, taps_ref, bias_ref, same_ref, gext_ref, gvec_ref, acc_s):
    rows = gxs_ref.shape[0]
    halo = CONVK - 1
    taps = taps_ref[...]
    bias = bias_ref[...]
    pieces = []
    conv = bias
    for k in range(CONVK):
        piece = ext_ref[k * SUB : k * SUB + rows, :]
        if k < halo:
            piece = piece * same_ref[k]
        pieces.append(piece)
        conv = conv + taps[k : k + 1, :] * piece
    sig = 1.0 / (1.0 + jnp.exp(-conv))
    grad = gxs_ref[...] + dot(gproj_ref[...], xproj_ref[...], NT)
    grad = grad * (sig * (1.0 + conv * (1.0 - sig)))
    acc_s[...] = jnp.zeros_like(acc_s)
    for k in range(CONVK):
        gvec_ref[k : k + 1, :] = jnp.sum(grad * pieces[k], axis=0, keepdims=True)
        part = taps[k : k + 1, :] * grad
        if k < halo:
            part = part * same_ref[k]
        acc_s[k * SUB : k * SUB + rows, :] += part
    gvec_ref[CONVK : CONVK + 1, :] = jnp.sum(grad, axis=0, keepdims=True)
    gvec_ref[CONVK + 1 : SUB, :] = jnp.zeros((SUB - CONVK - 1, LANES), jnp.float32)
    gext_ref[...] = acc_s[...].astype(jnp.bfloat16)


def run_conv(gxs, gproj, xproj, ext, taps, bias, same, part):
    rows, width = gxs.shape
    long = ext.shape[0]
    first = part * (width // LANES)

    def col(count):
        return pl.BlockSpec((count, LANES), lambda c: (0, c + first))

    return pl.pallas_call(
        conv_kernel,
        grid=(width // LANES,),
        in_specs=[
            col_spec(rows), full_spec(gproj.shape), pl.BlockSpec((LANES, XW), lambda c: (c + first, 0)), col(long),
            col(CONVK), col(1), full_spec(same.shape),
        ],
        out_specs=[col_spec(long), col_spec(SUB)],
        out_shape=[b16s(long, width), f32s(SUB, width)],
        scratch_shapes=[vm(long, LANES)],
        compiler_params=params(),
        cost_estimate=pl.CostEstimate(flops=rows * width * 260, bytes_accessed=rows * width * 10, transcendentals=rows * width),
        name="conv",
    )(gxs, gproj, xproj, ext, taps, bias, same)


def gelu_pair(v):
    inner = 0.7978845608 * (v + 0.044715 * v * v * v)
    t = jnp.tanh(inner)
    value = 0.5 * v * (1.0 + t)
    slope = 0.5 * (1.0 + t) + 0.5 * v * (1.0 - t * t) * (0.7978845608 * (1.0 + 3.0 * 0.044715 * v * v))
    return value, slope


PARTS = 2


def expert_kernel(blocks, peers, final, *refs):
    weights, refs = refs[:blocks], refs[blocks:]
    step = pl.program_id(0)
    if final:
        x_ref, g_ref, before, out_ref, hid_ref, pre_ref, up_s, down_s, acc_y, acc_g = refs

        @pl.when(step == 0)
        def _():
            acc_y[...] = before[:, :D].astype(jnp.float32)
            acc_g[...] = before[:, D:].astype(jnp.float32)

    else:
        xs, gs, refs = refs[:peers], refs[peers : 2 * peers], refs[2 * peers :]
        out_ref, x_ref, g_ref, hid_ref, pre_ref, up_s, down_s, acc_y, acc_g = refs
        cap = xs[0].shape[1]

        @pl.when(step == 0)
        def _():
            for d in range(peers):
                at = slice(d * cap, (d + 1) * cap)
                piece = xs[d][0]
                x_ref[at, :] = piece[:, :D]
                gate = jnp.sum(piece[:, D:].astype(jnp.float32), axis=1, keepdims=True)
                g_ref[at, :] = (gate * gs[d][0].astype(jnp.float32)).astype(jnp.bfloat16)
            acc_y[...] = jnp.zeros_like(acc_y)
            acc_g[...] = jnp.zeros_like(acc_g)

    size = weights[0].shape[1]
    each = blocks // PARTS
    for h in range(PARTS):

        @pl.when(step == h)
        def _():
            for k in range(each):
                at = slice(k * size, (k + 1) * size)
                up_s[at, :] = weights[h * each + k][0]
                down_s[at, :] = weights[h * each + k][1]

    tile = x_ref.shape[0] // 3

    def body(r, carry):
        at = pl.ds(pl.multiple_of(r * tile, tile), tile)
        value, slope = gelu_pair(dot(x_ref[at, :], up_s[...], NT))
        hidden = value.astype(jnp.bfloat16)
        grad_pre = (slope * dot(g_ref[at, :], down_s[...], NT)).astype(jnp.bfloat16)
        hid_ref[at, :] = hidden
        pre_ref[at, :] = grad_pre
        acc_y[at, :] += dot(hidden, down_s[...], NN)
        acc_g[at, :] += dot(grad_pre, up_s[...], NN)
        return carry

    lax.fori_loop(0, 3, body, 0)

    @pl.when(step == PARTS - 1)
    def _():
        out_ref[:, :D] = acc_y[...].astype(jnp.bfloat16)
        out_ref[:, D:] = acc_g[...].astype(jnp.bfloat16)


def run_expert(weights, e, xs, gs, before):
    blocks = len(weights)
    final = before is not None
    size = weights[0].shape[1]
    peers = 1 if final else len(xs)
    rows = xs.shape[0] if final else peers * xs[0].shape[1]
    cols = blocks * size
    part = cols // PARTS
    once = dict(pipeline_mode=pl.Buffered(1))

    def pick(shape):
        return pl.BlockSpec((1,) + shape, lambda h: (e, 0, 0), **once)

    in_specs = [pl.BlockSpec((2, size, D), lambda h: (e, 0, 0), **once)] * blocks
    column = pl.BlockSpec((rows, part), lambda h: (0, h))
    kept_specs, kept = [column, column], [b16s(rows, cols), b16s(rows, cols)]
    if final:
        operands = [xs, gs, before]
        in_specs += [full_spec(v.shape) for v in operands]
    else:
        operands = [*xs, *gs]
        in_specs += [pick(v.shape[1:]) for v in operands]
        kept_specs = [full_spec((rows, D))] * 2 + kept_specs
        kept = [b16s(rows, D)] * 2 + kept
    return pl.pallas_call(
        functools.partial(expert_kernel, blocks, peers, final),
        grid=(PARTS,),
        in_specs=in_specs,
        out_specs=[full_spec((rows, 2 * D))] + kept_specs,
        out_shape=[b16s(rows, 2 * D)] + kept,
        scratch_shapes=[
            pltpu.VMEM((part, D), jnp.bfloat16), pltpu.VMEM((part, D), jnp.bfloat16), vm(rows, D), vm(rows, D),
        ],
        compiler_params=params(),
        cost_estimate=pl.CostEstimate(flops=1000, bytes_accessed=1000, transcendentals=0),
        name="expert",
    )(*weights, *operands)


def weight_kernel(hid_ref, pre_ref, x_ref, g_ref, up_ref, down_ref):
    up_ref[...] = dot(pre_ref[...], x_ref[...], TN).astype(jnp.bfloat16)
    down_ref[...] = dot(hid_ref[...], g_ref[...], TN).astype(jnp.bfloat16)


def run_weight(hid, pre, x, g):
    rows, cols = hid.shape
    part = cols // 6
    column = pl.BlockSpec((rows, part), lambda c: (0, c))
    out = pl.BlockSpec((part, D), lambda c: (c, 0))
    return pl.pallas_call(
        weight_kernel,
        grid=(6,),
        in_specs=[column, column, full_spec((rows, D)), full_spec((rows, D))],
        out_specs=[out, out],
        out_shape=[b16s(cols, D), b16s(cols, D)],
        compiler_params=params(),
        cost_estimate=pl.CostEstimate(flops=1000, bytes_accessed=1000, transcendentals=0),
        name="weight",
    )(hid, pre, x, g)


def halves_of(value, seqs):
    split = value.reshape(value.shape[:-2] + (seqs, HALVES, value.shape[-1]))
    return split[..., 0, :], split[..., 1, :]


def join_halves(first, second):
    both = jnp.stack([first, second], axis=-2)
    return both.reshape(both.shape[:-3] + (both.shape[-3] * HALVES, both.shape[-1]))


def chained(own, decay, steps, beside):
    start = jnp.zeros_like(own)
    carry = own
    for k in range(lax.axis_size("seq") - 1):
        start = shifted(carry.astype(jnp.bfloat16), "seq", steps)
        if k < len(beside):
            start, beside[k] = held_for(start, beside[k])
        start = start.astype(jnp.float32)
        carry = own + decay * start
    return start


def start_states(ends, sums, rates, seqs, beside):
    end_0, end_1 = halves_of(ends, seqs)
    sum_0, sum_1 = halves_of(sums, seqs)
    decay_0 = jnp.exp(rates * sum_0)
    decay_1 = jnp.exp(rates * sum_1)
    start = chained(decay_1 * end_0 + end_1, decay_0 * decay_1, 1, beside)
    return join_halves(start, decay_0 * start + end_0), (decay_0, decay_1)


def last_grads(leads, decays, seqs, beside):
    decay_0, decay_1 = decays
    lead_0, lead_1 = halves_of(leads, seqs)
    last = chained(lead_0 + decay_0 * lead_1, decay_0 * decay_1, -1, beside)
    return join_halves(lead_1 + decay_1 * last, last)


def ring(value, axis, step):
    count = lax.axis_size(axis)
    return lax.ppermute(value, axis, [(i, (i + step) % count) for i in range(count)])


def partner(value, axis, bits):
    count = lax.axis_size(axis)
    return lax.ppermute(value, axis, [(i, i ^ bits) for i in range(count)])


def held_for(first, *others):
    flat, tree = jax.tree.flatten((first,) + others)
    return jax.tree.unflatten(tree, lax.optimization_barrier(flat))


class Gather:
    def __init__(self, own):
        self.here, self.there = [own], []
        self.peers = lax.axis_size("seq")

    def step(self):
        at = len(self.there)
        block = self.here[at]
        if at < self.peers - 1:
            self.there.append(ring(block, "dp", 1))
            self.here.append(ring(block, "seq", 1))
        else:
            half = block.shape[0] // 2
            self.there.append([ring(block[:half], "dp", 1), ring(self.there[-1][half:], "seq", 1)])

    def hold(self, value):
        value, here, there = held_for(value, self.here[1:], self.there)
        self.here[1:], self.there = here, there
        return value

    def done(self):
        return len(self.there) == self.peers


class Reduce:
    def __init__(self, here, there, x_first):
        self.peers = lax.axis_size("seq")
        here = here.reshape(self.peers, -1, D)
        there = there.reshape(self.peers, -1, D)
        self.x_first, self.k, self.total = x_first, self.peers, None
        self.blocks = [(here[k], there[k]) for k in range(self.peers)]
        if x_first:
            self.moving = ring(there, "dp", 1)
        else:
            self.advance()

    def term(self, k):
        if self.x_first:
            return self.blocks[k][0].astype(jnp.float32) + self.other[k].astype(jnp.float32)
        return jnp.stack(self.blocks[k]).astype(jnp.float32)

    def advance(self):
        self.k -= 1
        self.total = self.term(self.k) if self.total is None else self.term(self.k) + self.moving.astype(jnp.float32)
        if self.k > 0:
            self.moving = ring(self.total.astype(jnp.bfloat16), "seq", -1)
        elif self.x_first:
            self.moving = None
        else:
            self.moving = ring(self.total[1].astype(jnp.bfloat16), "dp", 1)

    def step(self):
        if self.moving is None:
            return
        if self.x_first and self.total is None:
            self.other = self.moving
            self.advance()
        elif self.k > 0:
            self.advance()
        else:
            self.total = self.total[0] + self.moving.astype(jnp.float32)
            self.moving = None

    def finish(self):
        while self.moving is not None:
            self.step()
        return self.total


def settle(value, reduces):
    live = [r for r in reduces if r.moving is not None]
    value, moved = held_for(value, [r.moving for r in live])
    for r, m in zip(live, moved):
        r.moving = m
    return value


def hold_all(value, reduces):
    live = [r for r in reduces if r.moving is not None]
    value, moved = held_for(value, [r.moving for r in live])
    for r, m in zip(live, moved):
        r.moving = m
        r.step()
    return value


class Halving:
    def __init__(self, value, axes, near_first):
        self.dims = [(axis, 1 << k) for axis in axes for k in reversed(range(lax.axis_size(axis).bit_length() - 1))]
        self.plan = [d for d in self.dims if near_first and d == ("expert", 1)]
        self.plan += [d for d in self.dims if d[0] == "expert" and d not in self.plan]
        self.plan += [d for d in self.dims if d not in self.plan]
        self.value = value.reshape((2,) * len(self.plan) + value.shape[1:])
        self.start()

    def start(self):
        axis, bit = self.plan.pop(0)
        dim = self.dims.index((axis, bit))
        self.dims.pop(dim)
        low, high = (lax.index_in_dim(self.value, k, dim, False) for k in range(2))
        upper = (lax.axis_index(axis) // bit) % 2 == 1
        self.keep = jnp.where(upper, high, low)
        self.moving = partner(jnp.where(upper, low, high).astype(jnp.bfloat16), axis, bit)

    def step(self):
        self.value = self.keep.astype(jnp.float32) + self.moving.astype(jnp.float32)
        self.moving = None
        if self.plan:
            self.start()

    def finish(self):
        while self.moving is not None:
            self.step()
        return self.value


def sum_everywhere(value):
    for axis in ALL:
        size = lax.axis_size(axis)
        if size <= 4:
            value = tree_sum([value] + [partner(value, axis, d) for d in range(1, size)])
            continue
        bits = 1
        while bits < size:
            value = value + partner(value, axis, bits)
            bits *= 2
    return value


def exchange(blocks):
    return [blocks[0]] + [partner(blocks[d], "expert", d) for d in range(1, len(blocks))]


def local(
    tokens, segment_ids, routes, keep_mask, out_grad, norm_one, in_proj, conv_weight, conv_bias, x_proj,
    dt_proj, dt_bias, a_log, d_skip, out_proj, norm_two, router, expert_up, expert_down,
):
    seqs, length = tokens.shape[:2]
    rows = seqs * length
    steps = length // HALVES
    halo = CONVK - 1
    capacity = seqs * max(2, length * 3 // 16)
    f32, b16 = jnp.float32, jnp.bfloat16
    own = in_proj.shape[1]

    small = jnp.concatenate(
        [x_proj, dt_proj.T, conv_weight.T, conv_bias[:, None], dt_bias[:, None], a_log.T, d_skip[:, None]], axis=1
    )
    used = small.shape[1]
    small = jnp.pad(small, ((0, 0), (0, PACK - used)))
    entry = lax.all_gather(jnp.concatenate([in_proj.T, small.reshape(-1, D)], axis=0), ALL, axis=0, tiled=False)
    shard = jnp.stack([m for e in range(expert_up.shape[0]) for m in (expert_up[e].T, expert_down[e])])
    shard, entry = held_for(shard, entry)
    middle = entry.shape[0] // 2
    conv_full = entry[:middle, :own].reshape(DI, D)
    gate_full = entry[middle:, :own].reshape(DI, D)
    small = entry[:, own:].reshape(DI, PACK)
    out_full = lax.all_gather(out_proj, ALL, axis=0, tiled=True)
    local_experts = expert_up.shape[0]
    gather = Gather(shard)
    gather.step()

    xproj_full = small[:, :XW]
    dtw = small[:, XW : XW + DTR]
    at = XW + DTR
    rest = small[:, at:used].T
    conv_w = rest[:CONVK].astype(f32)
    cbias = rest[CONVK : CONVK + 1].astype(f32)
    dtb = rest[CONVK + 1 : CONVK + 2]
    alog = rest[CONVK + 2 : CONVK + 2 + NSTATE]
    skip = rest[CONVK + 2 + NSTATE :]

    halo_tokens = shifted(tokens[:, length - halo :], "seq", 1)
    halo_segs = shifted(segment_ids[:, length - halo :].astype(f32), "seq", 1)
    inputs = lax.optimization_barrier(to_ext_rows(tokens, halo_tokens)).astype(f32)
    seg_ext = to_ext_rows(segment_ids.astype(f32), halo_segs)
    drop = to_rows(keep_mask).astype(f32)
    route = to_rows(routes[..., 0])
    grad_low = lax.optimization_barrier(to_rows(out_grad))
    grad_final = grad_low.astype(f32)
    skip_rows = halo * SUB
    seg = seg_ext[skip_rows:]
    same = [(seg_ext[k * SUB : k * SUB + rows] == seg).astype(f32)[:, None] for k in range(halo)]
    same_wide = jnp.broadcast_to(jnp.stack(same), (halo, rows, LANES))
    cut = jnp.broadcast_to((1.0 - same[halo - 1]) * BIG, (rows, LANES))

    onehot = (route[:, None] == jnp.arange(EXPERTS, dtype=jnp.int32)).astype(f32)
    order = jnp.arange(rows)
    below = (order[None, :] < order[:, None]).astype(b16)
    rank = jnp.sum(dot(below, onehot.astype(b16), NN) * onehot, axis=-1).astype(jnp.int32)
    peers = lax.axis_size("expert")
    target = (route // local_experts) ^ lax.axis_index("expert")
    slot = (target * local_experts + route % local_experts) * capacity + rank
    placing = (jnp.arange(EXPERTS * capacity, dtype=jnp.int32)[:, None] == slot[None, :]).astype(b16)

    def dispatch(values):
        sent = dot(placing, values, NN, b16).reshape(peers, local_experts, capacity, values.shape[1])
        return exchange([sent[d] for d in range(peers)])

    gain_one = norm_one.astype(f32)
    inv_one = lax.rsqrt(jnp.mean(inputs * inputs, axis=-1, keepdims=True) + norm_eps)
    normed_one = (inputs * inv_one * gain_one).astype(b16)
    ext = dot(normed_one, conv_full, NT)
    gate_z = dot(normed_one[skip_rows:], gate_full, NT)
    conv_out = cbias + conv_w[halo] * ext[skip_rows:]
    for k in range(halo):
        conv_out = conv_out + conv_w[k] * (same[k] * ext[k * SUB : k * SUB + rows])
    xs = jax.nn.silu(conv_out).astype(b16)
    proj = dot(xs, xproj_full, NN)
    delta_in = proj[:, :DTR].astype(b16)
    bc = proj[:, DTR:]
    grad_arrived = dispatch(grad_low)
    delta, ends, sums = run_end(xs, delta_in, dtw, dtb, alog, bc, cut)
    ends, grad_arrived = held_for(gather.hold(ends), grad_arrived)
    rates = -jnp.exp(alog.astype(f32))[:, None, :]
    beside = [gate_z]
    starts, decays = start_states(ends, sums, rates, seqs, beside)
    gate_z = beside[0]
    starts = gather.hold(starts)
    gather.step()
    branch, ssm, held = run_out(xs, delta, alog, bc, cut, starts, gate_z, skip)
    tokens_rows = inputs[skip_rows:]
    first_sum = tokens_rows + dot(branch, out_full, NN)

    gain_two = norm_two.astype(f32)
    inv_two = lax.rsqrt(jnp.mean(first_sum * first_sum, axis=-1, keepdims=True) + norm_eps)
    normed_two = (first_sum * inv_two * gain_two).astype(b16)
    probs = jax.nn.softmax(dot(normed_two, router, NN), axis=-1)
    gate_raw = jnp.sum(probs * onehot, axis=-1)
    gate = gate_raw * drop
    gate_high = lax.reduce_precision(gate, 8, 7)
    gate_mid = lax.reduce_precision(gate - gate_high, 8, 7)
    gate_low = gate - gate_high - gate_mid
    gates = jnp.stack([gate_high, gate_mid, gate_low], axis=1).astype(b16)
    message = jnp.concatenate([normed_two, jnp.pad(gates, ((0, 0), (0, LANES - 3)))], axis=1)
    message = gather.hold(message)
    gather.step()
    arrived = gather.hold(dispatch(message))
    while not gather.done():
        gather.step()
    partial, for_weights = [], []
    for e in range(local_experts):
        done, *rest = run_expert(gather.here, e, arrived, grad_arrived, None)
        partial.append(done)
        for_weights.append(rest)
    partial = gather.hold(partial)
    theirs = gather.there[:-1] + [jnp.concatenate(gather.there[-1], axis=0)]
    returned = []
    for e in range(local_experts):
        done, *rest = run_expert(theirs, e, *for_weights[e][:2], partial[e])
        for_weights[e] += rest
        if e > 0:
            for_weights[e], returned = held_for(for_weights[e], returned)
        returned.append(exchange([part for part in done.reshape(peers, capacity, 2 * D)]))
    weight_grads = []
    for e in range(local_experts):
        x_rows, g_rows, *kept = for_weights[e]
        sides = [run_weight(kept[2 * k], kept[2 * k + 1], x_rows, g_rows) for k in range(2)]
        weight_grads += [(sides[0][m], sides[1][m]) for m in range(2)]
    returned[-1], weight_grads = held_for(returned[-1], weight_grads)
    count = len(weight_grads)
    reduces = [Reduce(g[0], g[1], i < count - 1) for i, g in enumerate(weight_grads)]
    returned = [jnp.stack([returned[e][d] for e in range(local_experts)]) for d in range(peers)]

    back_rows = jnp.stack(returned).reshape(EXPERTS * capacity, 2 * D)
    combined = dot(placing, back_rows, TN)
    expert_rows, grad_back = combined[:, :D], combined[:, D:]
    output = from_rows(first_sum + gate[:, None] * expert_rows, seqs, b16)

    grad_gate = jnp.sum(grad_final * expert_rows, axis=-1) * drop
    grad_logits = (grad_gate * gate_raw)[:, None] * (onehot - probs)
    logits_low = grad_logits.astype(b16)
    router_grad = dot(normed_two, logits_low, TN)
    grad_two = grad_back + dot(logits_low, router, NT)
    gain_two_grad = jnp.sum(grad_two * (first_sum * inv_two), axis=0)
    scaled = grad_two * gain_two
    grad_first = (
        grad_final + inv_two * scaled
        - first_sum * (inv_two * inv_two * inv_two * jnp.mean(scaled * first_sum, axis=-1, keepdims=True))
    )
    first_low = grad_first.astype(b16)
    out_grad_part = dot(branch, first_low, TN, b16)
    grad_branch = dot(first_low, out_full, NT)
    grad_branch, out_grad_part = held_for(grad_branch, out_grad_part)
    grad_branch = hold_all(grad_branch, reduces[-1:])

    leads, grad_z, grad_ssm = run_first(delta, alog, bc, cut, grad_branch, gate_z, ssm)
    leads = settle(leads, [reduces[0], reduces[-1]])
    gate_part = dot(grad_z, normed_one[skip_rows:], TN, b16)
    grad_normed_z = dot(grad_z, gate_full, NN)
    beside = [gate_part, grad_normed_z, router_grad]
    last = last_grads(leads, decays, seqs, beside)
    gate_part, grad_normed_z, router_grad = beside
    last, out_grad_part, gate_part = held_for(last, out_grad_part, gate_part)
    out_sum = lax.psum_scatter(out_grad_part, ALL, scatter_dimension=0, tiled=True)
    gate_own = lax.psum_scatter(gate_part, ("seq", "expert"), scatter_dimension=0, tiled=True)
    grad_delta_in, gbc, parts = 0.0, 0.0, []
    width = DI // SPLITS
    for part in range(SPLITS):
        if part == SPLITS - 1:
            last, out_sum = held_for(last, out_sum)
        last = hold_all(last, reduces[: 1 + part] + reduces[-1:] if 1 + part < count else reduces)
        gxs, gpre, galog, gvec, gbc_part = run_back(xs, delta, alog, bc, cut, grad_ssm, skip, held, last, part)
        grad_delta_in = grad_delta_in + dot(gpre, dtw[part * width : (part + 1) * width], NN)
        gbc = gbc + gbc_part[:, : 2 * NSTATE]
        dtproj_part = dot(gpre, delta_in, TN)
        last, gxs, dtproj_part, grad_delta_in, gbc, galog, gvec = held_for(
            last, gxs, dtproj_part, grad_delta_in, gbc, galog, gvec
        )
        parts.append((gxs, dtproj_part, galog, gvec))
    grad_proj = jnp.concatenate([grad_delta_in, gbc], axis=1).astype(b16)
    grad_proj = hold_all(grad_proj, reduces)
    xproj_grad = dot(xs, grad_proj, TN)
    zeros = jnp.zeros((CONVK + 1, DI), f32)
    vecs = jnp.concatenate([p[3] for p in parts], axis=1)
    small_grad = jnp.concatenate(
        [
            xproj_grad,
            jnp.concatenate([p[1] for p in parts], axis=0),
            zeros.T,
            vecs[0][:, None],
            jnp.concatenate([p[2] for p in parts], axis=1).T,
            vecs[1][:, None],
        ],
        axis=1,
    ).astype(b16)
    small_grad = jnp.pad(small_grad, ((0, 0), (0, PACK - used)))
    small_grad, grad_proj = held_for(small_grad, grad_proj)
    small_half = Halving(small_grad.reshape(-1, own // 2, PACK), ALL, True)
    gexts, conv_parts, conv_grads = [], [], []
    for part in range(SPLITS):
        gext, gvec = run_conv(parts[part][0], grad_proj, xproj_full, ext, conv_w, cbias, same_wide, part)
        conv_parts.append(dot(gext, normed_one, TN, b16))
        gexts.append(gext)
        conv_grads.append(gvec)
    conv_all, gexts, gate_own = held_for(jnp.concatenate(conv_parts, axis=0), gexts, gate_own)
    conv_own = lax.psum_scatter(conv_all, ("seq", "expert"), scatter_dimension=0, tiled=True).astype(f32)
    gexts = hold_all(gexts, reduces)
    grad_normed = sum(dot(gexts[k], conv_full[k * width : (k + 1) * width], NN) for k in range(SPLITS))
    over = grad_normed[:skip_rows].reshape(halo, seqs, HALVES, D)
    from_next = shifted(over[:, :, 0], "seq", -1)
    edge = jnp.stack([over[:, :, 1], from_next], axis=2).reshape(skip_rows, D)
    grad_normed = grad_normed[skip_rows:] + grad_normed_z
    grad_normed = grad_normed + jnp.pad(edge, ((rows - skip_rows, 0), (0, 0)))
    inv_rows = inv_one[skip_rows:]
    gain_one_grad = jnp.sum(grad_normed * (tokens_rows * inv_rows), axis=0)
    scaled_one = grad_normed * gain_one
    grad_tokens = (
        grad_first + inv_rows * scaled_one
        - tokens_rows * (inv_rows * inv_rows * inv_rows * jnp.mean(scaled_one * tokens_rows, axis=-1, keepdims=True))
    )
    conv_grad = jnp.concatenate(conv_grads, axis=1)[: CONVK + 1]
    flat = jnp.concatenate([gain_one_grad, gain_two_grad, router_grad.reshape(-1), conv_grad.reshape(-1)])
    flat = sum_everywhere(flat.reshape(-1, LANES)).reshape(-1)
    gain_one_sum, gain_two_sum = flat[:D], flat[D : 2 * D]
    small_sum = small_half.finish()
    is_gate = lax.axis_index("dp") == 1
    gate_own = gate_own.astype(f32)
    in_sum = jnp.where(is_gate, gate_own, conv_own)
    in_sum = in_sum + ring(jnp.where(is_gate, conv_own, gate_own).astype(b16), "dp", 1).astype(f32)
    router_sum = flat[2 * D : (2 + EXPERTS) * D].reshape(D, EXPERTS)
    conv_sum = flat[(2 + EXPERTS) * D :].reshape(CONVK + 1, DI)
    place = (lax.axis_index("dp") * lax.axis_size("seq") + lax.axis_index("seq")) * peers + lax.axis_index("expert")
    channels = own // 2
    conv_sum = lax.dynamic_slice_in_dim(conv_sum, place * channels, channels, axis=1)

    small_sum = small_sum.T
    return (
        output,
        from_rows(grad_tokens, seqs, f32),
        gain_one_sum,
        in_sum.T,
        conv_sum[:CONVK],
        conv_sum[CONVK],
        small_sum[:XW].T,
        small_sum[XW : XW + DTR],
        small_sum[at + CONVK + 1],
        small_sum[at + CONVK + 2 : at + CONVK + 2 + NSTATE],
        small_sum[used - 1],
        out_sum.astype(f32),
        gain_two_sum,
        router_sum,
        jnp.stack([r.finish().T for r in reduces[0::2]]),
        jnp.stack([r.finish() for r in reduces[1::2]]),
    )


def solution(mesh):
    batch = ("dp", "expert")
    split = ("dp", "seq")
    return jax.shard_map(
        local,
        mesh=mesh,
        in_specs=(
            P(batch, "seq", None),
            P(batch, "seq"),
            P(batch, "seq", None),
            P(batch, "seq"),
            P(batch, "seq", None),
            P(),
            P(None, ALL),
            P(None, ALL),
            P(ALL),
            P(ALL, None),
            P(None, ALL),
            P(ALL),
            P(None, ALL),
            P(ALL),
            P(ALL, None),
            P(),
            P(),
            P("expert", None, split),
            P("expert", split, None),
        ),
        out_specs=(
            P(batch, "seq", None),
            P(batch, "seq", None),
            P(),
            P(None, ALL),
            P(None, ALL),
            P(ALL),
            P(ALL, None),
            P(None, ALL),
            P(ALL),
            P(None, ALL),
            P(ALL),
            P(ALL, None),
            P(),
            P(),
            P("expert", None, split),
            P("expert", split, None),
        ),
        check_vma=False,
    )
```
